32 devices in a mesh: dp: 4 (over z), fsdp: 8 (over y, x, core).
Axes of the slice: x: 2, y: 2, z: 4, core: 2. Of those that a mesh axis runs over, the one named last changes fastest.
Arguments:
- patches: bfloat16 [64, 577, 768], P(('dp', 'fsdp')), may hold values from -6 to 6
- segment_ids: int32 [64, 577], P(('dp', 'fsdp')), may hold values from 0 to 7, never falling along the last dimension, each value on 1 to 145 neighbouring positions
- selected: int32 [64, 577], P(('dp', 'fsdp')), may hold values 0 or 1
- cotangent: bfloat16 [64, 577, 768], P(('dp', 'fsdp')), may hold values from -6 to 6
- ln1_gain: bfloat16 [768], P(('dp', 'fsdp')), may hold values from 0.5 to 1.5
- ln1_bias: bfloat16 [768], P(('dp', 'fsdp')), may hold values from -1 to 1
- w_router: bfloat16 [768], P(('dp', 'fsdp')), may hold values from -0.21875 to 0.21875
- w_query: bfloat16 [768, 768], P(('dp', 'fsdp')), may hold values from -0.21875 to 0.21875
- b_query: bfloat16 [768], P(('dp', 'fsdp')), may hold values from -1.5 to 1.5
- w_key: bfloat16 [768, 768], P(('dp', 'fsdp')), may hold values from -0.21875 to 0.21875
- w_value: bfloat16 [768, 768], P(('dp', 'fsdp')), may hold values from -0.21875 to 0.21875
- b_value: bfloat16 [768], P(('dp', 'fsdp')), may hold values from -1.5 to 1.5
- w_out: bfloat16 [768, 768], P(('dp', 'fsdp')), may hold values from -1.25 to 1.25
- b_out: bfloat16 [768], P(('dp', 'fsdp')), may hold values from -1.5 to 1.5
- ln2_gain: bfloat16 [768], P(('dp', 'fsdp')), may hold values from 0.5 to 1.5
- ln2_bias: bfloat16 [768], P(('dp', 'fsdp')), may hold values from -1 to 1
- w_up: bfloat16 [768, 3072], P(('dp', 'fsdp')), may hold values from -0.21875 to 0.21875
- b_up: bfloat16 [3072], P(('dp', 'fsdp')), may hold values from -1.5 to 1.5
- w_down: bfloat16 [3072, 768], P(('dp', 'fsdp')), may hold values from -0.109375 to 0.109375
- b_down: bfloat16 [768], P(('dp', 'fsdp')), may hold values from -1.5 to 1.5
Outputs:
- mixed_out: bfloat16 [64, 577, 768], P(('dp', 'fsdp'))
- grad_patches: bfloat16 [64, 577, 768], P(('dp', 'fsdp'))
- grad_ln1_gain: float32 [768], P(('dp', 'fsdp'))
- grad_ln1_bias: float32 [768], P(('dp', 'fsdp'))
- grad_w_router: float32 [768], P(('dp', 'fsdp'))
- grad_w_query: float32 [768, 768], P(('dp', 'fsdp'))
- grad_b_query: float32 [768], P(('dp', 'fsdp'))
- grad_w_key: float32 [768, 768], P(('dp', 'fsdp'))
- grad_w_value: float32 [768, 768], P(('dp', 'fsdp'))
- grad_b_value: float32 [768], P(('dp', 'fsdp'))
- grad_w_out: float32 [768, 768], P(('dp', 'fsdp'))
- grad_b_out: float32 [768], P(('dp', 'fsdp'))
- grad_ln2_gain: float32 [768], P(('dp', 'fsdp'))
- grad_ln2_bias: float32 [768], P(('dp', 'fsdp'))
- grad_w_up: float32 [768, 3072], P(('dp', 'fsdp'))
- grad_b_up: float32 [3072], P(('dp', 'fsdp'))
- grad_w_down: float32 [3072, 768], P(('dp', 'fsdp'))
- grad_b_down: float32 [768], P(('dp', 'fsdp'))
The draws below stay inside these ranges and needn't reach their ends.
Inputs may be any that keep to these rules, and one draw needn't show every extreme that they name: `segment_ids`: in each packed row the image numbers never fall, and one image has exactly 145 patches; none has more.
All inputs are finite; a program needn't handle non-finite values. No bound on the sum of `selected` on one device may be relied on, other than what follows from the above.
Results may differ from the reference program's by a relative error of at most 0.013.
Values may be sent and summed in bfloat16 or wider, within the bound.
A program may use at most 192 MiB of HBM per device.

```python
import math
import jax
import jax.numpy as jnp
import numpy as np
from jax import lax

D = 768
FF = 3072
HEAD = 64
L = 577
SEG_COUNT = 8
SEG_MOST = 145
ROWS = 64


def place_ends(drawn, stream_key, low, largest):
    dims = drawn.shape
    spot = [jax.random.randint(jax.random.fold_in(stream_key, axis), (), 0, dims[axis]) for axis in range(len(dims))]
    drawn = drawn.at[tuple(spot)].set(low)
    longest = dims.index(max(dims))
    spot[longest] = (spot[longest] + 1) % dims[longest]
    return drawn.at[tuple(spot)].set(largest)


def spiked(array, own_key, source, target, parts, factor):
    owner, partner = [(jnp.arange(array.shape[position]) // (array.shape[position] // parts)).reshape([-1 if axis == position else 1 for axis in range(array.ndim)]) for position in (source, target)]
    chosen = jax.random.permutation(own_key, parts)[partner]
    strong = (owner == chosen) | (owner == (partner + parts // 2) % parts)
    return jnp.where(strong, factor * array, array)


def block_scale(key, shape, split, least, largest):
    factor_of = 1.0
    for position, shards_of in split:
        draws = jax.random.uniform(jax.random.fold_in(jax.random.fold_in(key, 6), position), (shards_of,), jnp.float32, least / len(split), largest / len(split))
        factor_of = factor_of * jnp.repeat(jnp.exp(draws), shape[position] // shards_of).reshape((-1,) + (1,) * (len(shape) - 1 - position))
    return factor_of


def split_up(count, total, most, slope):
    weights = [(1 << 20) // math.isqrt(standing ** slope) + 1 for standing in range(2, count + 1)]
    rest, holding = total - most - (count - 1), [1] * (count - 1)
    while rest > 0:
        candidates = [i for i in range(count - 1) if holding[i] < most]
        mass, left = sum([weights[i] for i in candidates]), rest
        for i in candidates:
            more = min(most - holding[i], max(1, left * weights[i] // mass), rest)
            holding[i] = holding[i] + more
            rest = rest - more
    return np.array([most] + holding)


def ragged(rng, amount, total, most, lean):
    if amount == 2:
        one = jax.random.randint(rng, (), max(1, total - most), min(most, total - 1) + 1)
        return jnp.stack([one, total - one])
    lengths = jnp.asarray(split_up(amount, total, most, lean), jnp.int32)
    twos = (amount - 1) // 2
    source_of, sink = lengths[1:1 + 2 * twos:2], lengths[2:2 + 2 * twos:2]
    margin = jnp.minimum(source_of - 1, most - sink)
    moved = jax.random.randint(jax.random.fold_in(rng, 1), (twos,), 0, 1 << 20) % (margin + 1)
    lengths = lengths.at[1:1 + 2 * twos:2].set(source_of - moved).at[2:2 + 2 * twos:2].set(sink + moved)
    return lengths[jax.random.permutation(jax.random.fold_in(rng, 2), amount)]


def noise(own_key, dims, deviation, most, split=(), kind=jnp.bfloat16):
    values = deviation * jax.random.normal(own_key, dims, jnp.float32)
    if split:
        values = values * block_scale(own_key, dims, split, -0.22, 0.18)
    return jnp.clip(values, -most, most).astype(kind)


def gaussian_with(rng, extent, deviation, bound, split, heavy, kind=jnp.bfloat16):
    values = deviation * jax.random.normal(rng, extent, jnp.float32)
    if split:
        values = values * block_scale(rng, extent, split, -0.22, 0.18)
    return jnp.clip(spiked(values, jax.random.fold_in(rng, 3), *heavy), -bound, bound).astype(kind)


def setup_inputs(seed: int = 0) -> dict:
    streams_of = jax.random.split(jax.random.key(seed), 21)
    patches = noise(streams_of[0], (ROWS, L, D), 1.0, 6.0, ((0, 32),))
    segment_ids = jax.vmap(lambda own: jnp.searchsorted(jnp.cumsum(ragged(own, SEG_COUNT, L, SEG_MOST, 0)), jnp.arange(L), side="right"))(jax.random.split(streams_of[1], ROWS)).reshape((ROWS, L)).astype(jnp.int32)
    selected = place_ends((jax.random.randint(streams_of[2], (ROWS, L), 0, 2) < 1).astype(jnp.int32), jax.random.fold_in(streams_of[2], 1), 0, 1)
    cotangent = gaussian_with(streams_of[3], (ROWS, L, D), 1.0, 6.0, ((0, 32),), (0, 2, 32, 2.75))
    ln1_gain = jnp.clip(1.0 + 0.1 * jax.random.normal(streams_of[4], (D,), jnp.float32), 0.5, 1.5).astype(jnp.bfloat16)
    ln1_bias = noise(streams_of[5], (D,), 0.2, 1.0, ((0, 32),))
    w_router = noise(streams_of[6], (D,), D ** -0.5, 0.21875, ((0, 32),))
    w_query = noise(streams_of[7], (D, D), D ** -0.5, 0.21875, ((0, 32),))
    b_query = noise(streams_of[8], (D,), 0.3, 1.5, ((0, 32),))
    w_key = noise(streams_of[9], (D, D), D ** -0.5, 0.21875, ((0, 32),))
    w_value = noise(streams_of[10], (D, D), D ** -0.5, 0.21875, ((0, 32),))
    b_value = noise(streams_of[11], (D,), 0.3, 1.5, ((0, 32),))
    w_out = noise(streams_of[12], (D, D), (D // 32) ** -0.5, 1.25, ((0, 32),))
    b_out = noise(streams_of[13], (D,), 0.3, 1.5, ((0, 32),))
    ln2_gain = jnp.clip(1.0 + 0.1 * jax.random.normal(streams_of[14], (D,), jnp.float32), 0.5, 1.5).astype(jnp.bfloat16)
    ln2_bias = noise(streams_of[15], (D,), 0.2, 1.0, ((0, 32),))
    w_up = noise(streams_of[16], (D, FF), D ** -0.5, 0.21875, ((0, 32),))
    b_up = noise(streams_of[17], (FF,), 0.3, 1.5, ((0, 32),))
    w_down = noise(streams_of[18], (FF, D), FF ** -0.5, 0.109375, ((0, 32),))
    b_down = noise(streams_of[19], (D,), 0.3, 1.5, ((0, 32),))
    return dict(patches=patches, segment_ids=segment_ids, selected=selected, cotangent=cotangent, ln1_gain=ln1_gain, ln1_bias=ln1_bias, w_router=w_router, w_query=w_query, b_query=b_query, w_key=w_key, w_value=w_value, b_value=b_value, w_out=w_out, b_out=b_out, ln2_gain=ln2_gain, ln2_bias=ln2_bias, w_up=w_up, b_up=b_up, w_down=w_down, b_down=b_down)


PRECISE = lax.Precision.HIGHEST
EPSILON = 1e-06

@jax.custom_vjp
def low(v):
    return lax.optimization_barrier(v.astype(jnp.bfloat16)).astype(jnp.float32)

@jax.custom_vjp
def low_back(v):
    return v

def low_keep(v):
    return (low(v), None)

def low_pass(kept, grad):
    return (grad,)

def back_keep(v):
    return (v, None)

def back_low(kept, grad):
    return (low(grad),)
low.defvjp(low_keep, low_pass)
low_back.defvjp(back_keep, back_low)

def layer_norm(values, gain_vector, offset_vector):
    average = lax.optimization_barrier(jnp.mean(values, axis=-1, keepdims=True))
    centred = values - average
    spread = lax.optimization_barrier(jnp.mean(centred * centred, axis=-1, keepdims=True))
    return centred * lax.rsqrt(spread + EPSILON) * gain_vector + offset_vector

def matmul(left, right):
    return jnp.dot(left, right, precision=PRECISE)

def attend_row(entries):
    queries, key_rows, value_rows, segment_row, select_row = entries
    length = queries.shape[0]
    head_count = queries.shape[1] // HEAD
    query_heads = queries.reshape(length, head_count, HEAD)
    key_heads = key_rows.reshape(length, head_count, HEAD)
    value_heads = value_rows.reshape(length, head_count, HEAD)
    scores = jnp.einsum('qhd,khd->hqk', query_heads, key_heads, precision=PRECISE) * (1.0 / math.sqrt(HEAD))
    scores = low_back(scores)
    places = jnp.arange(length)
    allowed = (segment_row[:, None] == segment_row[None, :]) & ((select_row[None, :] == 1) | (places[:, None] == places[None, :]))
    masked = jnp.where(allowed[None], scores, -1e+30)
    soft_weights = low(jax.nn.softmax(masked, axis=-1))
    result = jnp.einsum('hqk,khd->qhd', soft_weights, value_heads, precision=PRECISE)
    return result.reshape(length, head_count * HEAD)

def reference(patches, segment_ids, selected, cotangent, ln1_gain, ln1_bias, w_router, w_query, b_query, w_key, w_value, b_value, w_out, b_out, ln2_gain, ln2_bias, w_up, b_up, w_down, b_down):
    chosen = selected.reshape(-1).astype(jnp.float32)

    def forward(tokens, gain_one, bias_one, router, query_w, query_b, key_w, value_w, value_b, out_w, out_b, gain_two, bias_two, up_w, up_b, down_w, down_b):
        flat_tokens = tokens.reshape(ROWS * L, D)
        hidden_in = low(layer_norm(flat_tokens, gain_one, bias_one))
        router_score = jax.nn.sigmoid(matmul(hidden_in, router))
        queries = low(low_back(matmul(hidden_in, query_w) + query_b))
        key_rows = low(low_back(matmul(hidden_in, key_w)))
        value_rows = low(low_back(matmul(hidden_in, value_w) + value_b))
        attended = lax.map(jax.checkpoint(attend_row), (queries.reshape(ROWS, L, D), key_rows.reshape(ROWS, L, D), value_rows.reshape(ROWS, L, D), segment_ids, selected))
        attended = low(low_back(attended.reshape(ROWS * L, D)))
        branch = low_back(matmul(attended, out_w) + out_b)
        middle = flat_tokens + (chosen * router_score)[:, None] * branch
        normed = low(layer_norm(middle, gain_two, bias_two))
        pre_act = low_back(matmul(normed, up_w) + up_b)
        activation = low(jax.nn.gelu(pre_act, approximate=False))
        result = middle + matmul(activation, down_w) + down_b
        return result.reshape(ROWS, L, D)
    layer_out, pullback = jax.vjp(forward, patches.astype(jnp.float32), ln1_gain.astype(jnp.float32), ln1_bias.astype(jnp.float32), w_router.astype(jnp.float32), w_query.astype(jnp.float32), b_query.astype(jnp.float32), w_key.astype(jnp.float32), w_value.astype(jnp.float32), b_value.astype(jnp.float32), w_out.astype(jnp.float32), b_out.astype(jnp.float32), ln2_gain.astype(jnp.float32), ln2_bias.astype(jnp.float32), w_up.astype(jnp.float32), b_up.astype(jnp.float32), w_down.astype(jnp.float32), b_down.astype(jnp.float32))
    gradients = pullback(cotangent.astype(jnp.float32))
    return (layer_out.astype(jnp.bfloat16), gradients[0].astype(jnp.bfloat16), gradients[1], gradients[2], gradients[3], gradients[4], gradients[5], gradients[6], gradients[7], gradients[8], gradients[9], gradients[10], gradients[11], gradients[12], gradients[13], gradients[14], gradients[15], gradients[16])
```

```python
from functools import partial
import math

import jax
import jax.numpy as jnp
from jax import lax
from jax.experimental import pallas as pl
from jax.experimental.pallas import tpu as pltpu
from jax.sharding import PartitionSpec as P

AXES = ("dp", "fsdp")
MESH = pl.DeviceIdType.MESH
BF = jnp.bfloat16
F32 = jnp.float32


class Place:
    def __init__(self):
        self.z = lax.axis_index("dp")
        self.f = lax.axis_index("fsdp")
        self.c = lax.rem(self.f, 2)
        self.x = lax.rem(self.f // 2, 2)
        self.y = self.f // 4
        self.chip = self.z * 4 + self.y * 2 + self.x
        self.chip_x = self.z * 4 + self.y * 2 + (1 - self.x)
        self.chip_y = self.z * 4 + (1 - self.y) * 2 + self.x
        self.to_core = (self.z, self.y * 4 + self.x * 2 + (1 - self.c))
        self.to_x = (self.z, self.y * 4 + (1 - self.x) * 2 + self.c)
        self.to_y = (self.z, (1 - self.y) * 4 + self.x * 2 + self.c)

    def to_z(self, step):
        return (lax.rem(self.z + step + 4, 4), self.f)


def greet(place):
    bar = pltpu.get_barrier_semaphore()
    others = [place.to_core, place.to_x, place.to_y] + [place.to_z(s) for s in (1, 2, 3)]
    for other in others:
        pl.semaphore_signal(bar, inc=1, device_id=other, device_id_type=MESH)
    pl.semaphore_wait(bar, len(others))


def push(src, dst, send, recv, to):
    return pltpu.make_async_remote_copy(
        src_ref=src, dst_ref=dst, send_sem=send, recv_sem=recv, device_id=to, device_id_type=MESH
    )


class Gather:
    def __init__(self, place, j, block, level, plane_first, sems):
        self.p, self.j, self.block, self.level, self.sems = place, j, block, level, sems
        self.plane_first = plane_first

    def copy(self, kind, i, ref, to):
        return push(ref, ref, self.sems.at[2 * kind, self.j, i], self.sems.at[2 * kind + 1, self.j, i], to)

    def piece(self, l):
        if self.plane_first:
            return self.level(l, self.p.c)
        return self.block(l * 4 + self.p.y * 2 + self.p.x)

    def up(self, k):
        return self.copy(0, k, self.piece(lax.rem(self.p.z - k + 4, 4)), self.p.to_z(1))

    def up_in(self, k):
        return self.copy(0, k, self.piece(lax.rem(self.p.z - k + 3, 4)), self.p.to_z(1))

    def down(self, k):
        return self.copy(1, k, self.piece(lax.rem(self.p.z + k, 4)), self.p.to_z(3))

    def down_in(self, k):
        return self.copy(1, k, self.piece(lax.rem(self.p.z + k + 1, 4)), self.p.to_z(3))

    def xs(self, l):
        return self.copy(2, l, self.block(l * 4 + self.p.y * 2 + self.p.x), self.p.to_x)

    def ys(self, l):
        return self.copy(3, l, self.block(l * 4 + self.p.y * 2 + self.p.x), self.p.to_y)

    def side_in(self, l, y_side):
        p = self.p
        chip = l * 4 + (p.y + y_side - 2 * p.y * y_side) * 2 + (p.x + (1 - y_side) - 2 * p.x * (1 - y_side))
        return self.copy(2 + y_side, l, self.block(chip), p.to_x)

    def forward(self, l):
        p = self.p
        chip = l * 4 + jnp.where(p.c == 0, (1 - p.y) * 2 + p.x, p.y * 2 + 1 - p.x)
        to = (p.z, jnp.where(p.c == 0, p.y * 4 + (1 - p.x) * 2 + p.c, (1 - p.y) * 4 + p.x * 2 + p.c))
        return self.copy(4, l, self.block(chip), to)

    def forward_in(self, l):
        return self.copy(4, l, self.block(l * 4 + (1 - self.p.y) * 2 + 1 - self.p.x), self.p.to_x)

    def cs(self, l):
        return self.copy(5, l, self.level(l, self.p.c), self.p.to_core)

    def cs_in(self, l):
        return self.copy(5, l, self.level(l, 1 - self.p.c), self.p.to_core)

    def sides(self, l):
        self.xs(l).start()
        self.ys(l).start()

    def ends(self, k):
        z = self.p.z

        @pl.when((z >= k) & (z < 3))
        def _():
            self.up(k).start()

        @pl.when((z + k <= 3) & (z > 0))
        def _():
            self.down(k).start()

    def begin(self):
        if not self.plane_first:
            self.ends(0)
        self.sides(self.p.z)

    def along_z(self, k):
        z = self.p.z

        @pl.when(z > k)
        def _():
            self.up_in(k).wait_recv()

        @pl.when(z + k < 3)
        def _():
            self.down_in(k).wait_recv()

        if k < 2:
            self.ends(k + 1)
        self.each(k + 1, (lambda l: self.cs(l).start()) if self.plane_first else self.sides)

    def each(self, k, what):
        z = self.p.z
        if k == 0:
            what(z)
            return

        @pl.when(z >= k)
        def _():
            what(z - k)

        @pl.when(z + k <= 3)
        def _():
            what(z + k)

    def turn(self, l):
        self.side_in(l, 1 - self.p.c).wait_recv()
        self.forward(l).start()
        self.side_in(l, self.p.c).wait_recv()

    def across(self, l):
        self.forward_in(l).wait_recv()
        if self.plane_first:
            self.ends(0)
        self.cs(l).start()

    def finish(self):
        z = self.p.z
        for l in range(4):
            if self.plane_first:
                continue
            self.xs(l).wait_send()
            self.ys(l).wait_send()
            self.forward(l).wait_send()
        if self.plane_first:
            self.xs(z).wait_send()
            self.ys(z).wait_send()
            self.forward(z).wait_send()
        for l in range(4):
            self.cs(l).wait_send()
            self.cs_in(l).wait_recv()
        for k in range(3):

            @pl.when((z >= k) & (z < 3))
            def _():
                self.up(k).wait_send()

            @pl.when((z + k <= 3) & (z > 0))
            def _():
                self.down(k).wait_send()


VECTORS = 9
TILE = 128


def vector_steps(p, values, out_ref, hold, landed, sems):
    send, recv = sems.at[0], sems.at[1]
    state = {}

    def begin():
        state["value"] = values()
        hold[0] = state["value"]
        push(hold.at[0], landed.at[0], send.at[0], recv.at[0], p.to_core).start()

    def then(i, to, after):
        def step():
            push(hold.at[i], landed.at[i], send.at[i], recv.at[i], to).wait()
            hold[i + 1] = hold[i] + landed[i]
            after()
        return step

    def next_side():
        push(hold.at[1], landed.at[1], send.at[1], recv.at[1], p.to_x).start()

    def next_other():
        push(hold.at[2], landed.at[2], send.at[2], recv.at[2], p.to_y).start()

    def line(s):
        return push(hold.at[3], landed.at[2 + s], send.at[2 + s], recv.at[2 + s], p.to_z(s))

    def next_line():
        for s in (1, 2, 3):
            line(s).start()

    def last():
        for s in (1, 2, 3):
            line(s).wait()
        out_ref[...] = hold[3] + landed[3] + landed[4] + landed[5]

    return [begin, then(0, p.to_core, next_side), then(1, p.to_x, next_other), then(2, p.to_y, next_line), last]


def cut(cols, share):
    first = int(round(cols * (1 - share) / TILE)) * TILE
    return first


PLANE_SHARE = 0.12


def gather_kernel(*refs):
    vectors, b_up = refs[:VECTORS], refs[VECTORS]
    wq, wk, wv, wo, wu, wd = refs[VECTORS + 1 : VECTORS + 7]
    out_a, out_u, out_d, out_v = refs[VECTORS + 7 : VECTORS + 11]
    held, give, take, packed, hold, landed, sems, pair_sems, own_sems, vec_sems = refs[VECTORS + 11 :]
    p = Place()
    width = wq.shape[1]
    rail = 2 * width
    rows = wq.shape[0]
    lower = p.c == 0
    loads = [pltpu.make_async_copy(w, held.at[0, :, pl.ds(i * width, width)], own_sems.at[3 + i]) for i, w in enumerate((wq, wk, wv, wo))]
    loads.append(pltpu.make_async_copy(wu, held.at[1], own_sems.at[7]))
    own_d = pltpu.make_async_copy(wd, out_d.at[p.chip, p.c], own_sems.at[2])
    for cp in loads:
        cp.start()
    own_d.start()
    greet(p)
    for cp in loads:
        cp.wait()
    mine = pl.ds(pl.multiple_of(p.c * rail, TILE), rail)
    other = pl.ds(pl.multiple_of((1 - p.c) * rail, TILE), rail)
    pair = []
    for i in range(2):
        give[i] = held[i, :, other].astype(F32)
        pair.append(push(give.at[i], take.at[i], pair_sems.at[0, i], pair_sems.at[1, i], p.to_core))
        pair[i].start()
    jobs = []

    def add_jobs(out, rail_cols, columns_by_rail):
        first = cut(rail_cols, PLANE_SHARE)
        for start, size, plane in ((0, first, False), (first, rail_cols - first, True)):
            if size == 0:
                continue
            if columns_by_rail:
                def lanes(c, start=start, size=size):
                    return pl.ds(pl.multiple_of(c * rail_cols + start, TILE), size)
                block = lambda chip, out=out, lanes=lanes: out.at[chip, :, lanes(p.c)]
                level = lambda l, c, out=out, lanes=lanes: out.at[pl.ds(l * 4, 4), :, lanes(c)]
            else:
                lane = pl.ds(start, size)
                block = lambda chip, out=out, lane=lane: out.at[chip, p.c, :, lane]
                level = lambda l, c, out=out, lane=lane: out.at[pl.ds(l * 4, 4), c, :, lane]
            jobs.append(Gather(p, len(jobs), block, level, plane, sems))

    add_jobs(out_a, rail, True)
    add_jobs(out_u, rail, True)
    add_jobs(out_d, width, False)
    own_d.wait()
    per = len(jobs) // 3
    for job in jobs[: 2 * per - 1 : -1]:
        job.begin()
    for i, out in enumerate((out_a, out_u)):
        pair[i].wait()
        own = held[i, :, mine].astype(F32)
        got = take[i]
        packed[i] = jnp.concatenate([jnp.where(lower, own, got), jnp.where(lower, got, own)], axis=0).astype(BF)
        cp = pltpu.make_async_copy(packed.at[i], out.at[p.chip, :, mine], own_sems.at[i])
        cp.start()
        cp.wait()
        for job in jobs[i * per : (i + 1) * per][::-1]:
            job.begin()
    device = p.z * 8 + p.f

    def spread(ref):
        count = ref.shape[1]
        total = count * 32
        lane = lax.broadcasted_iota(jnp.int32, (count, total), 1)
        row = lax.broadcasted_iota(jnp.int32, (count, total), 0)
        place = (lane == row + device * count).astype(BF)
        return jnp.dot(ref[...], place, preferred_element_type=F32)

    def values():
        rows_of = [spread(v) for v in vectors]
        up = spread(b_up)
        rows_of += [up[:, i * width : (i + 1) * width] for i in range(4)]
        rows_of.append(jnp.zeros((3, width), F32))
        return jnp.concatenate(rows_of, axis=0)

    steps = vector_steps(p, values, out_v, hold, landed, vec_sems)
    steps[0]()
    plane = [job for job in jobs if job.plane_first]
    line = [job for job in jobs if not job.plane_first]
    for job in plane:
        job.turn(p.z)
    steps[1]()
    for job in plane:
        job.across(p.z)
    for k in range(4):
        if k < 3:
            for job in line + plane:
                job.along_z(k)
        if k < 3:
            steps[k + 2]()
        for job in line:
            job.each(k, job.turn)
        for job in line:
            job.each(k, job.across)
    for job in jobs:
        job.finish()


def gather_all(vectors, b_up, matrices):
    wq, wd = matrices[0], matrices[5]
    rows, width = wq.shape
    rail = 2 * width
    depth = wd.shape[0]
    return pl.pallas_call(
        gather_kernel,
        out_shape=(
            jax.ShapeDtypeStruct((16, 2 * rows, 4 * width), BF),
            jax.ShapeDtypeStruct((16, 2 * rows, 4 * width), BF),
            jax.ShapeDtypeStruct((16, 2, depth, width), BF),
            jax.ShapeDtypeStruct((16, width), F32),
        ),
        in_specs=[pl.BlockSpec(memory_space=pltpu.VMEM)] * (VECTORS + 1) + [pl.BlockSpec(memory_space=pl.ANY)] * 6,
        out_specs=(pl.BlockSpec(memory_space=pl.ANY),) * 3 + (pl.BlockSpec(memory_space=pltpu.VMEM),),
        scratch_shapes=[
            pltpu.VMEM((2, rows, 2 * rail), BF),
            pltpu.VMEM((2, rows, rail), F32),
            pltpu.VMEM((2, rows, rail), F32),
            pltpu.VMEM((2, 2 * rows, rail), BF),
            pltpu.VMEM((4, 16, width), F32),
            pltpu.VMEM((6, 16, width), F32),
            pltpu.SemaphoreType.DMA((12, 6, 4)),
            pltpu.SemaphoreType.DMA((2, 2)),
            pltpu.SemaphoreType.DMA((8,)),
            pltpu.SemaphoreType.DMA((2, 6)),
        ],
        compiler_params=pltpu.CompilerParams(collective_id=0, has_side_effects=True, vmem_limit_bytes=60 * 2**20),
        name="gather_weights",
    )(*[v[None] for v in vectors], b_up[None], *matrices)


class Scatter:
    def __init__(self, place, j, level, bufs, sems):
        self.p, self.j, self.level, self.sems = place, j, level, sems
        self.acc, self.got, self.one, self.two, self.give, self.line, self.low, self.high, self.fin = bufs
        p = place
        rail0 = p.c == 0
        self.me = p.y * 2 + p.x
        self.first = jnp.where(rail0, p.y * 2 + 1 - p.x, (1 - p.y) * 2 + p.x)
        self.second = jnp.where(rail0, (1 - p.y) * 2 + p.x, p.y * 2 + 1 - p.x)
        self.diag = (1 - p.y) * 2 + 1 - p.x
        self.to_first = (p.z, self.first * 2 + p.c)
        self.to_second = (p.z, self.second * 2 + p.c)

    def move(self, kind, l, src, dst, to):
        return push(src, dst, self.sems.at[0, kind, self.j, l], self.sems.at[1, kind, self.j, l], to)

    def own(self, l):
        return pltpu.make_async_copy(self.level(l, self.p.c), self.acc.at[l], self.sems.at[0, 0, self.j, l])

    def core(self, l):
        return self.move(1, l, self.level(l, 1 - self.p.c), self.got.at[l], self.p.to_core)

    def step1(self, l, slot):
        block = self.first if slot == 0 else self.diag
        return self.move(2 + slot, l, self.acc.at[l, block], self.one.at[l, slot], self.to_first)

    def step2(self, l):
        return self.move(4, l, self.give.at[l], self.two.at[l], self.to_second)

    def up(self, l):
        return self.move(5, l, self.line.at[l], self.low.at[l], self.p.to_z(1))

    def down(self, l):
        return self.move(6, l, self.line.at[l], self.high.at[l], self.p.to_z(3))

    def begin(self, l):
        self.core(l).start()
        self.own(l).start()

    def pair(self, l):
        self.own(l).wait()
        self.core(l).wait_recv()
        self.acc[l] = (self.acc[l].astype(F32) + self.got[l].astype(F32)).astype(BF)
        self.step1(l, 0).start()
        self.step1(l, 1).start()

    def side(self, l):
        self.step1(l, 1).wait_recv()
        self.give[l] = (self.acc[l, self.second].astype(F32) + self.one[l, 1].astype(F32)).astype(BF)
        self.step2(l).start()

    def plane_sum(self, l):
        return self.acc[l, self.me].astype(F32) + self.one[l, 0].astype(F32) + self.two[l].astype(F32)

    def plane(self, l):
        z = self.p.z
        self.step1(l, 0).wait_recv()
        self.step2(l).wait_recv()

        @pl.when(l > z)
        def _():
            @pl.when(z > 0)
            def _():
                self.up(l).wait_recv()
                self.line[l] = (self.plane_sum(l) + self.low[l].astype(F32)).astype(BF)

            @pl.when(z == 0)
            def _():
                self.line[l] = self.plane_sum(l).astype(BF)

            self.up(l).start()

        @pl.when(l < z)
        def _():
            @pl.when(z < 3)
            def _():
                self.down(l).wait_recv()
                self.line[l] = (self.plane_sum(l) + self.high[l].astype(F32)).astype(BF)

            @pl.when(z == 3)
            def _():
                self.line[l] = self.plane_sum(l).astype(BF)

            self.down(l).start()

    def last(self):
        z = self.p.z
        self.step1(z, 0).wait_recv()
        self.step2(z).wait_recv()
        self.fin[...] = self.plane_sum(z)

        @pl.when(z > 0)
        def _():
            self.up(z).wait_recv()
            self.fin[...] += self.low[z].astype(F32)

        @pl.when(z < 3)
        def _():
            self.down(z).wait_recv()
            self.fin[...] += self.high[z].astype(F32)

    def finish(self):
        z = self.p.z
        for l in range(4):
            self.core(l).wait_send()
            self.step1(l, 0).wait_send()
            self.step1(l, 1).wait_send()
            self.step2(l).wait_send()

            @pl.when(z < l)
            def _():
                self.up(l).wait_send()

            @pl.when(z > l)
            def _():
                self.down(l).wait_send()


def level_order(p):
    low = p.z < 2
    zz = jnp.where(low, p.z, 3 - p.z)
    order = [3, 2, 1 - zz, zz]
    return [jnp.where(low, l, 3 - l) for l in order]


def scatter_kernel(ga, gu, gd, vec, out_a, out_u, out_d, out_v, *refs):
    bufs = [refs[0:9], refs[9:18], refs[18:27]]
    hold, landed, sems, last_sems, vec_sems = refs[27:]
    p = Place()
    rail = ga.shape[2] // 2
    rows = ga.shape[1] // 2

    def by_lanes(ref):
        return lambda l, c: ref.at[pl.ds(l * 4, 4), :, pl.ds(pl.multiple_of(c * rail, TILE), rail)]

    jobs = [
        Scatter(p, 0, lambda l, c: gd.at[pl.ds(l * 4, 4), c], bufs[0], sems),
        Scatter(p, 1, by_lanes(gu), bufs[1], sems),
        Scatter(p, 2, by_lanes(ga), bufs[2], sems),
    ]
    greet(p)
    order = level_order(p)
    items = [(job, l) for l in order for job in jobs]
    for job, l in items:
        job.begin(l)
    steps = vector_steps(p, lambda: vec[...], out_v, hold, landed, vec_sems)
    count = len(items)
    for i in range(count + 2):
        if i < count:
            job, l = items[i]
            job.pair(l)
        if 1 <= i <= count:
            job, l = items[i - 1]
            job.side(l)
        if 2 <= i <= count + 1:
            job, l = items[i - 2]
            if i - 2 < count - 3:
                job.plane(l)
            else:
                job.last()
        if 1 <= i <= 5:
            steps[i - 1]()
    outs = (out_d, out_u, out_a)
    out_d[...] = jobs[0].fin[...]
    mine = pl.ds(pl.multiple_of(p.c * rail, TILE), rail)
    sends = []
    for i in (1, 2):
        fin, out = jobs[i].fin, outs[i]
        lanes = out.at[:, mine]
        cp = push(
            fin.at[pl.ds(pl.multiple_of((1 - p.c) * rows, 8), rows)], lanes,
            last_sems.at[0, i], last_sems.at[1, i], p.to_core,
        )
        cp.start()
        sends.append(cp)
        out[:, mine] = fin[pl.ds(pl.multiple_of(p.c * rows, 8), rows), :]
    for job in jobs:
        job.finish()
    for cp in sends:
        cp.wait()


def scatter_all(ga, gu, gd, vec):
    rows = ga.shape[1] // 2
    cols = ga.shape[2]
    rail = cols // 2
    depth, width = gd.shape[2], gd.shape[3]

    def bufs(r, n):
        return [
            pltpu.VMEM((4, 4, r, n), BF),
            pltpu.VMEM((4, 4, r, n), BF),
            pltpu.VMEM((4, 2, r, n), BF),
            pltpu.VMEM((4, r, n), BF),
            pltpu.VMEM((4, r, n), BF),
            pltpu.VMEM((4, r, n), BF),
            pltpu.VMEM((4, r, n), BF),
            pltpu.VMEM((4, r, n), BF),
            pltpu.VMEM((r, n), F32),
        ]

    return pl.pallas_call(
        scatter_kernel,
        out_shape=(
            jax.ShapeDtypeStruct((rows, cols), F32),
            jax.ShapeDtypeStruct((rows, cols), F32),
            jax.ShapeDtypeStruct((depth, width), F32),
            jax.ShapeDtypeStruct((16, width), F32),
        ),
        in_specs=[pl.BlockSpec(memory_space=pl.ANY)] * 3 + [pl.BlockSpec(memory_space=pltpu.VMEM)],
        out_specs=(pl.BlockSpec(memory_space=pltpu.VMEM),) * 4,
        scratch_shapes=bufs(depth, width) + bufs(2 * rows, rail) + bufs(2 * rows, rail) + [
            pltpu.VMEM((4, 16, width), F32),
            pltpu.VMEM((6, 16, width), F32),
            pltpu.SemaphoreType.DMA((2, 7, 3, 4)),
            pltpu.SemaphoreType.DMA((2, 3)),
            pltpu.SemaphoreType.DMA((2, 6)),
        ],
        compiler_params=pltpu.CompilerParams(collective_id=1, has_side_effects=True, vmem_limit_bytes=60 * 2**20),
        name="scatter_gradients",
    )(ga, gu, gd, vec)


HEAD = 64


EPSILON = 1e-06


def layer_norm(values, gain_vector, offset_vector):
    average = jnp.mean(values, axis=-1, keepdims=True)
    centred = values - average
    spread = jnp.mean(centred * centred, axis=-1, keepdims=True)
    return centred * lax.rsqrt(spread + EPSILON) * gain_vector + offset_vector


def allowed_pairs(segment_row, select_row):
    places = jnp.arange(segment_row.shape[0])
    return (segment_row[:, None] == segment_row[None, :]) & (
        (select_row[None, :] == 1) | (places[:, None] == places[None, :])
    )


def split_heads(values):
    return values.reshape(values.shape[0], values.shape[1] // HEAD, HEAD)


def attend_forward(entries):
    queries, key_rows, value_rows, segment_row, select_row = entries
    query_heads = split_heads(queries)
    key_heads = split_heads(key_rows)
    value_heads = split_heads(value_rows)
    scores = jnp.einsum(
        "qhd,khd->hqk", query_heads, key_heads, preferred_element_type=jnp.float32
    ) * (1.0 / math.sqrt(HEAD))
    allowed = allowed_pairs(segment_row, select_row)
    masked = jnp.where(allowed[None], scores, -1e30)
    top_score = jnp.max(masked, axis=-1, keepdims=True)
    expd = jnp.exp(masked - top_score)
    total = jnp.sum(expd, axis=-1, keepdims=True)
    soft_weights = (expd / total).astype(jnp.bfloat16)
    result = jnp.einsum(
        "hqk,khd->qhd", soft_weights, value_heads, preferred_element_type=jnp.float32
    )
    log_total = top_score[..., 0] + jnp.log(total[..., 0])
    return (result.reshape(queries.shape).astype(jnp.bfloat16), log_total)


def attend_backward(entries):
    queries, key_rows, value_rows, grad_attn, log_total, segment_row, select_row = entries
    query_heads = split_heads(queries)
    key_heads = split_heads(key_rows)
    value_heads = split_heads(value_rows)
    grad_heads = split_heads(grad_attn)
    key_scale = 1.0 / math.sqrt(HEAD)
    scores = (
        jnp.einsum("qhd,khd->hqk", query_heads, key_heads, preferred_element_type=jnp.float32)
        * key_scale
    )
    allowed = allowed_pairs(segment_row, select_row)
    soft_weights = jnp.where(allowed[None], jnp.exp(scores - log_total[..., None]), 0.0)
    grad_weights = jnp.einsum(
        "qhd,khd->hqk", grad_heads, value_heads, preferred_element_type=jnp.float32
    )
    inner_sum = jnp.sum(soft_weights * grad_weights, axis=-1, keepdims=True)
    grad_scores = (soft_weights * (grad_weights - inner_sum)).astype(jnp.bfloat16)
    grad_query = (
        jnp.einsum("hqk,khd->qhd", grad_scores, key_heads, preferred_element_type=jnp.float32)
        * key_scale
    )
    grad_key = (
        jnp.einsum("hqk,qhd->khd", grad_scores, query_heads, preferred_element_type=jnp.float32)
        * key_scale
    )
    grad_value = jnp.einsum(
        "hqk,qhd->khd",
        soft_weights.astype(jnp.bfloat16),
        grad_heads,
        preferred_element_type=jnp.float32,
    )
    shape_back = queries.shape
    return (
        grad_query.reshape(shape_back).astype(jnp.bfloat16),
        grad_key.reshape(shape_back).astype(jnp.bfloat16),
        grad_value.reshape(shape_back).astype(jnp.bfloat16),
    )


def project(left, right):
    return jnp.dot(left, right, preferred_element_type=jnp.float32)


def project_back(left, right):
    return jnp.einsum("te,de->td", left, right, preferred_element_type=jnp.float32)


def outer_sum(left, right):
    return jnp.einsum("td,te->de", left, right, preferred_element_type=jnp.float32)


def local(
    small,
    patches,
    segment_ids,
    selected,
    cotangent,
    ln1_gain,
    ln1_bias,
    w_router,
    w_query,
    b_query,
    w_key,
    w_value,
    b_value,
    w_out,
    b_out,
    ln2_gain,
    ln2_bias,
    w_up,
    b_up,
    w_down,
    b_down,
):
    vectors = (ln1_gain, ln1_bias, w_router, b_query, b_value, b_out, ln2_gain, ln2_bias, b_down)
    matrices = (w_query, w_key, w_value, w_out, w_up, w_down)
    if small:
        attn_w, up_w, down_w, table = gather_all(vectors, b_up, matrices)
        attn_w = attn_w.reshape(-1, attn_w.shape[2])
        up_w = up_w.reshape(-1, up_w.shape[2])
        down_w = down_w.reshape(-1, down_w.shape[3])
        table = table.astype(BF)
        full = [table[i] for i in range(VECTORS)] + [table[VECTORS : VECTORS + 4].reshape(-1)]
    else:
        full = [lax.all_gather(v, AXES, axis=0, tiled=True) for v in vectors + (b_up,)]
        attn_w = jnp.concatenate([lax.all_gather(w, AXES, axis=0, tiled=True) for w in matrices[:4]], axis=1)
        up_w = lax.all_gather(w_up, AXES, axis=0, tiled=True)
        down_w = lax.all_gather(w_down, AXES, axis=0, tiled=True)
    gain_one, bias_one, router, query_b, value_b, out_b, gain_two, bias_two, down_b, up_b = full
    query_w, key_w, value_w, out_w = jnp.split(attn_w, 4, axis=1)
    row_count, length, model_width = patches.shape
    token_count = row_count * length
    flat_tokens = patches.reshape(token_count, model_width).astype(jnp.float32)
    chosen = selected.reshape(-1).astype(jnp.float32)
    norm_one, ln1_pull = jax.vjp(
        layer_norm, flat_tokens, gain_one.astype(jnp.float32), bias_one.astype(jnp.float32)
    )
    hidden_in = norm_one.astype(jnp.bfloat16)
    router_score = jax.nn.sigmoid(jnp.dot(hidden_in, router, preferred_element_type=jnp.float32))
    queries = (project(hidden_in, query_w) + query_b.astype(jnp.float32)).astype(jnp.bfloat16)
    key_rows = project(hidden_in, key_w).astype(jnp.bfloat16)
    value_rows = (project(hidden_in, value_w) + value_b.astype(jnp.float32)).astype(jnp.bfloat16)
    row_shape = (row_count, length, model_width)
    attended, log_total = lax.map(
        attend_forward,
        (
            queries.reshape(row_shape),
            key_rows.reshape(row_shape),
            value_rows.reshape(row_shape),
            segment_ids,
            selected,
        ),
    )
    attended = attended.reshape(token_count, model_width)
    branch = project(attended, out_w) + out_b.astype(jnp.float32)
    gate_column = (chosen * router_score)[:, None]
    middle = flat_tokens + gate_column * branch
    norm_two, ln2_pull = jax.vjp(
        layer_norm, middle, gain_two.astype(jnp.float32), bias_two.astype(jnp.float32)
    )
    normed = norm_two.astype(jnp.bfloat16)
    pre_act = project(normed, up_w) + up_b.astype(jnp.float32)
    activation, gelu_pull = jax.vjp(partial(jax.nn.gelu, approximate=False), pre_act)
    act_low = activation.astype(jnp.bfloat16)
    result = middle + project(act_low, down_w) + down_b.astype(jnp.float32)
    mixed_out = result.astype(jnp.bfloat16).reshape(row_shape)
    grad_result = cotangent.reshape(token_count, model_width)
    grad_down_w = jnp.einsum("tf,td->fd", act_low, grad_result, preferred_element_type=jnp.float32)
    grad_down_b = jnp.sum(grad_result, axis=0, dtype=jnp.float32)
    grad_act = project_back(grad_result, down_w)
    grad_pre = gelu_pull(grad_act)[0].astype(jnp.bfloat16)
    grad_up_b = jnp.sum(grad_pre, axis=0, dtype=jnp.float32)
    grad_up_w = outer_sum(normed, grad_pre)
    grad_normed = project_back(grad_pre, up_w)
    grad_mid_norm, grad_gain_two, grad_bias_two = ln2_pull(grad_normed)
    grad_middle = grad_result.astype(jnp.float32) + grad_mid_norm
    grad_branch = (grad_middle * gate_column).astype(jnp.bfloat16)
    grad_score = jnp.sum(grad_middle * chosen[:, None] * branch, axis=-1)
    grad_logit = grad_score * router_score * (1.0 - router_score)
    grad_out_b = jnp.sum(grad_branch, axis=0, dtype=jnp.float32)
    grad_out_w = outer_sum(attended, grad_branch)
    grad_attn = project_back(grad_branch, out_w).astype(jnp.bfloat16)
    grad_query, grad_key, grad_value = lax.map(
        attend_backward,
        (
            queries.reshape(row_shape),
            key_rows.reshape(row_shape),
            value_rows.reshape(row_shape),
            grad_attn.reshape(row_shape),
            log_total,
            segment_ids,
            selected,
        ),
    )
    grad_query = grad_query.reshape(token_count, model_width)
    grad_key = grad_key.reshape(token_count, model_width)
    grad_value = grad_value.reshape(token_count, model_width)
    grad_query_b = jnp.sum(grad_query, axis=0, dtype=jnp.float32)
    grad_value_b = jnp.sum(grad_value, axis=0, dtype=jnp.float32)
    grad_query_w = outer_sum(hidden_in, grad_query)
    grad_key_w = outer_sum(hidden_in, grad_key)
    grad_value_w = outer_sum(hidden_in, grad_value)
    grad_router = jnp.sum(hidden_in * grad_logit[:, None], axis=0)
    grad_hidden = (
        project_back(grad_query, query_w)
        + project_back(grad_key, key_w)
        + project_back(grad_value, value_w)
        + grad_logit[:, None] * router.astype(jnp.float32)
    )
    grad_flat_norm, grad_gain_one, grad_bias_one = ln1_pull(grad_hidden)
    grad_patches = (grad_middle + grad_flat_norm).astype(jnp.bfloat16).reshape(row_shape)
    grad_vectors = (
        grad_gain_one, grad_bias_one, grad_router, grad_query_b, grad_value_b,
        grad_out_b, grad_gain_two, grad_bias_two, grad_down_b,
    )
    if small:
        grad_a = jnp.concatenate([grad_query_w, grad_key_w, grad_value_w, grad_out_w], axis=1).astype(BF)
        grad_u = grad_up_w.astype(BF)
        grad_d = grad_down_w.astype(BF)
        block = jnp.concatenate(
            [jnp.stack(grad_vectors), grad_up_b.reshape(4, -1), jnp.zeros((3, model_width), F32)]
        )
        own_a, own_u, own_d, own_v = scatter_all(
            grad_a.reshape(16, -1, grad_a.shape[1]),
            grad_u.reshape(16, -1, grad_u.shape[1]),
            grad_d.reshape(16, 2, -1, grad_d.shape[1]),
            block,
        )
        own_m = jnp.split(own_a, 4, axis=1) + [own_u, own_d]
        device = lax.axis_index("dp") * 8 + lax.axis_index("fsdp")
        part = ln1_gain.shape[0]
        mine = lax.dynamic_slice(own_v[:VECTORS], (0, device * part), (VECTORS, part))
        own = [mine[i] for i in range(VECTORS)]
        own_up_b = lax.dynamic_slice(own_v[VECTORS : VECTORS + 4].reshape(-1), (device * b_up.shape[0],), b_up.shape)
    else:
        own = [lax.psum_scatter(g, AXES, scatter_dimension=0, tiled=True) for g in grad_vectors]
        own_up_b = lax.psum_scatter(grad_up_b, AXES, scatter_dimension=0, tiled=True)
        own_m = [
            lax.psum_scatter(g, AXES, scatter_dimension=0, tiled=True)
            for g in (grad_query_w, grad_key_w, grad_value_w, grad_out_w, grad_up_w, grad_down_w)
        ]
    return (
        mixed_out, grad_patches, own[0], own[1], own[2], own_m[0], own[3], own_m[1], own_m[2], own[4],
        own_m[3], own[5], own[6], own[7], own_m[4], own_up_b, own_m[5], own[8],
    )


def solution(mesh):
    flat, rows2, rows3 = P(AXES), P(AXES, None), P(AXES, None, None)
    vec, mat = flat, rows2
    small = mesh.shape["dp"] == 4 and mesh.shape["fsdp"] == 8
    return jax.shard_map(
        partial(local, small),
        mesh=mesh,
        in_specs=(
            rows3, rows2, rows2, rows3, vec, vec, vec, mat, vec, mat, mat, vec, mat, vec, vec, vec, mat, vec, mat, vec,
        ),
        out_specs=(
            rows3, rows3, vec, vec, vec, mat, vec, mat, mat, vec, mat, vec, vec, vec, mat, vec, mat, vec,
        ),
        check_vma=False,
    )
```

```python
from functools import partial
import math

import jax
import jax.numpy as jnp
from jax import lax
from jax.experimental import pallas as pl
from jax.experimental.pallas import tpu as pltpu
from jax.sharding import PartitionSpec as P

AXES = ("dp", "fsdp")
MESH = pl.DeviceIdType.MESH
BF = jnp.bfloat16
F32 = jnp.float32


class Place:
    def __init__(self):
        self.z = lax.axis_index("dp")
        self.f = lax.axis_index("fsdp")
        self.c = lax.rem(self.f, 2)
        self.x = lax.rem(self.f // 2, 2)
        self.y = self.f // 4
        self.chip = self.z * 4 + self.y * 2 + self.x
        self.chip_x = self.z * 4 + self.y * 2 + (1 - self.x)
        self.chip_y = self.z * 4 + (1 - self.y) * 2 + self.x
        self.to_core = (self.z, self.y * 4 + self.x * 2 + (1 - self.c))
        self.to_x = (self.z, self.y * 4 + (1 - self.x) * 2 + self.c)
        self.to_y = (self.z, (1 - self.y) * 4 + self.x * 2 + self.c)

    def to_z(self, step):
        return (lax.rem(self.z + step + 4, 4), self.f)


def greet(place):
    bar = pltpu.get_barrier_semaphore()
    others = [place.to_core, place.to_x, place.to_y] + [place.to_z(s) for s in (1, 2, 3)]
    for other in others:
        pl.semaphore_signal(bar, inc=1, device_id=other, device_id_type=MESH)
    pl.semaphore_wait(bar, len(others))


def push(src, dst, send, recv, to):
    return pltpu.make_async_remote_copy(
        src_ref=src, dst_ref=dst, send_sem=send, recv_sem=recv, device_id=to, device_id_type=MESH
    )


class Gather:
    def __init__(self, place, j, block, level, plane_first, sems):
        self.p, self.j, self.block, self.level, self.sems = place, j, block, level, sems
        self.plane_first = plane_first

    def copy(self, kind, i, ref, to):
        return push(ref, ref, self.sems.at[2 * kind, self.j, i], self.sems.at[2 * kind + 1, self.j, i], to)

    def piece(self, l):
        if self.plane_first:
            return self.level(l, self.p.c)
        return self.block(l * 4 + self.p.y * 2 + self.p.x)

    def up(self, k):
        return self.copy(0, k, self.piece(lax.rem(self.p.z - k + 4, 4)), self.p.to_z(1))

    def up_in(self, k):
        return self.copy(0, k, self.piece(lax.rem(self.p.z - k + 3, 4)), self.p.to_z(1))

    def down(self, k):
        return self.copy(1, k, self.piece(lax.rem(self.p.z + k, 4)), self.p.to_z(3))

    def down_in(self, k):
        return self.copy(1, k, self.piece(lax.rem(self.p.z + k + 1, 4)), self.p.to_z(3))

    def xs(self, l):
        return self.copy(2, l, self.block(l * 4 + self.p.y * 2 + self.p.x), self.p.to_x)

    def ys(self, l):
        return self.copy(3, l, self.block(l * 4 + self.p.y * 2 + self.p.x), self.p.to_y)

    def side_in(self, l, y_side):
        p = self.p
        chip = l * 4 + (p.y + y_side - 2 * p.y * y_side) * 2 + (p.x + (1 - y_side) - 2 * p.x * (1 - y_side))
        return self.copy(2 + y_side, l, self.block(chip), p.to_x)

    def forward(self, l):
        p = self.p
        chip = l * 4 + jnp.where(p.c == 0, (1 - p.y) * 2 + p.x, p.y * 2 + 1 - p.x)
        to = (p.z, jnp.where(p.c == 0, p.y * 4 + (1 - p.x) * 2 + p.c, (1 - p.y) * 4 + p.x * 2 + p.c))
        return self.copy(4, l, self.block(chip), to)

    def forward_in(self, l):
        return self.copy(4, l, self.block(l * 4 + (1 - self.p.y) * 2 + 1 - self.p.x), self.p.to_x)

    def cs(self, l):
        return self.copy(5, l, self.level(l, self.p.c), self.p.to_core)

    def cs_in(self, l):
        return self.copy(5, l, self.level(l, 1 - self.p.c), self.p.to_core)

    def sides(self, l):
        self.xs(l).start()
        self.ys(l).start()

    def ends(self, k):
        z = self.p.z

        @pl.when((z >= k) & (z < 3))
        def _():
            self.up(k).start()

        @pl.when((z + k <= 3) & (z > 0))
        def _():
            self.down(k).start()

    def begin(self):
        if not self.plane_first:
            self.ends(0)
        self.sides(self.p.z)

    def along_z(self, k):
        z = self.p.z

        @pl.when(z > k)
        def _():
            self.up_in(k).wait_recv()

        @pl.when(z + k < 3)
        def _():
            self.down_in(k).wait_recv()

        if k < 2:
            self.ends(k + 1)
        self.each(k + 1, (lambda l: self.cs(l).start()) if self.plane_first else self.sides)

    def each(self, k, what):
        z = self.p.z
        if k == 0:
            what(z)
            return

        @pl.when(z >= k)
        def _():
            what(z - k)

        @pl.when(z + k <= 3)
        def _():
            what(z + k)

    def turn(self, l):
        self.side_in(l, 1 - self.p.c).wait_recv()
        self.forward(l).start()
        self.side_in(l, self.p.c).wait_recv()

    def across(self, l):
        self.forward_in(l).wait_recv()
        if self.plane_first:
            self.ends(0)
        self.cs(l).start()

    def finish(self):
        z = self.p.z
        for l in range(4):
            if self.plane_first:
                continue
            self.xs(l).wait_send()
            self.ys(l).wait_send()
            self.forward(l).wait_send()
        if self.plane_first:
            self.xs(z).wait_send()
            self.ys(z).wait_send()
            self.forward(z).wait_send()
        for l in range(4):
            self.cs(l).wait_send()
            self.cs_in(l).wait_recv()
        for k in range(3):

            @pl.when((z >= k) & (z < 3))
            def _():
                self.up(k).wait_send()

            @pl.when((z + k <= 3) & (z > 0))
            def _():
                self.down(k).wait_send()


VECTORS = 9
TILE = 128


def vector_steps(p, values, out_ref, hold, landed, sems):
    send, recv = sems.at[0], sems.at[1]
    state = {}

    def begin():
        state["value"] = values()
        hold[0] = state["value"]
        push(hold.at[0], landed.at[0], send.at[0], recv.at[0], p.to_core).start()

    def then(i, to, after):
        def step():
            push(hold.at[i], landed.at[i], send.at[i], recv.at[i], to).wait()
            hold[i + 1] = hold[i] + landed[i]
            after()
        return step

    def next_side():
        push(hold.at[1], landed.at[1], send.at[1], recv.at[1], p.to_x).start()

    def next_other():
        push(hold.at[2], landed.at[2], send.at[2], recv.at[2], p.to_y).start()

    def line(s):
        return push(hold.at[3], landed.at[2 + s], send.at[2 + s], recv.at[2 + s], p.to_z(s))

    def next_line():
        for s in (1, 2, 3):
            line(s).start()

    def last():
        for s in (1, 2, 3):
            line(s).wait()
        out_ref[...] = hold[3] + landed[3] + landed[4] + landed[5]

    return [begin, then(0, p.to_core, next_side), then(1, p.to_x, next_other), then(2, p.to_y, next_line), last]


def cut(cols, share):
    first = int(round(cols * (1 - share) / TILE)) * TILE
    return first


PLANE_SHARE = 0.12


def gather_kernel(*refs):
    vectors, b_up = refs[:VECTORS], refs[VECTORS]
    wq, wk, wv, wo, wu, wd = refs[VECTORS + 1 : VECTORS + 7]
    out_a, out_u, out_d, out_v = refs[VECTORS + 7 : VECTORS + 11]
    held, give, take, packed, hold, landed, sems, pair_sems, own_sems, vec_sems = refs[VECTORS + 11 :]
    p = Place()
    width = wq.shape[1]
    rail = 2 * width
    rows = wq.shape[0]
    lower = p.c == 0
    loads = [pltpu.make_async_copy(w, held.at[0, :, pl.ds(i * width, width)], own_sems.at[3 + i]) for i, w in enumerate((wq, wk, wv, wo))]
    loads.append(pltpu.make_async_copy(wu, held.at[1], own_sems.at[7]))
    own_d = pltpu.make_async_copy(wd, out_d.at[p.chip, p.c], own_sems.at[2])
    for cp in loads:
        cp.start()
    own_d.start()
    greet(p)
    for cp in loads:
        cp.wait()
    mine = pl.ds(pl.multiple_of(p.c * rail, TILE), rail)
    other = pl.ds(pl.multiple_of((1 - p.c) * rail, TILE), rail)
    pair = []
    for i in range(2):
        give[i] = held[i, :, other].astype(F32)
        pair.append(push(give.at[i], take.at[i], pair_sems.at[0, i], pair_sems.at[1, i], p.to_core))
        pair[i].start()
    jobs = []

    def add_jobs(out, rail_cols, columns_by_rail):
        first = cut(rail_cols, PLANE_SHARE)
        for start, size, plane in ((0, first, False), (first, rail_cols - first, True)):
            if size == 0:
                continue
            if columns_by_rail:
                def lanes(c, start=start, size=size):
                    return pl.ds(pl.multiple_of(c * rail_cols + start, TILE), size)
                block = lambda chip, out=out, lanes=lanes: out.at[chip, :, lanes(p.c)]
                level = lambda l, c, out=out, lanes=lanes: out.at[pl.ds(l * 4, 4), :, lanes(c)]
            else:
                lane = pl.ds(start, size)
                block = lambda chip, out=out, lane=lane: out.at[chip, p.c, :, lane]
                level = lambda l, c, out=out, lane=lane: out.at[pl.ds(l * 4, 4), c, :, lane]
            jobs.append(Gather(p, len(jobs), block, level, plane, sems))

    add_jobs(out_a, rail, True)
    add_jobs(out_u, rail, True)
    add_jobs(out_d, width, False)
    own_d.wait()
    per = len(jobs) // 3
    for job in jobs[: 2 * per - 1 : -1]:
        job.begin()
    for i, out in enumerate((out_a, out_u)):
        pair[i].wait()
        own = held[i, :, mine].astype(F32)
        got = take[i]
        packed[i] = jnp.concatenate([jnp.where(lower, own, got), jnp.where(lower, got, own)], axis=0).astype(BF)
        cp = pltpu.make_async_copy(packed.at[i], out.at[p.chip, :, mine], own_sems.at[i])
        cp.start()
        cp.wait()
        for job in jobs[i * per : (i + 1) * per][::-1]:
            job.begin()
    device = p.z * 8 + p.f

    def spread(ref):
        count = ref.shape[1]
        total = count * 32
        lane = lax.broadcasted_iota(jnp.int32, (count, total), 1)
        row = lax.broadcasted_iota(jnp.int32, (count, total), 0)
        place = (lane == row + device * count).astype(BF)
        return jnp.dot(ref[...], place, preferred_element_type=F32)

    def values():
        rows_of = [spread(v) for v in vectors]
        up = spread(b_up)
        rows_of += [up[:, i * width : (i + 1) * width] for i in range(4)]
        rows_of.append(jnp.zeros((3, width), F32))
        return jnp.concatenate(rows_of, axis=0)

    steps = vector_steps(p, values, out_v, hold, landed, vec_sems)
    steps[0]()
    plane = [job for job in jobs if job.plane_first]
    line = [job for job in jobs if not job.plane_first]
    for job in plane:
        job.turn(p.z)
    steps[1]()
    for job in plane:
        job.across(p.z)
    for k in range(4):
        if k < 3:
            for job in line + plane:
                job.along_z(k)
        if k < 3:
            steps[k + 2]()
        for job in line:
            job.each(k, job.turn)
        for job in line:
            job.each(k, job.across)
    for job in jobs:
        job.finish()


def gather_all(vectors, b_up, matrices):
    wq, wd = matrices[0], matrices[5]
    rows, width = wq.shape
    rail = 2 * width
    depth = wd.shape[0]
    return pl.pallas_call(
        gather_kernel,
        out_shape=(
            jax.ShapeDtypeStruct((16, 2 * rows, 4 * width), BF),
            jax.ShapeDtypeStruct((16, 2 * rows, 4 * width), BF),
            jax.ShapeDtypeStruct((16, 2, depth, width), BF),
            jax.ShapeDtypeStruct((16, width), F32),
        ),
        in_specs=[pl.BlockSpec(memory_space=pltpu.VMEM)] * (VECTORS + 1) + [pl.BlockSpec(memory_space=pl.ANY)] * 6,
        out_specs=(pl.BlockSpec(memory_space=pl.ANY),) * 3 + (pl.BlockSpec(memory_space=pltpu.VMEM),),
        scratch_shapes=[
            pltpu.VMEM((2, rows, 2 * rail), BF),
            pltpu.VMEM((2, rows, rail), F32),
            pltpu.VMEM((2, rows, rail), F32),
            pltpu.VMEM((2, 2 * rows, rail), BF),
            pltpu.VMEM((4, 16, width), F32),
            pltpu.VMEM((6, 16, width), F32),
            pltpu.SemaphoreType.DMA((12, 6, 4)),
            pltpu.SemaphoreType.DMA((2, 2)),
            pltpu.SemaphoreType.DMA((8,)),
            pltpu.SemaphoreType.DMA((2, 6)),
        ],
        compiler_params=pltpu.CompilerParams(collective_id=0, has_side_effects=True, vmem_limit_bytes=60 * 2**20),
        name="gather_weights",
    )(*[v[None] for v in vectors], b_up[None], *matrices)


class Scatter:
    def __init__(self, place, j, level, bufs, sems):
        self.p, self.j, self.level, self.sems = place, j, level, sems
        self.acc, self.got, self.one, self.two, self.give, self.line, self.low, self.high, self.fin = bufs
        p = place
        rail0 = p.c == 0
        self.me = p.y * 2 + p.x
        self.first = jnp.where(rail0, p.y * 2 + 1 - p.x, (1 - p.y) * 2 + p.x)
        self.second = jnp.where(rail0, (1 - p.y) * 2 + p.x, p.y * 2 + 1 - p.x)
        self.diag = (1 - p.y) * 2 + 1 - p.x
        self.to_first = (p.z, self.first * 2 + p.c)
        self.to_second = (p.z, self.second * 2 + p.c)

    def move(self, kind, l, src, dst, to):
        return push(src, dst, self.sems.at[0, kind, self.j, l], self.sems.at[1, kind, self.j, l], to)

    def own(self, l):
        return pltpu.make_async_copy(self.level(l, self.p.c), self.acc.at[l], self.sems.at[0, 0, self.j, l])

    def core(self, l):
        return self.move(1, l, self.level(l, 1 - self.p.c), self.got.at[l], self.p.to_core)

    def step1(self, l, slot):
        block = self.first if slot == 0 else self.diag
        return self.move(2 + slot, l, self.acc.at[l, block], self.one.at[l, slot], self.to_first)

    def step2(self, l):
        return self.move(4, l, self.give.at[l], self.two.at[l], self.to_second)

    def up(self, l):
        return self.move(5, l, self.line.at[l], self.low.at[l], self.p.to_z(1))

    def down(self, l):
        return self.move(6, l, self.line.at[l], self.high.at[l], self.p.to_z(3))

    def begin(self, l):
        self.core(l).start()
        self.own(l).start()

    def pair(self, l):
        self.own(l).wait()
        self.core(l).wait_recv()
        self.acc[l] = (self.acc[l].astype(F32) + self.got[l].astype(F32)).astype(BF)
        self.step1(l, 0).start()
        self.step1(l, 1).start()

    def side(self, l):
        self.step1(l, 1).wait_recv()
        self.give[l] = (self.acc[l, self.second].astype(F32) + self.one[l, 1].astype(F32)).astype(BF)
        self.step2(l).start()

    def plane_sum(self, l):
        return self.acc[l, self.me].astype(F32) + self.one[l, 0].astype(F32) + self.two[l].astype(F32)

    def plane(self, l):
        z = self.p.z
        self.step1(l, 0).wait_recv()
        self.step2(l).wait_recv()

        @pl.when(l > z)
        def _():
            @pl.when(z > 0)
            def _():
                self.up(l).wait_recv()
                self.line[l] = (self.plane_sum(l) + self.low[l].astype(F32)).astype(BF)

            @pl.when(z == 0)
            def _():
                self.line[l] = self.plane_sum(l).astype(BF)

            self.up(l).start()

        @pl.when(l < z)
        def _():
            @pl.when(z < 3)
            def _():
                self.down(l).wait_recv()
                self.line[l] = (self.plane_sum(l) + self.high[l].astype(F32)).astype(BF)

            @pl.when(z == 3)
            def _():
                self.line[l] = self.plane_sum(l).astype(BF)

            self.down(l).start()

    def last(self):
        z = self.p.z
        self.step1(z, 0).wait_recv()
        self.step2(z).wait_recv()
        self.fin[...] = self.plane_sum(z)

        @pl.when(z > 0)
        def _():
            self.up(z).wait_recv()
            self.fin[...] += self.low[z].astype(F32)

        @pl.when(z < 3)
        def _():
            self.down(z).wait_recv()
            self.fin[...] += self.high[z].astype(F32)

    def finish(self):
        z = self.p.z
        for l in range(4):
            self.core(l).wait_send()
            self.step1(l, 0).wait_send()
            self.step1(l, 1).wait_send()
            self.step2(l).wait_send()

            @pl.when(z < l)
            def _():
                self.up(l).wait_send()

            @pl.when(z > l)
            def _():
                self.down(l).wait_send()


def level_order(p):
    low = p.z < 2
    zz = jnp.where(low, p.z, 3 - p.z)
    order = [3, 2, 1 - zz, zz]
    return [jnp.where(low, l, 3 - l) for l in order]


def scatter_kernel(ga, gu, gd, vec, out_a, out_u, out_d, out_v, *refs):
    bufs = [refs[0:9], refs[9:18], refs[18:27]]
    hold, landed, sems, last_sems, vec_sems = refs[27:]
    p = Place()
    rail = ga.shape[2] // 2
    rows = ga.shape[1] // 2

    def by_lanes(ref):
        return lambda l, c: ref.at[pl.ds(l * 4, 4), :, pl.ds(pl.multiple_of(c * rail, TILE), rail)]

    jobs = [
        Scatter(p, 0, lambda l, c: gd.at[pl.ds(l * 4, 4), c], bufs[0], sems),
        Scatter(p, 1, by_lanes(gu), bufs[1], sems),
        Scatter(p, 2, by_lanes(ga), bufs[2], sems),
    ]
    greet(p)
    order = level_order(p)
    items = [(job, l) for l in order for job in jobs]
    for job, l in items:
        job.begin(l)
    steps = vector_steps(p, lambda: vec[...], out_v, hold, landed, vec_sems)
    count = len(items)
    for i in range(count + 2):
        if i < count:
            job, l = items[i]
            job.pair(l)
        if 1 <= i <= count:
            job, l = items[i - 1]
            job.side(l)
        if 2 <= i <= count + 1:
            job, l = items[i - 2]
            if i - 2 < count - 3:
                job.plane(l)
            else:
                job.last()
        if 1 <= i <= 5:
            steps[i - 1]()
    outs = (out_d, out_u, out_a)
    out_d[...] = jobs[0].fin[...]
    mine = pl.ds(pl.multiple_of(p.c * rail, TILE), rail)
    sends = []
    for i in (1, 2):
        fin, out = jobs[i].fin, outs[i]
        lanes = out.at[:, mine]
        cp = push(
            fin.at[pl.ds(pl.multiple_of((1 - p.c) * rows, 8), rows)], lanes,
            last_sems.at[0, i], last_sems.at[1, i], p.to_core,
        )
        cp.start()
        sends.append(cp)
        out[:, mine] = fin[pl.ds(pl.multiple_of(p.c * rows, 8), rows), :]
    for job in jobs:
        job.finish()
    for cp in sends:
        cp.wait()


def scatter_all(ga, gu, gd, vec):
    rows = ga.shape[1] // 2
    cols = ga.shape[2]
    rail = cols // 2
    depth, width = gd.shape[2], gd.shape[3]

    def bufs(r, n):
        return [
            pltpu.VMEM((4, 4, r, n), BF),
            pltpu.VMEM((4, 4, r, n), BF),
            pltpu.VMEM((4, 2, r, n), BF),
            pltpu.VMEM((4, r, n), BF),
            pltpu.VMEM((4, r, n), BF),
            pltpu.VMEM((4, r, n), BF),
            pltpu.VMEM((4, r, n), BF),
            pltpu.VMEM((4, r, n), BF),
            pltpu.VMEM((r, n), F32),
        ]

    return pl.pallas_call(
        scatter_kernel,
        out_shape=(
            jax.ShapeDtypeStruct((rows, cols), F32),
            jax.ShapeDtypeStruct((rows, cols), F32),
            jax.ShapeDtypeStruct((depth, width), F32),
            jax.ShapeDtypeStruct((16, width), F32),
        ),
        in_specs=[pl.BlockSpec(memory_space=pl.ANY)] * 3 + [pl.BlockSpec(memory_space=pltpu.VMEM)],
        out_specs=(pl.BlockSpec(memory_space=pltpu.VMEM),) * 4,
        scratch_shapes=bufs(depth, width) + bufs(2 * rows, rail) + bufs(2 * rows, rail) + [
            pltpu.VMEM((4, 16, width), F32),
            pltpu.VMEM((6, 16, width), F32),
            pltpu.SemaphoreType.DMA((2, 7, 3, 4)),
            pltpu.SemaphoreType.DMA((2, 3)),
            pltpu.SemaphoreType.DMA((2, 6)),
        ],
        compiler_params=pltpu.CompilerParams(collective_id=1, has_side_effects=True, vmem_limit_bytes=60 * 2**20),
        name="scatter_gradients",
    )(ga, gu, gd, vec)


HEAD = 64
EPSILON = 1e-06
LANES = 128
FAR = -1e30
GAIN1, BIAS1, ROUTER, B_QUERY, B_VALUE, B_OUT, GAIN2, BIAS2, B_DOWN, B_UP = range(10)


def dot(a, b):
    return lax.dot_general(a, b, (((1,), (0,)), ((), ())), preferred_element_type=F32)


def dot_nt(a, b):
    return lax.dot_general(a, b, (((1,), (1,)), ((), ())), preferred_element_type=F32)


def dot_tn(a, b):
    return lax.dot_general(a, b, (((0,), (0,)), ((), ())), preferred_element_type=F32)


def up_to(count, step):
    return (count + step - 1) // step * step


def iota(shape, dim):
    return lax.broadcasted_iota(jnp.int32, shape, dim)


def normalized(x):
    centred = x - jnp.mean(x, axis=-1, keepdims=True)
    scale = lax.rsqrt(jnp.mean(centred * centred, axis=-1, keepdims=True) + EPSILON)
    return centred * scale, scale


def norm_back(n, scale, gain, e):
    eg = e * gain
    return scale * (eg - jnp.mean(eg, axis=-1, keepdims=True) - n * jnp.mean(eg * n, axis=-1, keepdims=True))


def column_of(row, size):
    eye = iota((size, size), 0) == iota((size, size), 1)
    return jnp.sum(jnp.where(eye, jnp.broadcast_to(row, (size, size)), 0.0), axis=1, keepdims=True)


def order_of(picked_ref, order_ref):
    cap = picked_ref.shape[1]
    before = jnp.where(iota((cap, cap), 0) < iota((cap, cap), 1), 1.0, 0.0).astype(BF)
    order_ref[...] = dot(picked_ref[...].astype(BF), before)


def pad_rows(selected, segment, picked_ref, marks_ref):
    count, length = selected.shape
    picked_ref[...] = jnp.zeros_like(picked_ref)
    picked_ref[0:count, 0:length] = selected[...].astype(F32)
    if marks_ref is not None:
        marks_ref[...] = jnp.zeros_like(marks_ref)
        marks_ref[0:count, 0:length] = segment[...].astype(F32)


def row_of(ref, r):
    return jnp.sum(jnp.where(iota(ref.shape, 0) == r, ref[...], 0.0), axis=0, keepdims=True)


def to_picked(order, picked, size):
    cap = order.shape[1]
    hit = (order == iota((size, cap), 0).astype(F32)) & (picked > 0.5)
    return jnp.where(hit, 1.0, 0.0)


def from_picked(order, picked, size):
    cap = order.shape[1]
    place = column_of(jnp.where(picked > 0.5, order, -1.0), cap)
    return jnp.where(place == iota((cap, size), 1).astype(F32), 1.0, 0.0).astype(BF)


def sizes(cap):
    return [(w, up_to(w, LANES)) for w in range(LANES + HEAD, cap, LANES) if w < cap - LANES] + [(cap, cap)]


def each_size(count, cap, what):
    low = 0
    for rows, keys in sizes(cap):

        @pl.when((count > low) & (count <= rows))
        def _(rows=rows, keys=keys):
            what(rows, keys)

        low = rows


def forbidden(hit, marks, count, size):
    segment_of = dot_nt(jnp.broadcast_to(marks, (8, marks.shape[1])).astype(BF), hit.astype(BF))[0:1]
    segment_of = jnp.where(iota((1, size), 1) < count, segment_of, 99.0)
    column = jnp.sum(hit * marks, axis=1, keepdims=True)
    column = jnp.where(iota((size, 1), 0) < count, column, 99.0)
    return jnp.where(column == segment_of, 0.0, FAR)


def two_heads(pair):
    first = iota(pair.shape, 1) < HEAD
    zero = jnp.zeros_like(pair)
    return jnp.concatenate([jnp.where(first, pair, zero), jnp.where(first, zero, pair)], axis=0)


def one_pair(turned):
    size = turned.shape[1] // 2
    return jnp.concatenate([turned[:HEAD, :size], turned[HEAD:, size:]], axis=0).T


def attend_kernel(x, segment, selected, wa, table, mid, xc, h, qkv, attn, branch, logs, gates, xs, picked, marks, order, bar):
    cap = xs.shape[0]
    length, width = x.shape[1], x.shape[2]
    span = mid.shape[1]
    pad_rows(selected, segment, picked, marks)
    order_of(picked, order)
    xs[...] = jnp.zeros_like(xs)

    def row(r, carry):
        sel, place, mark = row_of(picked, r), row_of(order, r), row_of(marks, r)
        count = jnp.sum(sel).astype(jnp.int32)
        xs[0:length, :] = x[r]
        mid[r] = xs[0:span, :].astype(F32)

        def work(rows, keys):
            hit = to_picked(place, sel, keys)
            block = forbidden(hit, mark, count, keys)
            bar[0:keys, 0:keys] = block
            bar[0:keys, keys : 2 * keys] = block
            x_in = dot(hit[:rows].astype(BF), xs[...])
            xc[r, 0:rows, :] = x_in.astype(BF)
            n, _ = normalized(x_in)
            h_in = (n * table[GAIN1 : GAIN1 + 1, :] + table[BIAS1 : BIAS1 + 1, :]).astype(BF)
            h[r, 0:rows, :] = h_in
            gate = jax.nn.sigmoid(jnp.sum(h_in.astype(F32) * table[ROUTER : ROUTER + 1, :], axis=1, keepdims=True))
            for i, b in enumerate((B_QUERY, None, B_VALUE)):
                part = dot(h_in, wa[:, i * width : (i + 1) * width])
                if b is not None:
                    part = part + table[b : b + 1, :]
                qkv[r, 0:rows, i * width : (i + 1) * width] = part.astype(BF)
            if keys > rows:
                qkv[r, rows:keys, :] = jnp.zeros((keys - rows, 3 * width), BF)

            def pair(i, carry):
                lane = i * LANES
                q = qkv[r, 0:keys, pl.ds(pl.multiple_of(lane, LANES), LANES)]
                k = qkv[r, 0:keys, pl.ds(pl.multiple_of(lane + width, LANES), LANES)]
                v = qkv[r, 0:keys, pl.ds(pl.multiple_of(lane + 2 * width, LANES), LANES)]
                s = dot_nt(k, two_heads(q * BF(HEAD**-0.5))) + bar[0:keys, 0 : 2 * keys]
                top = jnp.max(s, axis=0, keepdims=True)
                e = jnp.exp(s - top)
                total = jnp.sum(e, axis=0, keepdims=True)
                out = one_pair(dot_tn(v, e.astype(BF)) * (1.0 / total))
                attn[r, 0:keys, pl.ds(pl.multiple_of(lane, LANES), LANES)] = out.astype(BF)
                logs[r, i, 0:1, 0 : 2 * keys] = top + jnp.log(total)
                return carry

            lax.fori_loop(0, width // LANES, pair, 0)
            gates[r, 0:rows, :] = jnp.broadcast_to(gate, (rows, LANES))
            out = dot(attn[r, 0:rows, :], wa[:, 3 * width :]) + table[B_OUT : B_OUT + 1, :]
            branch[r, 0:rows, :] = out.astype(BF)
            back = from_picked(place, sel, keys)[:span, :rows]
            mid[r] += dot(back, (out * gate).astype(BF))

        each_size(count, cap, work)
        return carry

    lax.fori_loop(0, x.shape[0], row, 0)


def attend(patches, segment, selected, wa, table):
    count, length, width = patches.shape
    cap, span = up_to(length, LANES), up_to(length, 16)

    def out(cols, kind):
        return jax.ShapeDtypeStruct((count, cap, cols), kind)

    return pl.pallas_call(
        attend_kernel,
        out_shape=(
            jax.ShapeDtypeStruct((count, span, width), F32),
            out(width, BF), out(width, BF), out(3 * width, BF), out(width, BF), out(width, BF),
            jax.ShapeDtypeStruct((count, width // LANES, 1, 2 * cap), F32),
            out(LANES, F32),
        ),
        in_specs=[pl.BlockSpec(memory_space=pltpu.VMEM)] * 5,
        out_specs=(pl.BlockSpec(memory_space=pltpu.VMEM),) * 8,
        scratch_shapes=[
            pltpu.VMEM((cap, width), BF),
            pltpu.VMEM((8, cap), F32),
            pltpu.VMEM((8, cap), F32),
            pltpu.VMEM((8, cap), F32),
            pltpu.VMEM((cap, 2 * cap), F32),
        ],
        compiler_params=pltpu.CompilerParams(vmem_limit_bytes=60 * 2**20),
        name="attend",
    )(patches, segment, selected, wa, table)


def attend_back_kernel(
    gm, segment, selected, wa, table, xc, h, qkv, attn, branch, logs, gates,
    grad_x, grad_a, sums, high, picked, marks, order, bar, ga, dqkv,
):
    cap = high.shape[0]
    span, width = gm.shape[1], gm.shape[2]
    length = grad_x.shape[1]
    pad_rows(selected, segment, picked, marks)
    order_of(picked, order)
    high[...] = jnp.zeros_like(high)
    grad_a[...] = jnp.zeros_like(grad_a)
    sums[...] = jnp.zeros_like(sums)

    def add(i, v):
        sums[i : i + 1, :] += jnp.sum(v, axis=0, keepdims=True)

    def add_weight(i, j, v):
        at = slice(i * width, j * width)
        grad_a[:, at] = (grad_a[:, at].astype(F32) + v).astype(BF)

    def row(r, carry):
        sel, place, mark = row_of(picked, r), row_of(order, r), row_of(marks, r)
        count = jnp.sum(sel).astype(jnp.int32)
        high[0:span, :] = gm[r].astype(BF)

        @pl.when(count == 0)
        def _():
            grad_x[r] = gm[r].astype(BF)[:length]

        def work(rows, keys):
            hit = to_picked(place, sel, keys)
            block = forbidden(hit, mark, count, keys)
            bar[0:keys, 0:keys] = block
            bar[0:keys, keys : 2 * keys] = block
            take = hit[:rows].astype(BF)
            g = dot(take, high[...])
            gate = gates[r, 0:rows, 0:1]
            grad_logit = jnp.sum(g * branch[r, 0:rows, :].astype(F32), axis=1, keepdims=True) * gate * (1.0 - gate)
            gb = g * gate
            add(B_OUT, gb.astype(BF).astype(F32))
            gb = gb.astype(BF)
            add_weight(3, 4, dot_tn(attn[r, 0:rows, :], gb))
            ga[0:rows, :] = dot_nt(gb, wa[:, 3 * width :]).astype(BF)
            if keys > rows:
                ga[rows:keys, :] = jnp.zeros((keys - rows, width), BF)

            def pair(i, carry):
                at = pl.ds(pl.multiple_of(i * LANES, LANES), LANES)
                at_k = pl.ds(pl.multiple_of(i * LANES + width, LANES), LANES)
                at_v = pl.ds(pl.multiple_of(i * LANES + 2 * width, LANES), LANES)
                q2 = two_heads(qkv[r, 0:keys, at] * BF(HEAD**-0.5))
                k = qkv[r, 0:keys, at_k]
                v = qkv[r, 0:keys, at_v]
                g2 = two_heads(ga[0:keys, at])
                p = jnp.exp(dot_nt(k, q2) + bar[0:keys, 0 : 2 * keys] - logs[r, i, 0:1, 0 : 2 * keys])
                dp = dot_nt(v, g2)
                ds = (p * (dp - jnp.sum(p * dp, axis=0, keepdims=True))).astype(BF)
                dqkv[0:keys, at] = one_pair(dot_tn(k, ds) * HEAD**-0.5).astype(BF)
                dqkv[0:keys, at_k] = dot(ds, q2).astype(BF)
                dqkv[0:keys, at_v] = dot(p.astype(BF), g2).astype(BF)
                return carry

            lax.fori_loop(0, width // LANES, pair, 0)
            add(B_QUERY, dqkv[0:rows, 0:width].astype(F32))
            add(B_VALUE, dqkv[0:rows, 2 * width :].astype(F32))
            h_in = h[r, 0:rows, :]
            add(ROUTER, h_in.astype(F32) * grad_logit)
            add_weight(0, 3, dot_tn(h_in, dqkv[0:rows, :]))
            gh = dot_nt(dqkv[0:rows, :], wa[:, : 3 * width]) + grad_logit * table[ROUTER : ROUTER + 1, :]
            n, scale = normalized(xc[r, 0:rows, :].astype(F32))
            add(GAIN1, n * gh)
            add(BIAS1, gh)
            dx = norm_back(n, scale, table[GAIN1 : GAIN1 + 1, :], gh).astype(BF)
            back = from_picked(place, sel, keys)[:span, :rows]
            grad_x[r] = (gm[r] + dot(back, dx)).astype(BF)[:length]

        each_size(count, cap, work)
        return carry

    lax.fori_loop(0, gm.shape[0], row, 0)


def attend_back(gm, segment, selected, wa, table, kept):
    count, span, width = gm.shape
    length = segment.shape[1]
    cap = up_to(length, LANES)
    return pl.pallas_call(
        attend_back_kernel,
        out_shape=(
            jax.ShapeDtypeStruct((count, length, width), BF),
            jax.ShapeDtypeStruct(wa.shape, BF),
            jax.ShapeDtypeStruct((16, width), F32),
        ),
        in_specs=[pl.BlockSpec(memory_space=pltpu.VMEM)] * 12,
        out_specs=(pl.BlockSpec(memory_space=pltpu.VMEM),) * 3,
        scratch_shapes=[
            pltpu.VMEM((cap, width), BF),
            pltpu.VMEM((8, cap), F32),
            pltpu.VMEM((8, cap), F32),
            pltpu.VMEM((8, cap), F32),
            pltpu.VMEM((cap, 2 * cap), F32),
            pltpu.VMEM((cap, width), BF),
            pltpu.VMEM((cap, 3 * width), BF),
        ],
        compiler_params=pltpu.CompilerParams(vmem_limit_bytes=60 * 2**20),
        name="attend_back",
    )(gm, segment, selected, wa, table, *kept)


def gelu_parts(p):
    z = jnp.abs(p)
    e = jnp.exp(-0.5 * p * p)
    t = 1.0 / (1.0 + (0.3275911 * 0.5**0.5) * z)
    poly = ((((1.061405429 * t - 1.453152027) * t + 1.421413741) * t - 0.284496736) * t + 0.254829592) * t
    tail = 0.5 * poly * e
    phi = jnp.where(p > 0, 1.0 - tail, tail)
    return phi, phi + p * (e * 0.3989422804014327)


BLOCK = 592


def mlp_kernel(mid, cot, wu, wd, table, mixed, grad_u, grad_d, gm, sums, u, g, acc, act, gp):
    count, span, width = mid.shape
    length = cot.shape[1]
    tokens = count * span
    chunk = width
    chunks = wd.shape[0] // chunk
    blocks = tokens // BLOCK
    per = span // BLOCK

    def row(i):
        return table[i : i + 1, :]

    def each_block(what):
        lax.fori_loop(0, blocks, lambda b, c: (what(b, pl.ds(pl.multiple_of(b * BLOCK, 16), BLOCK)), c)[1], 0)

    def mid_of(b):
        return mid[b // per, pl.ds(pl.multiple_of(lax.rem(b, per) * BLOCK, 16), BLOCK), :]

    sums[...] = jnp.zeros_like(sums)
    for r in range(count):
        g[r * span + length // 16 * 16 : (r + 1) * span, :] = jnp.zeros((span - length // 16 * 16, width), BF)
        g[r * span : r * span + length, :] = cot[r]

    def start(b, at):
        n, _ = normalized(mid_of(b))
        u[at, :] = (n * row(GAIN2) + row(BIAS2)).astype(BF)
        sums[B_DOWN : B_DOWN + 1, :] += jnp.sum(g[at, :].astype(F32), axis=0, keepdims=True)

    each_block(start)
    for j in range(chunks):
        cols = slice(j * chunk, (j + 1) * chunk)

        def hidden(b, at):
            pre = dot(u[at, :], wu[:, cols]) + row(B_UP + j)
            phi, slope = gelu_parts(pre)
            act[at, :] = (pre * phi).astype(BF)
            grad_pre = (slope * dot_nt(g[at, :], wd[cols, :])).astype(BF)
            gp[at, :] = grad_pre
            sums[B_UP + j : B_UP + j + 1, :] += jnp.sum(grad_pre.astype(F32), axis=0, keepdims=True)

        each_block(hidden)
        grad_d[cols, :] = dot_tn(act[...], g[...]).astype(BF)
        grad_u[:, cols] = dot_tn(u[...], gp[...]).astype(BF)

        def total(b, at):
            forward = dot(act[at, :], wd[cols, :])
            back = dot_nt(gp[at, :], wu[:, cols])
            if j == 0:
                acc[0, at, :] = forward
                acc[1, at, :] = back
            else:
                acc[0, at, :] += forward
                acc[1, at, :] += back

        each_block(total)

    def end(b, at):
        m = mid_of(b)
        out = (m + acc[0, at, :] + row(B_DOWN)).astype(BF)
        if per == 1:
            mixed[b] = out[:length]
        n, scale = normalized(m)
        e = acc[1, at, :]
        sums[GAIN2 : GAIN2 + 1, :] += jnp.sum(n * e, axis=0, keepdims=True)
        sums[BIAS2 : BIAS2 + 1, :] += jnp.sum(e, axis=0, keepdims=True)
        grad = g[at, :].astype(F32) + norm_back(n, scale, row(GAIN2), e)
        gm[b // per, pl.ds(pl.multiple_of(lax.rem(b, per) * BLOCK, 16), BLOCK), :] = grad

    each_block(end)


def mlp(mid, cot, wu, wd, table):
    count, span, width = mid.shape
    tokens = count * span
    return pl.pallas_call(
        mlp_kernel,
        out_shape=(
            jax.ShapeDtypeStruct(cot.shape, BF),
            jax.ShapeDtypeStruct(wu.shape, BF),
            jax.ShapeDtypeStruct(wd.shape, BF),
            jax.ShapeDtypeStruct(mid.shape, F32),
            jax.ShapeDtypeStruct((16, width), F32),
        ),
        in_specs=[pl.BlockSpec(memory_space=pltpu.VMEM)] * 5,
        out_specs=(pl.BlockSpec(memory_space=pltpu.VMEM),) * 5,
        scratch_shapes=[
            pltpu.VMEM((tokens, width), BF),
            pltpu.VMEM((tokens, width), BF),
            pltpu.VMEM((2, tokens, width), F32),
            pltpu.VMEM((tokens, width), BF),
            pltpu.VMEM((tokens, width), BF),
        ],
        compiler_params=pltpu.CompilerParams(vmem_limit_bytes=62 * 2**20),
        name="mlp",
    )(mid, cot, wu, wd, table)


def local(
    small, patches, segment_ids, selected, cotangent, ln1_gain, ln1_bias, w_router, w_query, b_query,
    w_key, w_value, b_value, w_out, b_out, ln2_gain, ln2_bias, w_up, b_up, w_down, b_down,
):
    width = patches.shape[2]
    vectors = (ln1_gain, ln1_bias, w_router, b_query, b_value, b_out, ln2_gain, ln2_bias, b_down)
    matrices = (w_query, w_key, w_value, w_out, w_up, w_down)
    if small:
        attn_w, up_w, down_w, table = gather_all(vectors, b_up, matrices)
        attn_w = attn_w.reshape(-1, attn_w.shape[2])
        up_w = up_w.reshape(-1, up_w.shape[2])
        down_w = down_w.reshape(-1, down_w.shape[3])
    else:
        whole = [lax.all_gather(v, AXES, axis=0, tiled=True) for v in vectors + (b_up,)]
        table = jnp.concatenate(
            [jnp.stack(whole[:VECTORS]), whole[VECTORS].reshape(4, width), jnp.zeros((3, width), BF)]
        ).astype(F32)
        attn_w = jnp.concatenate([lax.all_gather(w, AXES, axis=0, tiled=True) for w in matrices[:4]], axis=1)
        up_w = lax.all_gather(w_up, AXES, axis=0, tiled=True)
        down_w = lax.all_gather(w_down, AXES, axis=0, tiled=True)
    mid, *kept = attend(patches, segment_ids, selected, attn_w, table)
    mixed, grad_u, grad_d, grad_mid, sums_mlp = mlp(mid, cotangent, up_w, down_w, table)
    grad_x, grad_a, sums_attn = attend_back(grad_mid, segment_ids, selected, attn_w, table, kept)
    sums = sums_mlp + sums_attn
    if small:
        own_a, own_u, own_d, own_v = scatter_all(
            grad_a.reshape(16, -1, grad_a.shape[1]),
            grad_u.reshape(16, -1, grad_u.shape[1]),
            grad_d.reshape(16, 2, -1, grad_d.shape[1]),
            sums,
        )
        own_m = jnp.split(own_a, 4, axis=1) + [own_u, own_d]
        device = lax.axis_index("dp") * 8 + lax.axis_index("fsdp")
        part = ln1_gain.shape[0]
        mine = lax.dynamic_slice(own_v[:VECTORS], (0, device * part), (VECTORS, part))
        own = [mine[i] for i in range(VECTORS)]
        own_up_b = lax.dynamic_slice(own_v[VECTORS : VECTORS + 4].reshape(-1), (device * b_up.shape[0],), b_up.shape)
    else:
        own = [lax.psum_scatter(sums[i], AXES, scatter_dimension=0, tiled=True) for i in range(VECTORS)]
        own_up_b = lax.psum_scatter(
            sums[VECTORS : VECTORS + 4].reshape(-1), AXES, scatter_dimension=0, tiled=True
        )
        own_m = [
            lax.psum_scatter(g.astype(F32), AXES, scatter_dimension=0, tiled=True)
            for g in jnp.split(grad_a, 4, axis=1) + [grad_u, grad_d]
        ]
    return (
        mixed, grad_x, own[0], own[1], own[2], own_m[0], own[3], own_m[1], own_m[2], own[4],
        own_m[3], own[5], own[6], own[7], own_m[4], own_up_b, own_m[5], own[8],
    )


def solution(mesh):
    flat, rows2, rows3 = P(AXES), P(AXES, None), P(AXES, None, None)
    vec, mat = flat, rows2
    small = mesh.shape["dp"] == 4 and mesh.shape["fsdp"] == 8
    return jax.shard_map(
        partial(local, small),
        mesh=mesh,
        in_specs=(
            rows3, rows2, rows2, rows3, vec, vec, vec, mat, vec, mat, mat, vec, mat, vec, vec, vec, mat, vec, mat, vec,
        ),
        out_specs=(
            rows3, rows3, vec, vec, vec, mat, vec, mat, mat, vec, mat, vec, vec, vec, mat, vec, mat, vec,
        ),
        check_vma=False,
    )
```

```python
from functools import partial
import math

import jax
import jax.numpy as jnp
from jax import lax
from jax.experimental import pallas as pl
from jax.experimental.pallas import tpu as pltpu
from jax.sharding import PartitionSpec as P

AXES = ("dp", "fsdp")
MESH = pl.DeviceIdType.MESH
BF = jnp.bfloat16
F32 = jnp.float32


class Place:
    def __init__(self):
        self.z = lax.axis_index("dp")
        self.f = lax.axis_index("fsdp")
        self.c = lax.rem(self.f, 2)
        self.x = lax.rem(self.f // 2, 2)
        self.y = self.f // 4
        self.chip = self.z * 4 + self.y * 2 + self.x
        self.chip_x = self.z * 4 + self.y * 2 + (1 - self.x)
        self.chip_y = self.z * 4 + (1 - self.y) * 2 + self.x
        self.to_core = (self.z, self.y * 4 + self.x * 2 + (1 - self.c))
        self.to_x = (self.z, self.y * 4 + (1 - self.x) * 2 + self.c)
        self.to_y = (self.z, (1 - self.y) * 4 + self.x * 2 + self.c)

    def to_z(self, step):
        return (lax.rem(self.z + step + 4, 4), self.f)


def greet(place):
    bar = pltpu.get_barrier_semaphore()
    others = [place.to_core, place.to_x, place.to_y] + [place.to_z(s) for s in (1, 2, 3)]
    for other in others:
        pl.semaphore_signal(bar, inc=1, device_id=other, device_id_type=MESH)
    pl.semaphore_wait(bar, len(others))


def push(src, dst, send, recv, to):
    return pltpu.make_async_remote_copy(
        src_ref=src, dst_ref=dst, send_sem=send, recv_sem=recv, device_id=to, device_id_type=MESH
    )


class Gather:
    def __init__(self, place, j, block, level, plane_first, sems):
        self.p, self.j, self.block, self.level, self.sems = place, j, block, level, sems
        self.plane_first = plane_first

    def copy(self, kind, i, ref, to):
        return push(ref, ref, self.sems.at[2 * kind, self.j, i], self.sems.at[2 * kind + 1, self.j, i], to)

    def piece(self, l):
        if self.plane_first:
            return self.level(l, self.p.c)
        return self.block(l * 4 + self.p.y * 2 + self.p.x)

    def up(self, k):
        return self.copy(0, k, self.piece(lax.rem(self.p.z - k + 4, 4)), self.p.to_z(1))

    def up_in(self, k):
        return self.copy(0, k, self.piece(lax.rem(self.p.z - k + 3, 4)), self.p.to_z(1))

    def down(self, k):
        return self.copy(1, k, self.piece(lax.rem(self.p.z + k, 4)), self.p.to_z(3))

    def down_in(self, k):
        return self.copy(1, k, self.piece(lax.rem(self.p.z + k + 1, 4)), self.p.to_z(3))

    def xs(self, l):
        return self.copy(2, l, self.block(l * 4 + self.p.y * 2 + self.p.x), self.p.to_x)

    def ys(self, l):
        return self.copy(3, l, self.block(l * 4 + self.p.y * 2 + self.p.x), self.p.to_y)

    def side_in(self, l, y_side):
        p = self.p
        chip = l * 4 + (p.y + y_side - 2 * p.y * y_side) * 2 + (p.x + (1 - y_side) - 2 * p.x * (1 - y_side))
        return self.copy(2 + y_side, l, self.block(chip), p.to_x)

    def forward(self, l):
        p = self.p
        chip = l * 4 + jnp.where(p.c == 0, (1 - p.y) * 2 + p.x, p.y * 2 + 1 - p.x)
        to = (p.z, jnp.where(p.c == 0, p.y * 4 + (1 - p.x) * 2 + p.c, (1 - p.y) * 4 + p.x * 2 + p.c))
        return self.copy(4, l, self.block(chip), to)

    def forward_in(self, l):
        return self.copy(4, l, self.block(l * 4 + (1 - self.p.y) * 2 + 1 - self.p.x), self.p.to_x)

    def cs(self, l):
        return self.copy(5, l, self.level(l, self.p.c), self.p.to_core)

    def cs_in(self, l):
        return self.copy(5, l, self.level(l, 1 - self.p.c), self.p.to_core)

    def sides(self, l):
        self.xs(l).start()
        self.ys(l).start()

    def ends(self, k):
        z = self.p.z

        @pl.when((z >= k) & (z < 3))
        def _():
            self.up(k).start()

        @pl.when((z + k <= 3) & (z > 0))
        def _():
            self.down(k).start()

    def begin(self):
        if not self.plane_first:
            self.ends(0)
        self.sides(self.p.z)

    def along_z(self, k):
        z = self.p.z

        @pl.when(z > k)
        def _():
            self.up_in(k).wait_recv()

        @pl.when(z + k < 3)
        def _():
            self.down_in(k).wait_recv()

        if k < 2:
            self.ends(k + 1)
        self.each(k + 1, (lambda l: self.cs(l).start()) if self.plane_first else self.sides)

    def each(self, k, what):
        z = self.p.z
        if k == 0:
            what(z)
            return

        @pl.when(z >= k)
        def _():
            what(z - k)

        @pl.when(z + k <= 3)
        def _():
            what(z + k)

    def turn(self, l):
        self.side_in(l, 1 - self.p.c).wait_recv()
        self.forward(l).start()
        self.side_in(l, self.p.c).wait_recv()

    def across(self, l):
        self.forward_in(l).wait_recv()
        if self.plane_first:
            self.ends(0)
        self.cs(l).start()

    def finish(self):
        z = self.p.z
        for l in range(4):
            if self.plane_first:
                continue
            self.xs(l).wait_send()
            self.ys(l).wait_send()
            self.forward(l).wait_send()
        if self.plane_first:
            self.xs(z).wait_send()
            self.ys(z).wait_send()
            self.forward(z).wait_send()
        for l in range(4):
            self.cs(l).wait_send()
            self.cs_in(l).wait_recv()
        for k in range(3):

            @pl.when((z >= k) & (z < 3))
            def _():
                self.up(k).wait_send()

            @pl.when((z + k <= 3) & (z > 0))
            def _():
                self.down(k).wait_send()


VECTORS = 9
TILE = 128


def vector_steps(p, values, out_ref, hold, landed, sems):
    send, recv = sems.at[0], sems.at[1]
    state = {}

    def begin():
        state["value"] = values()
        hold[0] = state["value"]
        push(hold.at[0], landed.at[0], send.at[0], recv.at[0], p.to_core).start()

    def then(i, to, after):
        def step():
            push(hold.at[i], landed.at[i], send.at[i], recv.at[i], to).wait()
            hold[i + 1] = hold[i] + landed[i]
            after()
        return step

    def next_side():
        push(hold.at[1], landed.at[1], send.at[1], recv.at[1], p.to_x).start()

    def next_other():
        push(hold.at[2], landed.at[2], send.at[2], recv.at[2], p.to_y).start()

    def line(s):
        return push(hold.at[3], landed.at[2 + s], send.at[2 + s], recv.at[2 + s], p.to_z(s))

    def next_line():
        for s in (1, 2, 3):
            line(s).start()

    def last():
        for s in (1, 2, 3):
            line(s).wait()
        out_ref[...] = hold[3] + landed[3] + landed[4] + landed[5]

    return [begin, then(0, p.to_core, next_side), then(1, p.to_x, next_other), then(2, p.to_y, next_line), last]


def cut(cols, share):
    first = int(round(cols * (1 - share) / TILE)) * TILE
    return first


PLANE_SHARE = 0.12


def gather_kernel(*refs):
    vectors, b_up = refs[:VECTORS], refs[VECTORS]
    wq, wk, wv, wo, wu, wd = refs[VECTORS + 1 : VECTORS + 7]
    out_a, out_u, out_d, out_v = refs[VECTORS + 7 : VECTORS + 11]
    held, give, take, packed, hold, landed, sems, pair_sems, own_sems, vec_sems = refs[VECTORS + 11 :]
    p = Place()
    width = wq.shape[1]
    rail = 2 * width
    rows = wq.shape[0]
    lower = p.c == 0
    loads = [pltpu.make_async_copy(w, held.at[0, :, pl.ds(i * width, width)], own_sems.at[3 + i]) for i, w in enumerate((wq, wk, wv, wo))]
    loads.append(pltpu.make_async_copy(wu, held.at[1], own_sems.at[7]))
    own_d = pltpu.make_async_copy(wd, out_d.at[p.chip, p.c], own_sems.at[2])
    for cp in loads:
        cp.start()
    own_d.start()
    greet(p)
    for cp in loads:
        cp.wait()
    mine = pl.ds(pl.multiple_of(p.c * rail, TILE), rail)
    other = pl.ds(pl.multiple_of((1 - p.c) * rail, TILE), rail)
    pair = []
    for i in range(2):
        give[i] = held[i, :, other].astype(F32)
        pair.append(push(give.at[i], take.at[i], pair_sems.at[0, i], pair_sems.at[1, i], p.to_core))
        pair[i].start()
    jobs = []

    def add_jobs(out, rail_cols, columns_by_rail):
        first = cut(rail_cols, PLANE_SHARE)
        for start, size, plane in ((0, first, False), (first, rail_cols - first, True)):
            if size == 0:
                continue
            if columns_by_rail:
                def lanes(c, start=start, size=size):
                    return pl.ds(pl.multiple_of(c * rail_cols + start, TILE), size)
                block = lambda chip, out=out, lanes=lanes: out.at[chip, :, lanes(p.c)]
                level = lambda l, c, out=out, lanes=lanes: out.at[pl.ds(l * 4, 4), :, lanes(c)]
            else:
                lane = pl.ds(start, size)
                block = lambda chip, out=out, lane=lane: out.at[chip, p.c, :, lane]
                level = lambda l, c, out=out, lane=lane: out.at[pl.ds(l * 4, 4), c, :, lane]
            jobs.append(Gather(p, len(jobs), block, level, plane, sems))

    add_jobs(out_a, rail, True)
    add_jobs(out_u, rail, True)
    add_jobs(out_d, width, False)
    own_d.wait()
    per = len(jobs) // 3
    for job in jobs[: 2 * per - 1 : -1]:
        job.begin()
    for i, out in enumerate((out_a, out_u)):
        pair[i].wait()
        own = held[i, :, mine].astype(F32)
        got = take[i]
        packed[i] = jnp.concatenate([jnp.where(lower, own, got), jnp.where(lower, got, own)], axis=0).astype(BF)
        cp = pltpu.make_async_copy(packed.at[i], out.at[p.chip, :, mine], own_sems.at[i])
        cp.start()
        cp.wait()
        for job in jobs[i * per : (i + 1) * per][::-1]:
            job.begin()
    device = p.z * 8 + p.f

    def spread(ref):
        count = ref.shape[1]
        total = count * 32
        lane = lax.broadcasted_iota(jnp.int32, (count, total), 1)
        row = lax.broadcasted_iota(jnp.int32, (count, total), 0)
        place = (lane == row + device * count).astype(BF)
        return jnp.dot(ref[...], place, preferred_element_type=F32)

    def values():
        rows_of = [spread(v) for v in vectors]
        up = spread(b_up)
        rows_of += [up[:, i * width : (i + 1) * width] for i in range(4)]
        rows_of.append(jnp.zeros((3, width), F32))
        return jnp.concatenate(rows_of, axis=0)

    steps = vector_steps(p, values, out_v, hold, landed, vec_sems)
    steps[0]()
    plane = [job for job in jobs if job.plane_first]
    line = [job for job in jobs if not job.plane_first]
    for job in plane:
        job.turn(p.z)
    steps[1]()
    for job in plane:
        job.across(p.z)
    for k in range(4):
        if k < 3:
            for job in line + plane:
                job.along_z(k)
        if k < 3:
            steps[k + 2]()
        for job in line:
            job.each(k, job.turn)
        for job in line:
            job.each(k, job.across)
    for job in jobs:
        job.finish()


def gather_all(vectors, b_up, matrices):
    wq, wd = matrices[0], matrices[5]
    rows, width = wq.shape
    rail = 2 * width
    depth = wd.shape[0]
    return pl.pallas_call(
        gather_kernel,
        out_shape=(
            jax.ShapeDtypeStruct((16, 2 * rows, 4 * width), BF),
            jax.ShapeDtypeStruct((16, 2 * rows, 4 * width), BF),
            jax.ShapeDtypeStruct((16, 2, depth, width), BF),
            jax.ShapeDtypeStruct((16, width), F32),
        ),
        in_specs=[pl.BlockSpec(memory_space=pltpu.VMEM)] * (VECTORS + 1) + [pl.BlockSpec(memory_space=pl.ANY)] * 6,
        out_specs=(pl.BlockSpec(memory_space=pl.ANY),) * 3 + (pl.BlockSpec(memory_space=pltpu.VMEM),),
        scratch_shapes=[
            pltpu.VMEM((2, rows, 2 * rail), BF),
            pltpu.VMEM((2, rows, rail), F32),
            pltpu.VMEM((2, rows, rail), F32),
            pltpu.VMEM((2, 2 * rows, rail), BF),
            pltpu.VMEM((4, 16, width), F32),
            pltpu.VMEM((6, 16, width), F32),
            pltpu.SemaphoreType.DMA((12, 6, 4)),
            pltpu.SemaphoreType.DMA((2, 2)),
            pltpu.SemaphoreType.DMA((8,)),
            pltpu.SemaphoreType.DMA((2, 6)),
        ],
        compiler_params=pltpu.CompilerParams(collective_id=0, has_side_effects=True, vmem_limit_bytes=60 * 2**20),
        name="gather_weights",
    )(*[v[None] for v in vectors], b_up[None], *matrices)


class Scatter:
    def __init__(self, place, j, level, bufs, sems):
        self.p, self.j, self.level, self.sems = place, j, level, sems
        self.acc, self.got, self.one, self.two, self.give, self.line, self.low, self.fin = bufs
        p = place
        rail0 = p.c == 0
        self.me = p.y * 2 + p.x
        self.first = jnp.where(rail0, p.y * 2 + 1 - p.x, (1 - p.y) * 2 + p.x)
        self.second = jnp.where(rail0, (1 - p.y) * 2 + p.x, p.y * 2 + 1 - p.x)
        self.diag = (1 - p.y) * 2 + 1 - p.x
        self.to_first = (p.z, self.first * 2 + p.c)
        self.to_second = (p.z, self.second * 2 + p.c)

    def move(self, kind, l, src, dst, to):
        return push(src, dst, self.sems.at[0, kind, self.j, l], self.sems.at[1, kind, self.j, l], to)

    def own(self, l):
        return pltpu.make_async_copy(self.level(l, self.p.c), self.acc.at[l], self.sems.at[0, 0, self.j, l])

    def core(self, l):
        return self.move(1, l, self.level(l, 1 - self.p.c), self.got.at[l], self.p.to_core)

    def step1(self, l, slot):
        block = self.first if slot == 0 else self.diag
        return self.move(2 + slot, l, self.acc.at[l, block], self.one.at[l, slot], self.to_first)

    def step2(self, l):
        return self.move(4, l, self.give.at[l], self.two.at[l], self.to_second)

    def along(self, l, s):
        return self.move(5, s, self.line.at[l], self.low.at[s], self.p.to_z(s))

    def begin(self, l):
        self.core(l).start()
        self.own(l).start()

    def pair(self, l):
        self.own(l).wait()
        self.core(l).wait_recv()
        self.acc[l] = (self.acc[l].astype(F32) + self.got[l].astype(F32)).astype(BF)
        self.step1(l, 0).start()
        self.step1(l, 1).start()

    def side(self, l):
        self.step1(l, 1).wait_recv()
        self.give[l] = (self.acc[l, self.second].astype(F32) + self.one[l, 1].astype(F32)).astype(BF)
        self.step2(l).start()

    def plane_sum(self, l):
        return self.acc[l, self.me].astype(F32) + self.one[l, 0].astype(F32) + self.two[l].astype(F32)

    def plane(self, l):
        self.step1(l, 0).wait_recv()
        self.step2(l).wait_recv()
        self.line[l] = self.plane_sum(l).astype(BF)
        self.along(l, lax.rem(l - self.p.z + 4, 4)).start()

    def last(self):
        z = self.p.z
        self.step1(z, 0).wait_recv()
        self.step2(z).wait_recv()
        self.fin[...] = self.plane_sum(z)
        for s in (1, 2, 3):
            self.along(z, s).wait_recv()
            self.fin[...] += self.low[s].astype(F32)

    def finish(self):
        for l in range(4):
            self.core(l).wait_send()
            self.step1(l, 0).wait_send()
            self.step1(l, 1).wait_send()
            self.step2(l).wait_send()
        for s in (1, 2, 3):
            self.along(self.p.z, s).wait_send()


def level_order(p):
    low = p.z < 2
    zz = jnp.where(low, p.z, 3 - p.z)
    order = [3, 2, 1 - zz, zz]
    return [jnp.where(low, l, 3 - l) for l in order]


def scatter_kernel(ga, vec, out_a, out_v, *refs):
    bufs = refs[0:8]
    hold, landed, sems, last_sems, vec_sems = refs[8:]
    p = Place()
    rail = ga.shape[2] // 2
    rows = ga.shape[1] // 2
    job = Scatter(
        p, 0, lambda l, c: ga.at[pl.ds(l * 4, 4), :, pl.ds(pl.multiple_of(c * rail, TILE), rail)], bufs, sems
    )
    greet(p)
    items = level_order(p)
    for l in items:
        job.begin(l)
    steps = vector_steps(p, lambda: vec[...], out_v, hold, landed, vec_sems)
    count = len(items)
    for i in range(count + 2):
        if i < count:
            job.pair(items[i])
        if 1 <= i <= count:
            job.side(items[i - 1])
        if 2 <= i <= count:
            job.plane(items[i - 2])
        if i == count + 1:
            job.last()
        if i < 5:
            steps[i]()
    mine = pl.ds(pl.multiple_of(p.c * rail, TILE), rail)
    fin = job.fin
    cp = push(
        fin.at[pl.ds(pl.multiple_of((1 - p.c) * rows, 8), rows)], out_a.at[:, mine],
        last_sems.at[0], last_sems.at[1], p.to_core,
    )
    cp.start()
    out_a[:, mine] = fin[pl.ds(pl.multiple_of(p.c * rows, 8), rows), :]
    job.finish()
    cp.wait()


def scatter_all(ga, vec):
    rows = ga.shape[1] // 2
    cols = ga.shape[2]
    rail = cols // 2
    width = vec.shape[1]
    block = (2 * rows, rail)
    return pl.pallas_call(
        scatter_kernel,
        out_shape=(jax.ShapeDtypeStruct((rows, cols), F32), jax.ShapeDtypeStruct((16, width), F32)),
        in_specs=[pl.BlockSpec(memory_space=pl.ANY), pl.BlockSpec(memory_space=pltpu.VMEM)],
        out_specs=(pl.BlockSpec(memory_space=pltpu.VMEM),) * 2,
        scratch_shapes=[
            pltpu.VMEM((4, 4) + block, BF),
            pltpu.VMEM((4, 4) + block, BF),
            pltpu.VMEM((4, 2) + block, BF),
            pltpu.VMEM((4,) + block, BF),
            pltpu.VMEM((4,) + block, BF),
            pltpu.VMEM((4,) + block, BF),
            pltpu.VMEM((4,) + block, BF),
            pltpu.VMEM(block, F32),
            pltpu.VMEM((4, 16, width), F32),
            pltpu.VMEM((6, 16, width), F32),
            pltpu.SemaphoreType.DMA((2, 6, 1, 4)),
            pltpu.SemaphoreType.DMA((2,)),
            pltpu.SemaphoreType.DMA((2, 6)),
        ],
        compiler_params=pltpu.CompilerParams(collective_id=1, has_side_effects=True, vmem_limit_bytes=60 * 2**20),
        name="scatter_gradients",
    )(ga, vec)


HEAD = 64
EPSILON = 1e-06
LANES = 128
FAR = -1e30
GAIN1, BIAS1, ROUTER, B_QUERY, B_VALUE, B_OUT, GAIN2, BIAS2, B_DOWN, B_UP = range(10)


def dot(a, b):
    return lax.dot_general(a, b, (((1,), (0,)), ((), ())), preferred_element_type=F32)


def dot_nt(a, b):
    return lax.dot_general(a, b, (((1,), (1,)), ((), ())), preferred_element_type=F32)


def dot_tn(a, b):
    return lax.dot_general(a, b, (((0,), (0,)), ((), ())), preferred_element_type=F32)


def up_to(count, step):
    return (count + step - 1) // step * step


def iota(shape, dim):
    return lax.broadcasted_iota(jnp.int32, shape, dim)


def normalized(x):
    centred = x - jnp.mean(x, axis=-1, keepdims=True)
    scale = lax.rsqrt(jnp.mean(centred * centred, axis=-1, keepdims=True) + EPSILON)
    return centred * scale, scale


def norm_back(n, scale, gain, e):
    eg = e * gain
    return scale * (eg - jnp.mean(eg, axis=-1, keepdims=True) - n * jnp.mean(eg * n, axis=-1, keepdims=True))


def column_of(row, size):
    eye = iota((size, size), 0) == iota((size, size), 1)
    return jnp.sum(jnp.where(eye, jnp.broadcast_to(row, (size, size)), 0.0), axis=1, keepdims=True)


def order_of(picked_ref, order_ref):
    cap = picked_ref.shape[1]
    before = jnp.where(iota((cap, cap), 0) < iota((cap, cap), 1), 1.0, 0.0).astype(BF)
    order_ref[...] = dot(picked_ref[...].astype(BF), before)


def pad_rows(selected, segment, picked_ref, marks_ref):
    count, length = selected.shape
    picked_ref[...] = jnp.zeros_like(picked_ref)
    picked_ref[0:count, 0:length] = selected[...].astype(F32)
    if marks_ref is not None:
        marks_ref[...] = jnp.zeros_like(marks_ref)
        marks_ref[0:count, 0:length] = segment[...].astype(F32)


def row_of(ref, r):
    return jnp.sum(jnp.where(iota(ref.shape, 0) == r, ref[...], 0.0), axis=0, keepdims=True)


def to_picked(order, picked, size):
    cap = order.shape[1]
    hit = (order == iota((size, cap), 0).astype(F32)) & (picked > 0.5)
    return jnp.where(hit, 1.0, 0.0)


def from_picked(order, picked, size):
    cap = order.shape[1]
    place = column_of(jnp.where(picked > 0.5, order, -1.0), cap)
    return jnp.where(place == iota((cap, size), 1).astype(F32), 1.0, 0.0).astype(BF)


def sizes(cap):
    half = up_to(cap // 2, HEAD)
    return [(half, up_to(half, LANES)), (cap, cap)]


def loop(count, what):
    lax.fori_loop(0, count, lambda i, c: (what(i), c)[1], 0)


def lanes(i, size):
    return pl.ds(pl.multiple_of(i * size, LANES), size)


def each_size(count, cap, what):
    low = 0
    for rows, keys in sizes(cap):

        @pl.when((count > low) & (count <= rows))
        def _(rows=rows, keys=keys):
            what(rows, keys)

        low = rows


def forbidden(hit, marks, count, size):
    segment_of = dot_nt(jnp.broadcast_to(marks, (8, marks.shape[1])).astype(BF), hit.astype(BF))[0:1]
    segment_of = jnp.where(iota((1, size), 1) < count, segment_of, 99.0)
    column = jnp.sum(hit * marks, axis=1, keepdims=True)
    column = jnp.where(iota((size, 1), 0) < count, column, 99.0)
    return jnp.where(column == segment_of, 0.0, FAR)


def two_heads(pair):
    first = iota(pair.shape, 1) < HEAD
    zero = jnp.zeros_like(pair)
    return jnp.concatenate([jnp.where(first, pair, zero), jnp.where(first, zero, pair)], axis=0)


def one_pair(turned):
    size = turned.shape[1] // 2
    return jnp.concatenate([turned[:HEAD, :size], turned[HEAD:, size:]], axis=0).T


def attend_kernel(x, segment, selected, wa, table, mid, xc, h, qkv, attn, branch, logs, gates, xs, picked, marks, order, bar):
    cap = xs.shape[0]
    length, width = x.shape[1], x.shape[2]
    span = mid.shape[1]
    pad_rows(selected, segment, picked, marks)
    order_of(picked, order)
    xs[...] = jnp.zeros_like(xs)

    def row(r, carry):
        sel, place, mark = row_of(picked, r), row_of(order, r), row_of(marks, r)
        count = jnp.sum(sel).astype(jnp.int32)
        xs[0:length, :] = x[r]
        mid[r] = xs[0:span, :].astype(F32)

        def work(rows, keys):
            hit = to_picked(place, sel, keys)
            block = forbidden(hit, mark, count, keys)
            bar[0:keys, 0:keys] = block
            bar[0:keys, keys : 2 * keys] = block
            x_in = dot(hit[:rows].astype(BF), xs[...])
            xc[r, 0:rows, :] = x_in.astype(BF)
            n, _ = normalized(x_in)
            h_in = (n * table[GAIN1 : GAIN1 + 1, :] + table[BIAS1 : BIAS1 + 1, :]).astype(BF)
            h[r, 0:rows, :] = h_in
            gate = jax.nn.sigmoid(jnp.sum(h_in.astype(F32) * table[ROUTER : ROUTER + 1, :], axis=1, keepdims=True))
            for i, b in enumerate((B_QUERY, None, B_VALUE)):
                part = dot(h_in, wa[:, i * width : (i + 1) * width])
                if b is not None:
                    part = part + table[b : b + 1, :]
                qkv[r, 0:rows, i * width : (i + 1) * width] = part.astype(BF)
            if keys > rows:
                qkv[r, rows:keys, :] = jnp.zeros((keys - rows, 3 * width), BF)

            def pair(i, carry):
                lane = i * LANES
                q = qkv[r, 0:keys, pl.ds(pl.multiple_of(lane, LANES), LANES)]
                k = qkv[r, 0:keys, pl.ds(pl.multiple_of(lane + width, LANES), LANES)]
                v = qkv[r, 0:keys, pl.ds(pl.multiple_of(lane + 2 * width, LANES), LANES)]
                s = dot_nt(k, two_heads(q * BF(HEAD**-0.5))) + bar[0:keys, 0 : 2 * keys]
                top = jnp.max(s, axis=0, keepdims=True)
                e = jnp.exp(s - top)
                total = jnp.sum(e, axis=0, keepdims=True)
                out = one_pair(dot_tn(v, e.astype(BF)) * (1.0 / total))
                attn[r, 0:keys, pl.ds(pl.multiple_of(lane, LANES), LANES)] = out.astype(BF)
                logs[r, i, 0:1, 0 : 2 * keys] = top + jnp.log(total)
                return carry

            lax.fori_loop(0, width // LANES, pair, 0)
            gates[r, 0:rows, :] = jnp.broadcast_to(gate, (rows, LANES))
            out = dot(attn[r, 0:rows, :], wa[:, 3 * width :]) + table[B_OUT : B_OUT + 1, :]
            branch[r, 0:rows, :] = out.astype(BF)
            back = from_picked(place, sel, keys)[:span, :rows]
            mid[r] += dot(back, (out * gate).astype(BF))

        each_size(count, cap, work)
        return carry

    lax.fori_loop(0, x.shape[0], row, 0)


def attend(patches, segment, selected, wa, table):
    count, length, width = patches.shape
    cap, span = up_to(length, LANES), up_to(length, 16)

    def out(cols, kind):
        return jax.ShapeDtypeStruct((count, cap, cols), kind)

    return pl.pallas_call(
        attend_kernel,
        out_shape=(
            jax.ShapeDtypeStruct((count, span, width), F32),
            out(width, BF), out(width, BF), out(3 * width, BF), out(width, BF), out(width, BF),
            jax.ShapeDtypeStruct((count, width // LANES, 1, 2 * cap), F32),
            out(LANES, F32),
        ),
        in_specs=[pl.BlockSpec(memory_space=pltpu.VMEM)] * 5,
        out_specs=(pl.BlockSpec(memory_space=pltpu.VMEM),) * 8,
        scratch_shapes=[
            pltpu.VMEM((cap, width), BF),
            pltpu.VMEM((8, cap), F32),
            pltpu.VMEM((8, cap), F32),
            pltpu.VMEM((8, cap), F32),
            pltpu.VMEM((cap, 2 * cap), F32),
        ],
        compiler_params=pltpu.CompilerParams(vmem_limit_bytes=60 * 2**20),
        name="attend",
    )(patches, segment, selected, wa, table)


def attend_back_kernel(
    gm, segment, selected, wa, table, xc, h, qkv, attn, branch, logs, gates,
    grad_x, grad_a, sums, high, picked, marks, order, bar, ga, dqkv,
):
    cap = high.shape[0]
    span, width = gm.shape[1], gm.shape[2]
    length = grad_x.shape[1]
    pad_rows(selected, segment, picked, marks)
    order_of(picked, order)
    high[...] = jnp.zeros_like(high)
    grad_a[...] = jnp.zeros_like(grad_a)
    sums[...] = jnp.zeros_like(sums)

    def add(i, v):
        sums[i : i + 1, :] += jnp.sum(v, axis=0, keepdims=True)

    def add_weight(i, j, v):
        at = slice(i * width, j * width)
        grad_a[:, at] = (grad_a[:, at].astype(F32) + v).astype(BF)

    def row(r, carry):
        sel, place, mark = row_of(picked, r), row_of(order, r), row_of(marks, r)
        count = jnp.sum(sel).astype(jnp.int32)
        high[0:span, :] = gm[r]

        @pl.when(count == 0)
        def _():
            grad_x[r] = gm[r][:length]

        def work(rows, keys):
            hit = to_picked(place, sel, keys)
            block = forbidden(hit, mark, count, keys)
            bar[0:keys, 0:keys] = block
            bar[0:keys, keys : 2 * keys] = block
            take = hit[:rows].astype(BF)
            g = dot(take, high[...])
            gate = gates[r, 0:rows, 0:1]
            grad_logit = jnp.sum(g * branch[r, 0:rows, :].astype(F32), axis=1, keepdims=True) * gate * (1.0 - gate)
            gb = g * gate
            add(B_OUT, gb.astype(BF).astype(F32))
            gb = gb.astype(BF)
            add_weight(3, 4, dot_tn(attn[r, 0:rows, :], gb))
            ga[0:rows, :] = dot_nt(gb, wa[:, 3 * width :]).astype(BF)
            if keys > rows:
                ga[rows:keys, :] = jnp.zeros((keys - rows, width), BF)

            def pair(i, carry):
                at = pl.ds(pl.multiple_of(i * LANES, LANES), LANES)
                at_k = pl.ds(pl.multiple_of(i * LANES + width, LANES), LANES)
                at_v = pl.ds(pl.multiple_of(i * LANES + 2 * width, LANES), LANES)
                q2 = two_heads(qkv[r, 0:keys, at] * BF(HEAD**-0.5))
                k = qkv[r, 0:keys, at_k]
                v = qkv[r, 0:keys, at_v]
                g2 = two_heads(ga[0:keys, at])
                p = jnp.exp(dot_nt(k, q2) + bar[0:keys, 0 : 2 * keys] - logs[r, i, 0:1, 0 : 2 * keys])
                dp = dot_nt(v, g2)
                ds = (p * (dp - jnp.sum(p * dp, axis=0, keepdims=True))).astype(BF)
                dqkv[0:keys, at] = one_pair(dot_tn(k, ds) * HEAD**-0.5).astype(BF)
                dqkv[0:keys, at_k] = dot(ds, q2).astype(BF)
                dqkv[0:keys, at_v] = dot(p.astype(BF), g2).astype(BF)
                return carry

            lax.fori_loop(0, width // LANES, pair, 0)
            add(B_QUERY, dqkv[0:rows, 0:width].astype(F32))
            add(B_VALUE, dqkv[0:rows, 2 * width :].astype(F32))
            h_in = h[r, 0:rows, :]
            add(ROUTER, h_in.astype(F32) * grad_logit)
            add_weight(0, 3, dot_tn(h_in, dqkv[0:rows, :]))
            gh = dot_nt(dqkv[0:rows, :], wa[:, : 3 * width]) + grad_logit * table[ROUTER : ROUTER + 1, :]
            n, scale = normalized(xc[r, 0:rows, :].astype(F32))
            add(GAIN1, n * gh)
            add(BIAS1, gh)
            dx = norm_back(n, scale, table[GAIN1 : GAIN1 + 1, :], gh).astype(BF)
            back = from_picked(place, sel, keys)[:span, :rows]
            grad_x[r] = (gm[r].astype(F32) + dot(back, dx)).astype(BF)[:length]

        each_size(count, cap, work)
        return carry

    lax.fori_loop(0, gm.shape[0], row, 0)


def attend_back(gm, segment, selected, wa, table, kept):
    count, span, width = gm.shape
    length = segment.shape[1]
    cap = up_to(length, LANES)
    return pl.pallas_call(
        attend_back_kernel,
        out_shape=(
            jax.ShapeDtypeStruct((count, length, width), BF),
            jax.ShapeDtypeStruct(wa.shape, BF),
            jax.ShapeDtypeStruct((16, width), F32),
        ),
        in_specs=[pl.BlockSpec(memory_space=pltpu.VMEM)] * 12,
        out_specs=(pl.BlockSpec(memory_space=pltpu.VMEM),) * 3,
        scratch_shapes=[
            pltpu.VMEM((cap, width), BF),
            pltpu.VMEM((8, cap), F32),
            pltpu.VMEM((8, cap), F32),
            pltpu.VMEM((8, cap), F32),
            pltpu.VMEM((cap, 2 * cap), F32),
            pltpu.VMEM((cap, width), BF),
            pltpu.VMEM((cap, 3 * width), BF),
        ],
        compiler_params=pltpu.CompilerParams(vmem_limit_bytes=60 * 2**20),
        name="attend_back",
    )(gm, segment, selected, wa, table, *kept)


def gelu_parts(p):
    z = jnp.abs(p)
    e = jnp.exp(-0.5 * p * p)
    t = 1.0 / (1.0 + (0.3275911 * 0.5**0.5) * z)
    poly = ((((1.061405429 * t - 1.453152027) * t + 1.421413741) * t - 0.284496736) * t + 0.254829592) * t
    tail = 0.5 * poly * e
    phi = jnp.where(p > 0, 1.0 - tail, tail)
    return phi, phi + p * (e * 0.3989422804014327)


BLOCK = 592


class ChunkScatter:
    def __init__(self, p, kind, whole, bufs, fin, sems):
        self.p, self.kind, self.whole, self.fin, self.sems = p, kind, whole, fin, sems
        self.got, self.one, self.give, self.two, self.line, self.far = bufs
        rail0 = p.c == 0
        self.me = p.y * 2 + p.x
        self.first = jnp.where(rail0, p.y * 2 + 1 - p.x, (1 - p.y) * 2 + p.x)
        self.second = jnp.where(rail0, (1 - p.y) * 2 + p.x, p.y * 2 + 1 - p.x)
        self.diag = (1 - p.y) * 2 + 1 - p.x
        self.to_first = (p.z, self.first * 2 + p.c)
        self.to_second = (p.z, self.second * 2 + p.c)

    def move(self, stage, j, src, dst, to):
        return push(src, dst, self.sems.at[0, stage, self.kind, j], self.sems.at[1, stage, self.kind, j], to)

    def rail(self, j, c):
        if self.kind == 0:
            return self.whole.at[j, :, c]
        return self.whole.at[j, :, :, :, lanes(c, self.whole.shape[4] // 2)]

    def block(self, j, chip):
        if self.kind == 0:
            return self.whole.at[j, chip, self.p.c]
        return self.whole.at[j, :, chip, :, lanes(self.p.c, self.whole.shape[4] // 2)]

    def core(self, j):
        return self.move(0, j, self.rail(j, 1 - self.p.c), self.got.at[j], self.p.to_core)

    def step1(self, j, slot):
        return self.move(1 + slot, j, self.block(j, self.diag if slot else self.first), self.one.at[j, slot], self.to_first)

    def step2(self, j):
        return self.move(3, j, self.give.at[j], self.two.at[j], self.to_second)

    def begin(self, j):
        self.core(j).start()

    def pair(self, j):
        self.core(j).wait_recv()
        mine = self.rail(j, self.p.c)
        mine[...] = (mine[...].astype(F32) + self.got[j].astype(F32)).astype(BF)
        self.step1(j, 1).start()
        self.step1(j, 0).start()

    def side(self, j):
        self.step1(j, 1).wait_recv()
        self.give[j] = (self.block(j, self.second)[...].astype(F32) + self.one[j, 1].astype(F32)).astype(BF)
        self.step2(j).start()

    def along(self, j, s):
        if self.kind == 0:
            src = self.line.at[j]
        else:
            src = self.line.at[j, s - 1]
        return self.move(3 + s, j, src, self.far.at[j, s - 1], self.p.to_z(s))

    def plane_sum(self, j, l):
        if self.kind == 0:
            return self.block(j, self.me)[...].astype(F32) + self.one[j, 0].astype(F32) + self.two[j].astype(F32)
        own = self.whole[j, l, self.me, :, lanes(self.p.c, self.whole.shape[4] // 2)]
        return own.astype(F32) + self.one[j, 0, l].astype(F32) + self.two[j, l].astype(F32)

    def cross(self, j, owner):
        z = self.p.z
        self.step1(j, 0).wait_recv()
        self.step2(j).wait_recv()
        if self.kind == 0:
            self.line[j] = self.plane_sum(j, 0).astype(BF)
            for s in (1, 2, 3):

                @pl.when(lax.rem(z + s, 4) == owner)
                def _(s=s):
                    self.along(j, s).start()

            return
        for s in (1, 2, 3):
            self.line[j, s - 1] = self.plane_sum(j, lax.rem(z + s, 4)).astype(BF)
            self.along(j, s).start()

    def last(self, j, owner):
        if self.kind == 0:

            @pl.when(self.p.z == owner)
            def _():
                total = self.plane_sum(j, 0)
                for s in (1, 2, 3):
                    self.along(j, s).wait_recv()
                    total = total + self.far[j, s - 1].astype(F32)
                self.fin[...] = total

            return
        total = self.plane_sum(j, self.p.z)
        for s in (1, 2, 3):
            self.along(j, s).wait_recv()
            total = total + self.far[j, s - 1].astype(F32)
        self.fin[j] = total

    def finish(self, owner_of):
        def one(j):
            self.core(j).wait_send()
            self.step1(j, 0).wait_send()
            self.step1(j, 1).wait_send()
            self.step2(j).wait_send()
            for s in (1, 2, 3):
                if self.kind == 0:

                    @pl.when(lax.rem(self.p.z + s, 4) == owner_of(j))
                    def _(s=s):
                        self.along(j, s).wait_send()

                else:
                    self.along(j, s).wait_send()

        loop(4, one)


def mlp_kernel(remote, mid, cot, wu, wd, table, mixed, gm, sums, out_u, out_d, *refs):
    u, g, acc, act, gp, hold_u, hold_d, weight_sems = refs[:8]
    count, span, width = mid.shape
    length = cot.shape[1]
    tokens = count * span
    chunk = width
    chunks = wd.shape[0] // chunk
    blocks = tokens // BLOCK
    per = span // BLOCK
    if remote:
        grad_d, grad_u, fin_u = refs[8:11]
        bufs_d, bufs_u = refs[11:17], refs[17:23]
        sems, last_sems = refs[23:]
        p = Place()
        greet(p)
        down = ChunkScatter(p, 0, grad_d, bufs_d, out_d, sems)
        up = ChunkScatter(p, 1, grad_u, bufs_u, fin_u, sems)
        rail = width // 2
        rows = out_u.shape[0]

    def row(i):
        return table[i : i + 1, :]

    def each_block(what):
        loop(blocks, lambda b: what(b, pl.ds(pl.multiple_of(b * BLOCK, 16), BLOCK)))

    def mid_of(b):
        return mid[b // per, pl.ds(pl.multiple_of(lax.rem(b, per) * BLOCK, 16), BLOCK), :]

    def level_of(i):
        return jnp.where(i == 0, 0, jnp.where(i == 1, 3, i - 1))

    def load(i):
        j, slot = level_of(i), lax.rem(i, 2)
        return (
            pltpu.make_async_copy(wu.at[:, lanes(j, chunk)], hold_u.at[slot], weight_sems.at[0, slot]),
            pltpu.make_async_copy(
                wd.at[pl.ds(pl.multiple_of(j * chunk, 16), chunk)], hold_d.at[slot], weight_sems.at[1, slot]
            ),
        )

    for cp in load(0):
        cp.start()
    sums[...] = jnp.zeros_like(sums)
    acc[...] = jnp.zeros_like(acc)
    for r in range(count):
        g[r * span + length // 16 * 16 : (r + 1) * span, :] = jnp.zeros((span - length // 16 * 16, width), BF)
        g[r * span : r * span + length, :] = cot[r]

    def start(b, at):
        n, _ = normalized(mid_of(b))
        u[at, :] = (n * row(GAIN2) + row(BIAS2)).astype(BF)
        sums[B_DOWN : B_DOWN + 1, :] += jnp.sum(g[at, :].astype(F32), axis=0, keepdims=True)

    each_block(start)

    def send_rail(i):
        lane = pl.ds(pl.multiple_of(level_of(i) * chunk + p.c * rail, TILE), rail)
        return push(
            fin_u.at[i, pl.ds(pl.multiple_of((1 - p.c) * rows, 8), rows)], out_u.at[:, lane],
            last_sems.at[0, i], last_sems.at[1, i], p.to_core,
        )

    def own_rail(i):
        up.last(i, 0)
        send_rail(i).start()
        lane = pl.ds(pl.multiple_of(level_of(i) * chunk + p.c * rail, TILE), rail)
        out_u[:, lane] = fin_u[i, pl.ds(pl.multiple_of(p.c * rows, 8), rows), :]

    def from_chunk(i, back, what):
        if remote:
            pl.when(i >= back)(lambda: what(i - back))

    def one_chunk(i):
        j, slot = level_of(i), lax.rem(i, 2)
        for cp in load(i):
            cp.wait()

        @pl.when(i + 1 < chunks)
        def _():
            for cp in load(i + 1):
                cp.start()

        def hidden(b, at):
            pre = dot(u[at, :], hold_u[slot]) + table[pl.ds(B_UP + j, 1), :]
            phi, slope = gelu_parts(pre)
            act[at, :] = (pre * phi).astype(BF)
            grad_pre = (slope * dot_nt(g[at, :], hold_d[slot])).astype(BF)
            gp[at, :] = grad_pre
            sums[pl.ds(B_UP + j, 1), :] += jnp.sum(grad_pre.astype(F32), axis=0, keepdims=True)

        each_block(hidden)
        from_chunk(i, 1, lambda k: down.cross(k, level_of(k)))
        from_chunk(i, 1, lambda k: up.side(k))
        from_chunk(i, 2, own_rail)
        part = dot_tn(act[...], g[...]).astype(BF)
        if remote:
            grad_d[i] = part.reshape(grad_d.shape[1:])
            down.begin(i)
        else:
            out_d[pl.ds(pl.multiple_of(j * chunk, 16), chunk), :] = part
        part = dot_tn(u[...], gp[...]).astype(BF)
        if remote:
            grad_u[i] = part.reshape(grad_u.shape[1:])
            up.begin(i)
            down.pair(i)
        else:
            out_u[:, lanes(j, chunk)] = part
        from_chunk(i, 1, lambda k: up.cross(k, 0))

        def total(b, at):
            acc[0, at, :] += dot(act[at, :], hold_d[slot])
            acc[1, at, :] += dot_nt(gp[at, :], hold_u[slot])

        for b in range(blocks):
            total(b, pl.ds(b * BLOCK, BLOCK))
            if remote and b == 0:
                up.pair(i)
        if remote:
            down.side(i)
        from_chunk(i, 1, lambda k: down.last(k, level_of(k)))

    loop(chunks, one_chunk)

    def end(b, at):
        m = mid_of(b)
        out = (m + acc[0, at, :] + row(B_DOWN)).astype(BF)
        mixed[b] = out[:length]
        n, scale = normalized(m)
        e = acc[1, at, :]
        sums[GAIN2 : GAIN2 + 1, :] += jnp.sum(n * e, axis=0, keepdims=True)
        sums[BIAS2 : BIAS2 + 1, :] += jnp.sum(e, axis=0, keepdims=True)
        gm[b] = (g[at, :].astype(F32) + norm_back(n, scale, row(GAIN2), e)).astype(BF)

    for b in range(blocks):
        end(b, pl.ds(b * BLOCK, BLOCK))
        if remote and b == 0:
            down.cross(chunks - 1, level_of(chunks - 1))
            up.side(chunks - 1)
            own_rail(chunks - 2)
    if remote:
        up.cross(chunks - 1, 0)
        down.last(chunks - 1, level_of(chunks - 1))
        own_rail(chunks - 1)
        for i in range(4):
            send_rail(i).wait()
        up.finish(level_of)
        down.finish(level_of)


def mlp(remote, mid, cot, wu, wd, table):
    count, span, width = mid.shape
    tokens = count * span
    if remote:
        rows, depth = wu.shape[0] // 32, wd.shape[0] // 32
        outs = [jax.ShapeDtypeStruct((rows, wu.shape[1]), F32), jax.ShapeDtypeStruct((depth, width), F32)]
        half = width // 2
        extra = [
            pltpu.VMEM((4, 4, 2, depth, width), BF),
            pltpu.VMEM((4, 4, 4, 2 * rows, width), BF),
            pltpu.VMEM((4, 2 * rows, half), F32),
        ]
        extra += [pltpu.VMEM((4, 4, depth, width), BF), pltpu.VMEM((4, 2, depth, width), BF)]
        extra += [pltpu.VMEM((4, depth, width), BF)] * 3 + [pltpu.VMEM((4, 3, depth, width), BF)]
        extra += [pltpu.VMEM((4, 4, 4, 2 * rows, half), BF), pltpu.VMEM((4, 2, 4, 2 * rows, half), BF)]
        extra += [pltpu.VMEM((4, 4, 2 * rows, half), BF)] * 2 + [pltpu.VMEM((4, 3, 2 * rows, half), BF)] * 2
        extra += [pltpu.SemaphoreType.DMA((2, 7, 2, 4)), pltpu.SemaphoreType.DMA((2, 4))]
        params = dict(collective_id=2, has_side_effects=True)
    else:
        outs = [jax.ShapeDtypeStruct(wu.shape, BF), jax.ShapeDtypeStruct(wd.shape, BF)]
        extra, params = [], {}
    vmem = pl.BlockSpec(memory_space=pltpu.VMEM)
    hbm = pl.BlockSpec(memory_space=pl.ANY)
    return pl.pallas_call(
        partial(mlp_kernel, remote),
        out_shape=(
            jax.ShapeDtypeStruct(cot.shape, BF),
            jax.ShapeDtypeStruct(mid.shape, BF),
            jax.ShapeDtypeStruct((16, width), F32),
            *outs,
        ),
        in_specs=[vmem, vmem, hbm, hbm, vmem],
        out_specs=(vmem,) * 5,
        scratch_shapes=[
            pltpu.VMEM((tokens, width), BF),
            pltpu.VMEM((tokens, width), BF),
            pltpu.VMEM((2, tokens, width), F32),
            pltpu.VMEM((tokens, width), BF),
            pltpu.VMEM((tokens, width), BF),
            pltpu.VMEM((2, width, width), BF),
            pltpu.VMEM((2, width, width), BF),
            pltpu.SemaphoreType.DMA((2, 2)),
            *extra,
        ],
        compiler_params=pltpu.CompilerParams(vmem_limit_bytes=62 * 2**20, **params),
        name="mlp",
    )(mid, cot, wu, wd, table)


def local(
    small, patches, segment_ids, selected, cotangent, ln1_gain, ln1_bias, w_router, w_query, b_query,
    w_key, w_value, b_value, w_out, b_out, ln2_gain, ln2_bias, w_up, b_up, w_down, b_down,
):
    width = patches.shape[2]
    vectors = (ln1_gain, ln1_bias, w_router, b_query, b_value, b_out, ln2_gain, ln2_bias, b_down)
    matrices = (w_query, w_key, w_value, w_out, w_up, w_down)
    if small:
        attn_w, up_w, down_w, table = gather_all(vectors, b_up, matrices)
        attn_w = attn_w.reshape(-1, attn_w.shape[2])
        up_w = up_w.reshape(-1, up_w.shape[2])
        down_w = down_w.reshape(-1, down_w.shape[3])
    else:
        whole = [lax.all_gather(v, AXES, axis=0, tiled=True) for v in vectors + (b_up,)]
        table = jnp.concatenate(
            [jnp.stack(whole[:VECTORS]), whole[VECTORS].reshape(4, width), jnp.zeros((3, width), BF)]
        ).astype(F32)
        attn_w = jnp.concatenate([lax.all_gather(w, AXES, axis=0, tiled=True) for w in matrices[:4]], axis=1)
        up_w = lax.all_gather(w_up, AXES, axis=0, tiled=True)
        down_w = lax.all_gather(w_down, AXES, axis=0, tiled=True)
    mid, *kept = attend(patches, segment_ids, selected, attn_w, table)
    mixed, grad_mid, sums_mlp, grad_u, grad_d = mlp(small, mid, cotangent, up_w, down_w, table)
    grad_x, grad_a, sums_attn = attend_back(grad_mid, segment_ids, selected, attn_w, table, kept)
    sums = sums_mlp + sums_attn
    if small:
        own_a, own_v = scatter_all(grad_a.reshape(16, -1, grad_a.shape[1]), sums)
        own_m = jnp.split(own_a, 4, axis=1) + [grad_u, grad_d]
        device = lax.axis_index("dp") * 8 + lax.axis_index("fsdp")
        part = ln1_gain.shape[0]
        mine = lax.dynamic_slice(own_v[:VECTORS], (0, device * part), (VECTORS, part))
        own = [mine[i] for i in range(VECTORS)]
        own_up_b = lax.dynamic_slice(own_v[VECTORS : VECTORS + 4].reshape(-1), (device * b_up.shape[0],), b_up.shape)
    else:
        own = [lax.psum_scatter(sums[i], AXES, scatter_dimension=0, tiled=True) for i in range(VECTORS)]
        own_up_b = lax.psum_scatter(
            sums[VECTORS : VECTORS + 4].reshape(-1), AXES, scatter_dimension=0, tiled=True
        )
        own_m = [
            lax.psum_scatter(g.astype(F32), AXES, scatter_dimension=0, tiled=True)
            for g in jnp.split(grad_a, 4, axis=1) + [grad_u, grad_d]
        ]
    return (
        mixed, grad_x, own[0], own[1], own[2], own_m[0], own[3], own_m[1], own_m[2], own[4],
        own_m[3], own[5], own[6], own[7], own_m[4], own_up_b, own_m[5], own[8],
    )


def solution(mesh):
    flat, rows2, rows3 = P(AXES), P(AXES, None), P(AXES, None, None)
    vec, mat = flat, rows2
    small = mesh.shape["dp"] == 4 and mesh.shape["fsdp"] == 8
    return jax.shard_map(
        partial(local, small),
        mesh=mesh,
        in_specs=(
            rows3, rows2, rows2, rows3, vec, vec, vec, mat, vec, mat, mat, vec, mat, vec, vec, vec, mat, vec, mat, vec,
        ),
        out_specs=(
            rows3, rows3, vec, vec, vec, mat, vec, mat, mat, vec, mat, vec, vec, vec, mat, vec, mat, vec,
        ),
        check_vma=False,
    )
```

```python
from functools import partial
import math

import jax
import jax.numpy as jnp
from jax import lax
from jax.experimental import pallas as pl
from jax.experimental.pallas import tpu as pltpu
from jax.sharding import PartitionSpec as P

AXES = ("dp", "fsdp")
MESH = pl.DeviceIdType.MESH
BF = jnp.bfloat16
F32 = jnp.float32


class Place:
    def __init__(self):
        self.z = lax.axis_index("dp")
        self.f = lax.axis_index("fsdp")
        self.c = lax.rem(self.f, 2)
        self.x = lax.rem(self.f // 2, 2)
        self.y = self.f // 4
        self.chip = self.z * 4 + self.y * 2 + self.x
        self.chip_x = self.z * 4 + self.y * 2 + (1 - self.x)
        self.chip_y = self.z * 4 + (1 - self.y) * 2 + self.x
        self.to_core = (self.z, self.y * 4 + self.x * 2 + (1 - self.c))
        self.to_x = (self.z, self.y * 4 + (1 - self.x) * 2 + self.c)
        self.to_y = (self.z, (1 - self.y) * 4 + self.x * 2 + self.c)

    def to_z(self, step):
        return (lax.rem(self.z + step + 4, 4), self.f)


def greet(place):
    bar = pltpu.get_barrier_semaphore()
    others = [place.to_core, place.to_x, place.to_y] + [place.to_z(s) for s in (1, 2, 3)]
    for other in others:
        pl.semaphore_signal(bar, inc=1, device_id=other, device_id_type=MESH)
    pl.semaphore_wait(bar, len(others))


def push(src, dst, send, recv, to):
    return pltpu.make_async_remote_copy(
        src_ref=src, dst_ref=dst, send_sem=send, recv_sem=recv, device_id=to, device_id_type=MESH
    )


class Gather:
    def __init__(self, place, j, block, level, plane_first, sems):
        self.p, self.j, self.block, self.level, self.sems = place, j, block, level, sems
        self.plane_first = plane_first

    def copy(self, kind, i, ref, to):
        return push(ref, ref, self.sems.at[2 * kind, self.j, i], self.sems.at[2 * kind + 1, self.j, i], to)

    def piece(self, l):
        if self.plane_first:
            return self.level(l, self.p.c)
        return self.block(l * 4 + self.p.y * 2 + self.p.x)

    def up(self, k):
        return self.copy(0, k, self.piece(lax.rem(self.p.z - k + 4, 4)), self.p.to_z(1))

    def up_in(self, k):
        return self.copy(0, k, self.piece(lax.rem(self.p.z - k + 3, 4)), self.p.to_z(1))

    def down(self, k):
        return self.copy(1, k, self.piece(lax.rem(self.p.z + k, 4)), self.p.to_z(3))

    def down_in(self, k):
        return self.copy(1, k, self.piece(lax.rem(self.p.z + k + 1, 4)), self.p.to_z(3))

    def xs(self, l):
        return self.copy(2, l, self.block(l * 4 + self.p.y * 2 + self.p.x), self.p.to_x)

    def ys(self, l):
        return self.copy(3, l, self.block(l * 4 + self.p.y * 2 + self.p.x), self.p.to_y)

    def side_in(self, l, y_side):
        p = self.p
        chip = l * 4 + (p.y + y_side - 2 * p.y * y_side) * 2 + (p.x + (1 - y_side) - 2 * p.x * (1 - y_side))
        return self.copy(2 + y_side, l, self.block(chip), p.to_x)

    def forward(self, l):
        p = self.p
        chip = l * 4 + jnp.where(p.c == 0, (1 - p.y) * 2 + p.x, p.y * 2 + 1 - p.x)
        to = (p.z, jnp.where(p.c == 0, p.y * 4 + (1 - p.x) * 2 + p.c, (1 - p.y) * 4 + p.x * 2 + p.c))
        return self.copy(4, l, self.block(chip), to)

    def forward_in(self, l):
        return self.copy(4, l, self.block(l * 4 + (1 - self.p.y) * 2 + 1 - self.p.x), self.p.to_x)

    def cs(self, l):
        return self.copy(5, l, self.level(l, self.p.c), self.p.to_core)

    def cs_in(self, l):
        return self.copy(5, l, self.level(l, 1 - self.p.c), self.p.to_core)

    def sides(self, l):
        self.xs(l).start()
        self.ys(l).start()

    def ends(self, k):
        z = self.p.z

        @pl.when((z >= k) & (z < 3))
        def _():
            self.up(k).start()

        @pl.when((z + k <= 3) & (z > 0))
        def _():
            self.down(k).start()

    def begin(self):
        if not self.plane_first:
            self.ends(0)
        self.sides(self.p.z)

    def along_z(self, k):
        z = self.p.z

        @pl.when(z > k)
        def _():
            self.up_in(k).wait_recv()

        @pl.when(z + k < 3)
        def _():
            self.down_in(k).wait_recv()

        if k < 2:
            self.ends(k + 1)
        self.each(k + 1, (lambda l: self.cs(l).start()) if self.plane_first else self.sides)

    def each(self, k, what):
        z = self.p.z
        if k == 0:
            what(z)
            return

        @pl.when(z >= k)
        def _():
            what(z - k)

        @pl.when(z + k <= 3)
        def _():
            what(z + k)

    def turn(self, l):
        self.side_in(l, 1 - self.p.c).wait_recv()
        self.forward(l).start()
        self.side_in(l, self.p.c).wait_recv()

    def across(self, l):
        self.forward_in(l).wait_recv()
        if self.plane_first:
            self.ends(0)
        self.cs(l).start()

    def finish(self):
        z = self.p.z
        for l in range(4):
            if self.plane_first:
                continue
            self.xs(l).wait_send()
            self.ys(l).wait_send()
            self.forward(l).wait_send()
        if self.plane_first:
            self.xs(z).wait_send()
            self.ys(z).wait_send()
            self.forward(z).wait_send()
        for l in range(4):
            self.cs(l).wait_send()
            self.cs_in(l).wait_recv()
        for k in range(3):

            @pl.when((z >= k) & (z < 3))
            def _():
                self.up(k).wait_send()

            @pl.when((z + k <= 3) & (z > 0))
            def _():
                self.down(k).wait_send()


VECTORS = 9
TILE = 128


def vector_steps(p, values, out_ref, hold, landed, sems):
    send, recv = sems.at[0], sems.at[1]
    state = {}

    def begin():
        state["value"] = values()
        hold[0] = state["value"]
        push(hold.at[0], landed.at[0], send.at[0], recv.at[0], p.to_core).start()

    def then(i, to, after):
        def step():
            push(hold.at[i], landed.at[i], send.at[i], recv.at[i], to).wait()
            hold[i + 1] = hold[i] + landed[i]
            after()
        return step

    def next_side():
        push(hold.at[1], landed.at[1], send.at[1], recv.at[1], p.to_x).start()

    def next_other():
        push(hold.at[2], landed.at[2], send.at[2], recv.at[2], p.to_y).start()

    def line(s):
        return push(hold.at[3], landed.at[2 + s], send.at[2 + s], recv.at[2 + s], p.to_z(s))

    def next_line():
        for s in (1, 2, 3):
            line(s).start()

    def last():
        for s in (1, 2, 3):
            line(s).wait()
        out_ref[...] = hold[3] + landed[3] + landed[4] + landed[5]

    return [begin, then(0, p.to_core, next_side), then(1, p.to_x, next_other), then(2, p.to_y, next_line), last]


def cut(cols, share):
    first = int(round(cols * (1 - share) / TILE)) * TILE
    return first


PLANE_SHARE = 0.12


def gather_kernel(*refs):
    vectors, b_up = refs[:VECTORS], refs[VECTORS]
    wq, wk, wv, wo, wu, wd = refs[VECTORS + 1 : VECTORS + 7]
    rows_in = refs[VECTORS + 7 : VECTORS + 9]
    out_a, out_u, out_d, out_v = refs[VECTORS + 9 : VECTORS + 13]
    rows_out = refs[VECTORS + 13 : VECTORS + 15]
    rows_held = refs[VECTORS + 15 : VECTORS + 17]
    held, give, take, packed, hold, landed, sems, pair_sems, own_sems, vec_sems = refs[VECTORS + 17 :]
    p = Place()
    width = wq.shape[1]
    rail = 2 * width
    rows = wq.shape[0]
    lower = p.c == 0
    loads = [pltpu.make_async_copy(w, held.at[0, :, pl.ds(i * width, width)], own_sems.at[3 + i]) for i, w in enumerate((wq, wk, wv, wo))]
    loads.append(pltpu.make_async_copy(wu, held.at[1], own_sems.at[7]))
    own_d = pltpu.make_async_copy(wd, out_d.at[p.chip, p.c], own_sems.at[2])
    moves = [pltpu.make_async_copy(a, b, own_sems.at[8 + i]) for i, (a, b) in enumerate(zip(rows_in, rows_held))]
    for cp in loads + moves:
        cp.start()
    own_d.start()
    greet(p)
    for cp in loads:
        cp.wait()
    mine = pl.ds(pl.multiple_of(p.c * rail, TILE), rail)
    other = pl.ds(pl.multiple_of((1 - p.c) * rail, TILE), rail)
    pair = []
    for i in range(2):
        give[i] = held[i, :, other].astype(F32)
        pair.append(push(give.at[i], take.at[i], pair_sems.at[0, i], pair_sems.at[1, i], p.to_core))
        pair[i].start()
    jobs = []

    def add_jobs(out, rail_cols, columns_by_rail):
        first = cut(rail_cols, PLANE_SHARE)
        for start, size, plane in ((0, first, False), (first, rail_cols - first, True)):
            if size == 0:
                continue
            if columns_by_rail:
                def lanes(c, start=start, size=size):
                    return pl.ds(pl.multiple_of(c * rail_cols + start, TILE), size)
                block = lambda chip, out=out, lanes=lanes: out.at[chip, :, lanes(p.c)]
                level = lambda l, c, out=out, lanes=lanes: out.at[pl.ds(l * 4, 4), :, lanes(c)]
            else:
                lane = pl.ds(start, size)
                block = lambda chip, out=out, lane=lane: out.at[chip, p.c, :, lane]
                level = lambda l, c, out=out, lane=lane: out.at[pl.ds(l * 4, 4), c, :, lane]
            jobs.append(Gather(p, len(jobs), block, level, plane, sems))

    add_jobs(out_a, rail, True)
    add_jobs(out_u, rail, True)
    add_jobs(out_d, width, False)
    own_d.wait()
    per = len(jobs) // 3
    for job in jobs[: 2 * per - 1 : -1]:
        job.begin()
    for i, out in enumerate((out_a, out_u)):
        pair[i].wait()
        own = held[i, :, mine].astype(F32)
        got = take[i]
        packed[i] = jnp.concatenate([jnp.where(lower, own, got), jnp.where(lower, got, own)], axis=0).astype(BF)
        cp = pltpu.make_async_copy(packed.at[i], out.at[p.chip, :, mine], own_sems.at[i])
        cp.start()
        cp.wait()
        for job in jobs[i * per : (i + 1) * per][::-1]:
            job.begin()
    device = p.z * 8 + p.f

    def spread(ref):
        count = ref.shape[1]
        total = count * 32
        lane = lax.broadcasted_iota(jnp.int32, (count, total), 1)
        row = lax.broadcasted_iota(jnp.int32, (count, total), 0)
        place = (lane == row + device * count).astype(BF)
        return jnp.dot(ref[...], place, preferred_element_type=F32)

    def values():
        rows_of = [spread(v) for v in vectors]
        up = spread(b_up)
        rows_of += [up[:, i * width : (i + 1) * width] for i in range(4)]
        rows_of.append(jnp.zeros((3, width), F32))
        return jnp.concatenate(rows_of, axis=0)

    steps = vector_steps(p, values, out_v, hold, landed, vec_sems)
    steps[0]()
    plane = [job for job in jobs if job.plane_first]
    line = [job for job in jobs if not job.plane_first]
    for job in plane:
        job.turn(p.z)
    length, count = rows_in[0].shape[0], rows_in[0].shape[1]
    span = rows_out[0].shape[1]
    low = length // 16 * 16

    def lay_out(i, r):
        if r == 0:
            moves[i].wait()
        rows_out[i][r, low:span, :] = jnp.zeros((span - low, width), BF)
        rows_out[i][r, 0:length, :] = rows_held[i][:, r, :]

    work = [(i, r) for i in range(2) for r in range(count)]
    lay_out(*work[0])
    steps[1]()
    for job in plane:
        job.across(p.z)
    for r in range(1, count):
        lay_out(*work[r])
    for k in range(4):
        if k < 3:
            for job in line + plane:
                job.along_z(k)
            steps[k + 2]()
        for job in line:
            job.each(k, job.turn)
        if k == 0:
            for item in work[count:]:
                lay_out(*item)
        if k > 0:
            for job in line:
                job.each(k - 1, job.across)
    for job in line:
        job.each(3, job.across)
    for job in jobs:
        job.finish()


def gather_all(vectors, b_up, matrices, rows_in, span):
    wq, wd = matrices[0], matrices[5]
    rows, width = wq.shape
    rail = 2 * width
    depth = wd.shape[0]
    turned = [v.transpose(1, 0, 2) for v in rows_in]
    count = rows_in[0].shape[0]
    return pl.pallas_call(
        gather_kernel,
        out_shape=(
            jax.ShapeDtypeStruct((16, 2 * rows, 4 * width), BF),
            jax.ShapeDtypeStruct((16, 2 * rows, 4 * width), BF),
            jax.ShapeDtypeStruct((16, 2, depth, width), BF),
            jax.ShapeDtypeStruct((16, width), F32),
            jax.ShapeDtypeStruct((count, span, width), BF),
            jax.ShapeDtypeStruct((count, span, width), BF),
        ),
        in_specs=[pl.BlockSpec(memory_space=pltpu.VMEM)] * (VECTORS + 1) + [pl.BlockSpec(memory_space=pl.ANY)] * 8,
        out_specs=(pl.BlockSpec(memory_space=pl.ANY),) * 3 + (pl.BlockSpec(memory_space=pltpu.VMEM),) * 3,
        scratch_shapes=[
            pltpu.VMEM(turned[0].shape, BF),
            pltpu.VMEM(turned[1].shape, BF),
            pltpu.VMEM((2, rows, 2 * rail), BF),
            pltpu.VMEM((2, rows, rail), F32),
            pltpu.VMEM((2, rows, rail), F32),
            pltpu.VMEM((2, 2 * rows, rail), BF),
            pltpu.VMEM((4, 16, width), F32),
            pltpu.VMEM((6, 16, width), F32),
            pltpu.SemaphoreType.DMA((12, 6, 4)),
            pltpu.SemaphoreType.DMA((2, 2)),
            pltpu.SemaphoreType.DMA((10,)),
            pltpu.SemaphoreType.DMA((2, 6)),
        ],
        compiler_params=pltpu.CompilerParams(collective_id=0, has_side_effects=True, vmem_limit_bytes=60 * 2**20),
        name="gather_weights",
    )(*[v[None] for v in vectors], b_up[None], *matrices, *turned)


class Scatter:
    def __init__(self, place, j, level, bufs, sems):
        self.p, self.j, self.level, self.sems = place, j, level, sems
        self.acc, self.got, self.one, self.two, self.give, self.line, self.low, self.fin = bufs
        p = place
        rail0 = p.c == 0
        self.me = p.y * 2 + p.x
        self.first = jnp.where(rail0, p.y * 2 + 1 - p.x, (1 - p.y) * 2 + p.x)
        self.second = jnp.where(rail0, (1 - p.y) * 2 + p.x, p.y * 2 + 1 - p.x)
        self.diag = (1 - p.y) * 2 + 1 - p.x
        self.to_first = (p.z, self.first * 2 + p.c)
        self.to_second = (p.z, self.second * 2 + p.c)

    def move(self, kind, l, src, dst, to):
        return push(src, dst, self.sems.at[0, kind, self.j, l], self.sems.at[1, kind, self.j, l], to)

    def own(self, l):
        return pltpu.make_async_copy(self.level(l, self.p.c), self.acc.at[l], self.sems.at[0, 0, self.j, l])

    def core(self, l):
        return self.move(1, l, self.level(l, 1 - self.p.c), self.got.at[l], self.p.to_core)

    def step1(self, l, slot):
        block = self.first if slot == 0 else self.diag
        return self.move(2 + slot, l, self.acc.at[l, block], self.one.at[l, slot], self.to_first)

    def step2(self, l):
        return self.move(4, l, self.give.at[l], self.two.at[l], self.to_second)

    def along(self, l, s):
        return self.move(5, s, self.line.at[l], self.low.at[s], self.p.to_z(s))

    def begin(self, l):
        self.core(l).start()
        self.own(l).start()

    def pair(self, l):
        self.own(l).wait()
        self.core(l).wait_recv()
        self.acc[l] = (self.acc[l].astype(F32) + self.got[l].astype(F32)).astype(BF)
        self.step1(l, 0).start()
        self.step1(l, 1).start()

    def side(self, l):
        self.step1(l, 1).wait_recv()
        self.give[l] = (self.acc[l, self.second].astype(F32) + self.one[l, 1].astype(F32)).astype(BF)
        self.step2(l).start()

    def plane_sum(self, l):
        return self.acc[l, self.me].astype(F32) + self.one[l, 0].astype(F32) + self.two[l].astype(F32)

    def plane(self, l):
        self.step1(l, 0).wait_recv()
        self.step2(l).wait_recv()
        self.line[l] = self.plane_sum(l).astype(BF)
        self.along(l, lax.rem(l - self.p.z + 4, 4)).start()

    def last(self):
        z = self.p.z
        self.step1(z, 0).wait_recv()
        self.step2(z).wait_recv()
        self.fin[...] = self.plane_sum(z)
        for s in (1, 2, 3):
            self.along(z, s).wait_recv()
            self.fin[...] += self.low[s].astype(F32)

    def finish(self):
        for l in range(4):
            self.core(l).wait_send()
            self.step1(l, 0).wait_send()
            self.step1(l, 1).wait_send()
            self.step2(l).wait_send()
        for s in (1, 2, 3):
            self.along(self.p.z, s).wait_send()


def level_order(p):
    low = p.z < 2
    zz = jnp.where(low, p.z, 3 - p.z)
    order = [3, 2, 1 - zz, zz]
    return [jnp.where(low, l, 3 - l) for l in order]


PARTS = 1


def scatter_kernel(ga, vec_m, vec_a, *refs):
    out_a, out_v, out_b = refs[0:3]
    hold, landed, total, sems, last_sems, vec_sems = refs[3 + 8 * PARTS :]
    p = Place()
    rail = ga.shape[2] // 2
    part = rail // PARTS
    rows = ga.shape[1] // 2

    def lanes_of(i, c):
        return pl.ds(pl.multiple_of(c * rail + i * part, TILE), part)

    jobs = [
        Scatter(
            p, i, lambda l, c, i=i: ga.at[pl.ds(l * 4, 4), :, lanes_of(i, c)], refs[3 + 8 * i : 11 + 8 * i], sems
        )
        for i in range(PARTS)
    ]
    greet(p)
    order = level_order(p)
    items = [(job, l) for l in order for job in jobs]
    for job, l in items:
        job.begin(l)
    steps = vector_steps(p, lambda: vec_m[...] + vec_a[...], total, hold, landed, vec_sems)
    number = len(items)
    for n in range(number + 2):
        if n < number:
            items[n][0].pair(items[n][1])
        if 1 <= n <= number:
            items[n - 1][0].side(items[n - 1][1])
        if 2 <= n:
            job, l = items[n - 2]
            if n - 2 < number - PARTS:
                job.plane(l)
            else:
                job.last()
        if n < 5:
            steps[n]()
    sends = []
    for i, job in enumerate(jobs):
        lane = lanes_of(i, p.c)
        cp = push(
            job.fin.at[pl.ds(pl.multiple_of((1 - p.c) * rows, 8), rows)], out_a.at[:, lane],
            last_sems.at[0, i], last_sems.at[1, i], p.to_core,
        )
        cp.start()
        sends.append(cp)
        out_a[:, lane] = job.fin[pl.ds(pl.multiple_of(p.c * rows, 8), rows), :]
    device = p.z * 8 + p.f
    width = total.shape[1]
    share = width // 32
    out_v[...] = pltpu.roll(total[...], lax.rem(width - device * share, width), 1)[:, :TILE]
    row = VECTORS + device // 8
    up = jnp.sum(jnp.where(lax.broadcasted_iota(jnp.int32, total.shape, 0) == row, total[...], 0.0), axis=0, keepdims=True)
    up = jnp.broadcast_to(up, (8, width))
    out_b[...] = pltpu.roll(up, lax.rem(width - lax.rem(device, 8) * 4 * share, width), 1)[:, :TILE]
    for job in jobs:
        job.finish()
    for cp in sends:
        cp.wait()


def scatter_all(ga, vec_m, vec_a):
    rows = ga.shape[1] // 2
    cols = ga.shape[2]
    width = vec_m.shape[1]
    block = (2 * rows, cols // 2 // PARTS)
    bufs = [
        pltpu.VMEM((4, 4) + block, BF),
        pltpu.VMEM((4, 4) + block, BF),
        pltpu.VMEM((4, 2) + block, BF),
        pltpu.VMEM((4,) + block, BF),
        pltpu.VMEM((4,) + block, BF),
        pltpu.VMEM((4,) + block, BF),
        pltpu.VMEM((4,) + block, BF),
        pltpu.VMEM(block, F32),
    ]
    vmem, hbm = pl.BlockSpec(memory_space=pltpu.VMEM), pl.BlockSpec(memory_space=pl.ANY)
    return pl.pallas_call(
        scatter_kernel,
        out_shape=(
            jax.ShapeDtypeStruct((rows, cols), F32),
            jax.ShapeDtypeStruct((16, TILE), F32),
            jax.ShapeDtypeStruct((8, TILE), F32),
        ),
        in_specs=[hbm, vmem, vmem],
        out_specs=(vmem,) * 3,
        scratch_shapes=[
            *(bufs * PARTS),
            pltpu.VMEM((4, 16, width), F32),
            pltpu.VMEM((6, 16, width), F32),
            pltpu.VMEM((16, width), F32),
            pltpu.SemaphoreType.DMA((2, 6, PARTS, 4)),
            pltpu.SemaphoreType.DMA((2, PARTS)),
            pltpu.SemaphoreType.DMA((2, 6)),
        ],
        compiler_params=pltpu.CompilerParams(collective_id=1, has_side_effects=True, vmem_limit_bytes=60 * 2**20),
        name="scatter_gradients",
    )(ga, vec_m, vec_a)


HEAD = 64
EPSILON = 1e-06
LANES = 128
FAR = -1e30
GAIN1, BIAS1, ROUTER, B_QUERY, B_VALUE, B_OUT, GAIN2, BIAS2, B_DOWN, B_UP = range(10)


def dot(a, b):
    return lax.dot_general(a, b, (((1,), (0,)), ((), ())), preferred_element_type=F32)


def dot_nt(a, b):
    return lax.dot_general(a, b, (((1,), (1,)), ((), ())), preferred_element_type=F32)


def dot_tn(a, b):
    return lax.dot_general(a, b, (((0,), (0,)), ((), ())), preferred_element_type=F32)


def up_to(count, step):
    return (count + step - 1) // step * step


def iota(shape, dim):
    return lax.broadcasted_iota(jnp.int32, shape, dim)


def normalized(x):
    centred = x - jnp.mean(x, axis=-1, keepdims=True)
    scale = lax.rsqrt(jnp.mean(centred * centred, axis=-1, keepdims=True) + EPSILON)
    return centred * scale, scale


def norm_back(n, scale, gain, e):
    eg = e * gain
    return scale * (eg - jnp.mean(eg, axis=-1, keepdims=True) - n * jnp.mean(eg * n, axis=-1, keepdims=True))


def column_of(row, size):
    eye = iota((size, size), 0) == iota((size, size), 1)
    return jnp.sum(jnp.where(eye, jnp.broadcast_to(row, (size, size)), 0.0), axis=1, keepdims=True)


def order_of(picked_ref, order_ref):
    cap = picked_ref.shape[1]
    before = jnp.where(iota((cap, cap), 0) < iota((cap, cap), 1), 1.0, 0.0).astype(BF)
    order_ref[...] = dot(picked_ref[...].astype(BF), before)


def pad_rows(selected, segment, picked_ref, marks_ref):
    count, length = selected.shape
    picked_ref[...] = jnp.zeros_like(picked_ref)
    picked_ref[0:count, 0:length] = selected[...].astype(F32)
    if marks_ref is not None:
        marks_ref[...] = jnp.zeros_like(marks_ref)
        marks_ref[0:count, 0:length] = segment[...].astype(F32)


def row_of(ref, r):
    return jnp.sum(jnp.where(iota(ref.shape, 0) == r, ref[...], 0.0), axis=0, keepdims=True)


def to_picked(order, picked, size):
    cap = order.shape[1]
    hit = (order == iota((size, cap), 0).astype(F32)) & (picked > 0.5)
    return jnp.where(hit, 1.0, 0.0)


def from_picked(order, picked, size):
    cap = order.shape[1]
    place = column_of(jnp.where(picked > 0.5, order, -1.0), cap)
    return jnp.where(place == iota((cap, size), 1).astype(F32), 1.0, 0.0).astype(BF)


def sizes(cap):
    half = up_to(cap // 2, HEAD)
    return [(half, up_to(half, LANES)), (cap, cap)]


def loop(count, what):
    lax.fori_loop(0, count, lambda i, c: (what(i), c)[1], 0)


def lanes(i, size):
    return pl.ds(pl.multiple_of(i * size, LANES), size)


def each_size(count, cap, what):
    low = 0
    for rows, keys in sizes(cap):

        @pl.when((count > low) & (count <= rows))
        def _(rows=rows, keys=keys):
            what(rows, keys)

        low = rows


def forbidden(hit, marks, count, size):
    segment_of = dot_nt(jnp.broadcast_to(marks, (8, marks.shape[1])).astype(BF), hit.astype(BF))[0:1]
    segment_of = jnp.where(iota((1, size), 1) < count, segment_of, 99.0)
    column = jnp.sum(hit * marks, axis=1, keepdims=True)
    column = jnp.where(iota((size, 1), 0) < count, column, 99.0)
    return jnp.where(column == segment_of, 0.0, FAR)


def two_heads(pair):
    first = iota(pair.shape, 1) < HEAD
    zero = jnp.zeros_like(pair)
    return jnp.concatenate([jnp.where(first, pair, zero), jnp.where(first, zero, pair)], axis=0)


def one_pair(turned):
    size = turned.shape[1] // 2
    return jnp.concatenate([turned[:HEAD, :size], turned[HEAD:, size:]], axis=0).T


def attend_kernel(x, segment, selected, wa, table, mid, xc, h, qkv, attn, branch, logs, gates, xs, picked, marks, order, bar):
    cap = xs.shape[0]
    span, width = x.shape[1], x.shape[2]
    pad_rows(selected, segment, picked, marks)
    order_of(picked, order)
    xs[...] = jnp.zeros_like(xs)

    def row(r, carry):
        sel, place, mark = row_of(picked, r), row_of(order, r), row_of(marks, r)
        count = jnp.sum(sel).astype(jnp.int32)
        xs[0:span, :] = x[r]
        mid[r] = x[r].astype(F32)

        def work(rows, keys):
            hit = to_picked(place, sel, keys)
            block = forbidden(hit, mark, count, keys)
            bar[0:keys, 0:keys] = block
            bar[0:keys, keys : 2 * keys] = block
            x_in = dot(hit[:rows].astype(BF), xs[...])
            xc[r, 0:rows, :] = x_in.astype(BF)
            n, _ = normalized(x_in)
            h_in = (n * table[GAIN1 : GAIN1 + 1, :] + table[BIAS1 : BIAS1 + 1, :]).astype(BF)
            h[r, 0:rows, :] = h_in
            gate = jax.nn.sigmoid(jnp.sum(h_in.astype(F32) * table[ROUTER : ROUTER + 1, :], axis=1, keepdims=True))
            for i, b in enumerate((B_QUERY, None, B_VALUE)):
                part = dot(h_in, wa[:, i * width : (i + 1) * width])
                if b is not None:
                    part = part + table[b : b + 1, :]
                qkv[r, 0:rows, i * width : (i + 1) * width] = part.astype(BF)
            if keys > rows:
                qkv[r, rows:keys, :] = jnp.zeros((keys - rows, 3 * width), BF)

            def pair(i, carry):
                lane = i * LANES
                q = qkv[r, 0:keys, pl.ds(pl.multiple_of(lane, LANES), LANES)]
                k = qkv[r, 0:keys, pl.ds(pl.multiple_of(lane + width, LANES), LANES)]
                v = qkv[r, 0:keys, pl.ds(pl.multiple_of(lane + 2 * width, LANES), LANES)]
                s = dot_nt(k, two_heads(q * BF(HEAD**-0.5))) + bar[0:keys, 0 : 2 * keys]
                top = jnp.max(s, axis=0, keepdims=True)
                e = jnp.exp(s - top)
                total = jnp.sum(e, axis=0, keepdims=True)
                out = one_pair(dot_tn(v, e.astype(BF)) * (1.0 / total))
                attn[r, 0:keys, pl.ds(pl.multiple_of(lane, LANES), LANES)] = out.astype(BF)
                logs[r, i, 0:1, 0 : 2 * keys] = top + jnp.log(total)
                return carry

            lax.fori_loop(0, width // LANES, pair, 0)
            gates[r, 0:rows, :] = jnp.broadcast_to(gate, (rows, LANES))
            out = dot(attn[r, 0:rows, :], wa[:, 3 * width :]) + table[B_OUT : B_OUT + 1, :]
            branch[r, 0:rows, :] = out.astype(BF)
            back = from_picked(place, sel, keys)[:span, :rows]
            mid[r] += dot(back, (out * gate).astype(BF))

        each_size(count, cap, work)
        return carry

    lax.fori_loop(0, x.shape[0], row, 0)


def attend(patches, segment, selected, wa, table):
    count, span, width = patches.shape
    cap = up_to(span, LANES)

    def out(cols, kind):
        return jax.ShapeDtypeStruct((count, cap, cols), kind)

    return pl.pallas_call(
        attend_kernel,
        out_shape=(
            jax.ShapeDtypeStruct((count, span, width), F32),
            out(width, BF), out(width, BF), out(3 * width, BF), out(width, BF), out(width, BF),
            jax.ShapeDtypeStruct((count, width // LANES, 1, 2 * cap), F32),
            out(LANES, F32),
        ),
        in_specs=[pl.BlockSpec(memory_space=pltpu.VMEM)] * 5,
        out_specs=(pl.BlockSpec(memory_space=pltpu.VMEM),) * 8,
        scratch_shapes=[
            pltpu.VMEM((cap, width), BF),
            pltpu.VMEM((8, cap), F32),
            pltpu.VMEM((8, cap), F32),
            pltpu.VMEM((8, cap), F32),
            pltpu.VMEM((cap, 2 * cap), F32),
        ],
        compiler_params=pltpu.CompilerParams(vmem_limit_bytes=60 * 2**20),
        name="attend",
    )(patches, segment, selected, wa, table)


def attend_back_kernel(
    mixed, gm, segment, selected, wa, table, xc, h, qkv, attn, branch, logs, gates,
    rows_x, rows_mixed, grad_a, sums, grad_x, high, picked, marks, order, bar, ga, dqkv,
):
    cap = high.shape[0]
    span, width = gm.shape[1], gm.shape[2]
    pad_rows(selected, segment, picked, marks)
    order_of(picked, order)
    high[...] = jnp.zeros_like(high)
    grad_a[...] = jnp.zeros_like(grad_a)
    sums[...] = jnp.zeros_like(sums)

    def add(i, v):
        sums[i : i + 1, :] += jnp.sum(v, axis=0, keepdims=True)

    def add_weight(i, j, v):
        at = slice(i * width, j * width)
        grad_a[:, at] = (grad_a[:, at].astype(F32) + v).astype(BF)

    def row(r, carry):
        sel, place, mark = row_of(picked, r), row_of(order, r), row_of(marks, r)
        count = jnp.sum(sel).astype(jnp.int32)
        high[0:span, :] = gm[r]

        @pl.when(count == 0)
        def _():
            grad_x[r] = gm[r]

        def work(rows, keys):
            hit = to_picked(place, sel, keys)
            block = forbidden(hit, mark, count, keys)
            bar[0:keys, 0:keys] = block
            bar[0:keys, keys : 2 * keys] = block
            take = hit[:rows].astype(BF)
            g = dot(take, high[...])
            gate = gates[r, 0:rows, 0:1]
            grad_logit = jnp.sum(g * branch[r, 0:rows, :].astype(F32), axis=1, keepdims=True) * gate * (1.0 - gate)
            gb = g * gate
            add(B_OUT, gb.astype(BF).astype(F32))
            gb = gb.astype(BF)
            add_weight(3, 4, dot_tn(attn[r, 0:rows, :], gb))
            ga[0:rows, :] = dot_nt(gb, wa[:, 3 * width :]).astype(BF)
            if keys > rows:
                ga[rows:keys, :] = jnp.zeros((keys - rows, width), BF)

            def pair(i, carry):
                at = pl.ds(pl.multiple_of(i * LANES, LANES), LANES)
                at_k = pl.ds(pl.multiple_of(i * LANES + width, LANES), LANES)
                at_v = pl.ds(pl.multiple_of(i * LANES + 2 * width, LANES), LANES)
                q2 = two_heads(qkv[r, 0:keys, at] * BF(HEAD**-0.5))
                k = qkv[r, 0:keys, at_k]
                v = qkv[r, 0:keys, at_v]
                g2 = two_heads(ga[0:keys, at])
                p = jnp.exp(dot_nt(k, q2) + bar[0:keys, 0 : 2 * keys] - logs[r, i, 0:1, 0 : 2 * keys])
                dp = dot_nt(v, g2)
                ds = (p * (dp - jnp.sum(p * dp, axis=0, keepdims=True))).astype(BF)
                dqkv[0:keys, at] = one_pair(dot_tn(k, ds) * HEAD**-0.5).astype(BF)
                dqkv[0:keys, at_k] = dot(ds, q2).astype(BF)
                dqkv[0:keys, at_v] = dot(p.astype(BF), g2).astype(BF)
                return carry

            lax.fori_loop(0, width // LANES, pair, 0)
            add(B_QUERY, dqkv[0:rows, 0:width].astype(F32))
            add(B_VALUE, dqkv[0:rows, 2 * width :].astype(F32))
            h_in = h[r, 0:rows, :]
            add(ROUTER, h_in.astype(F32) * grad_logit)
            add_weight(0, 3, dot_tn(h_in, dqkv[0:rows, :]))
            gh = dot_nt(dqkv[0:rows, :], wa[:, : 3 * width]) + grad_logit * table[ROUTER : ROUTER + 1, :]
            n, scale = normalized(xc[r, 0:rows, :].astype(F32))
            add(GAIN1, n * gh)
            add(BIAS1, gh)
            dx = norm_back(n, scale, table[GAIN1 : GAIN1 + 1, :], gh).astype(BF)
            back = from_picked(place, sel, keys)[:span, :rows]
            grad_x[r] = (gm[r].astype(F32) + dot(back, dx)).astype(BF)

        each_size(count, cap, work)
        return carry

    lax.fori_loop(0, gm.shape[0], row, 0)
    for r in range(gm.shape[0]):
        rows_x[:, r, :] = grad_x[r, 0 : rows_x.shape[0], :]
        rows_mixed[:, r, :] = mixed[r, 0 : rows_x.shape[0], :]


def attend_back(mixed, gm, segment, selected, wa, table, kept):
    count, span, width = gm.shape
    cap = up_to(span, LANES)
    rows_out = jax.ShapeDtypeStruct((segment.shape[1], count, width), BF)
    rows_x, rows_mixed, grad_a, sums = pl.pallas_call(
        attend_back_kernel,
        out_shape=(
            rows_out,
            rows_out,
            jax.ShapeDtypeStruct(wa.shape, BF),
            jax.ShapeDtypeStruct((16, width), F32),
        ),
        in_specs=[pl.BlockSpec(memory_space=pltpu.VMEM)] * 13,
        out_specs=(pl.BlockSpec(memory_space=pltpu.VMEM),) * 4,
        scratch_shapes=[
            pltpu.VMEM(gm.shape, BF),
            pltpu.VMEM((cap, width), BF),
            pltpu.VMEM((8, cap), F32),
            pltpu.VMEM((8, cap), F32),
            pltpu.VMEM((8, cap), F32),
            pltpu.VMEM((cap, 2 * cap), F32),
            pltpu.VMEM((cap, width), BF),
            pltpu.VMEM((cap, 3 * width), BF),
        ],
        compiler_params=pltpu.CompilerParams(vmem_limit_bytes=60 * 2**20),
        name="attend_back",
    )(mixed, gm, segment, selected, wa, table, *kept)
    return rows_x.transpose(1, 0, 2), rows_mixed.transpose(1, 0, 2), grad_a, sums


def gelu_parts(p):
    z = jnp.abs(p)
    e = jnp.exp(-0.5 * p * p)
    t = 1.0 / (1.0 + (0.3275911 * 0.5**0.5) * z)
    poly = ((((1.061405429 * t - 1.453152027) * t + 1.421413741) * t - 0.284496736) * t + 0.254829592) * t
    tail = 0.5 * poly * e
    phi = jnp.where(p > 0, 1.0 - tail, tail)
    return phi, phi + p * (e * 0.3989422804014327)


BLOCK = 592


class ChunkScatter:
    def __init__(self, p, kind, whole, bufs, fin, sems):
        self.p, self.kind, self.whole, self.fin, self.sems = p, kind, whole, fin, sems
        self.got, self.one, self.give, self.two, self.line, self.far = bufs
        rail0 = p.c == 0
        self.me = p.y * 2 + p.x
        self.first = jnp.where(rail0, p.y * 2 + 1 - p.x, (1 - p.y) * 2 + p.x)
        self.second = jnp.where(rail0, (1 - p.y) * 2 + p.x, p.y * 2 + 1 - p.x)
        self.diag = (1 - p.y) * 2 + 1 - p.x
        self.to_first = (p.z, self.first * 2 + p.c)
        self.to_second = (p.z, self.second * 2 + p.c)

    def move(self, stage, j, src, dst, to):
        return push(src, dst, self.sems.at[0, stage, self.kind, j], self.sems.at[1, stage, self.kind, j], to)

    def rail(self, j, c):
        if self.kind == 0:
            return self.whole.at[j, :, c]
        return self.whole.at[j, :, :, :, lanes(c, self.whole.shape[4] // 2)]

    def block(self, j, chip):
        if self.kind == 0:
            return self.whole.at[j, chip, self.p.c]
        return self.whole.at[j, :, chip, :, lanes(self.p.c, self.whole.shape[4] // 2)]

    def core(self, j):
        return self.move(0, j, self.rail(j, 1 - self.p.c), self.got.at[j], self.p.to_core)

    def step1(self, j, slot):
        return self.move(1 + slot, j, self.block(j, self.diag if slot else self.first), self.one.at[j, slot], self.to_first)

    def step2(self, j):
        return self.move(3, j, self.give.at[j], self.two.at[j], self.to_second)

    def begin(self, j):
        self.core(j).start()

    def pair(self, j):
        self.core(j).wait_recv()
        mine = self.rail(j, self.p.c)
        mine[...] = (mine[...].astype(F32) + self.got[j].astype(F32)).astype(BF)
        self.step1(j, 1).start()
        self.step1(j, 0).start()

    def side(self, j):
        self.step1(j, 1).wait_recv()
        self.give[j] = (self.block(j, self.second)[...].astype(F32) + self.one[j, 1].astype(F32)).astype(BF)
        self.step2(j).start()

    def along(self, j, s):
        if self.kind == 0:
            src = self.line.at[j]
        else:
            src = self.line.at[j, s - 1]
        return self.move(3 + s, j, src, self.far.at[j, s - 1], self.p.to_z(s))

    def plane_sum(self, j, l):
        if self.kind == 0:
            return self.block(j, self.me)[...].astype(F32) + self.one[j, 0].astype(F32) + self.two[j].astype(F32)
        own = self.whole[j, l, self.me, :, lanes(self.p.c, self.whole.shape[4] // 2)]
        return own.astype(F32) + self.one[j, 0, l].astype(F32) + self.two[j, l].astype(F32)

    def cross(self, j, owner):
        z = self.p.z
        self.step1(j, 0).wait_recv()
        self.step2(j).wait_recv()
        if self.kind == 0:
            self.line[j] = self.plane_sum(j, 0).astype(BF)
            for s in (1, 2, 3):

                @pl.when(lax.rem(z + s, 4) == owner)
                def _(s=s):
                    self.along(j, s).start()

            return
        for s in (1, 2, 3):
            self.line[j, s - 1] = self.plane_sum(j, lax.rem(z + s, 4)).astype(BF)
            self.along(j, s).start()

    def last(self, j, owner):
        if self.kind == 0:

            @pl.when(self.p.z == owner)
            def _():
                total = self.plane_sum(j, 0)
                for s in (1, 2, 3):
                    self.along(j, s).wait_recv()
                    total = total + self.far[j, s - 1].astype(F32)
                self.fin[...] = total

            return
        total = self.plane_sum(j, self.p.z)
        for s in (1, 2, 3):
            self.along(j, s).wait_recv()
            total = total + self.far[j, s - 1].astype(F32)
        self.fin[j] = total

    def finish(self, owner_of):
        def one(j):
            self.core(j).wait_send()
            self.step1(j, 0).wait_send()
            self.step1(j, 1).wait_send()
            self.step2(j).wait_send()
            for s in (1, 2, 3):
                if self.kind == 0:

                    @pl.when(lax.rem(self.p.z + s, 4) == owner_of(j))
                    def _(s=s):
                        self.along(j, s).wait_send()

                else:
                    self.along(j, s).wait_send()

        loop(4, one)


def mlp_kernel(remote, mid, g, wu, wd, table, mixed, gm, sums, out_u, out_d, *refs):
    u, acc, act, gp, hold_u, hold_d, weight_sems = refs[:7]
    count, span, width = mid.shape
    tokens = count * span
    chunk = width
    chunks = wd.shape[0] // chunk
    blocks = tokens // BLOCK
    per = span // BLOCK
    if remote:
        grad_d, grad_u, fin_u = refs[7:10]
        bufs_d, bufs_u = refs[10:16], refs[16:22]
        sems, last_sems = refs[22:]
        p = Place()
        greet(p)
        down = ChunkScatter(p, 0, grad_d, bufs_d, out_d, sems)
        up = ChunkScatter(p, 1, grad_u, bufs_u, fin_u, sems)
        rail = width // 2
        rows = out_u.shape[0]

    def row(i):
        return table[i : i + 1, :]

    def each_block(what):
        loop(blocks, lambda b: what(b, pl.ds(pl.multiple_of(b * BLOCK, 16), BLOCK)))

    def mid_of(b):
        return mid[b // per, pl.ds(pl.multiple_of(lax.rem(b, per) * BLOCK, 16), BLOCK), :]

    def level_of(i):
        return jnp.where(i == 0, 0, jnp.where(i == 1, 3, i - 1))

    def load(i):
        j, slot = level_of(i), lax.rem(i, 2)
        return (
            pltpu.make_async_copy(wu.at[:, lanes(j, chunk)], hold_u.at[slot], weight_sems.at[0, slot]),
            pltpu.make_async_copy(
                wd.at[pl.ds(pl.multiple_of(j * chunk, 16), chunk)], hold_d.at[slot], weight_sems.at[1, slot]
            ),
        )

    for cp in load(0):
        cp.start()
    sums[...] = jnp.zeros_like(sums)
    acc[...] = jnp.zeros_like(acc)
    def start(b, at):
        n, _ = normalized(mid_of(b))
        u[at, :] = (n * row(GAIN2) + row(BIAS2)).astype(BF)
        sums[B_DOWN : B_DOWN + 1, :] += jnp.sum(g[at, :].astype(F32), axis=0, keepdims=True)

    each_block(start)

    def send_rail(i):
        lane = pl.ds(pl.multiple_of(level_of(i) * chunk + p.c * rail, TILE), rail)
        return push(
            fin_u.at[i, pl.ds(pl.multiple_of((1 - p.c) * rows, 8), rows)], out_u.at[:, lane],
            last_sems.at[0, i], last_sems.at[1, i], p.to_core,
        )

    def own_rail(i):
        up.last(i, 0)
        send_rail(i).start()
        lane = pl.ds(pl.multiple_of(level_of(i) * chunk + p.c * rail, TILE), rail)
        out_u[:, lane] = fin_u[i, pl.ds(pl.multiple_of(p.c * rows, 8), rows), :]

    def from_chunk(i, back, what):
        if remote:
            pl.when(i >= back)(lambda: what(i - back))

    def one_chunk(i):
        j, slot = level_of(i), lax.rem(i, 2)
        for cp in load(i):
            cp.wait()

        @pl.when(i + 1 < chunks)
        def _():
            for cp in load(i + 1):
                cp.start()

        def hidden(b, at):
            pre = dot(u[at, :], hold_u[slot]) + table[pl.ds(B_UP + j, 1), :]
            phi, slope = gelu_parts(pre)
            act[at, :] = (pre * phi).astype(BF)
            grad_pre = (slope * dot_nt(g[at, :], hold_d[slot])).astype(BF)
            gp[at, :] = grad_pre
            sums[pl.ds(B_UP + j, 1), :] += jnp.sum(grad_pre.astype(F32), axis=0, keepdims=True)

        each_block(hidden)
        from_chunk(i, 1, lambda k: down.cross(k, level_of(k)))
        from_chunk(i, 1, lambda k: up.side(k))
        from_chunk(i, 2, own_rail)
        part = dot_tn(act[...], g[...]).astype(BF)
        if remote:
            grad_d[i] = part.reshape(grad_d.shape[1:])
            down.begin(i)
        else:
            out_d[pl.ds(pl.multiple_of(j * chunk, 16), chunk), :] = part
        part = dot_tn(u[...], gp[...]).astype(BF)
        if remote:
            grad_u[i] = part.reshape(grad_u.shape[1:])
            up.begin(i)
            down.pair(i)
        else:
            out_u[:, lanes(j, chunk)] = part
        from_chunk(i, 1, lambda k: up.cross(k, 0))

        def total(b, at):
            acc[0, at, :] += dot(act[at, :], hold_d[slot])
            acc[1, at, :] += dot_nt(gp[at, :], hold_u[slot])

        for b in range(blocks):
            total(b, pl.ds(b * BLOCK, BLOCK))
            if remote and b == 0:
                up.pair(i)
        if remote:
            down.side(i)
        from_chunk(i, 1, lambda k: down.last(k, level_of(k)))

    loop(chunks, one_chunk)

    def end(b, at):
        m = mid_of(b)
        out = (m + acc[0, at, :] + row(B_DOWN)).astype(BF)
        mixed[b] = out
        n, scale = normalized(m)
        e = acc[1, at, :]
        sums[GAIN2 : GAIN2 + 1, :] += jnp.sum(n * e, axis=0, keepdims=True)
        sums[BIAS2 : BIAS2 + 1, :] += jnp.sum(e, axis=0, keepdims=True)
        gm[b] = (g[at, :].astype(F32) + norm_back(n, scale, row(GAIN2), e)).astype(BF)

    for b in range(blocks):
        end(b, pl.ds(b * BLOCK, BLOCK))
        if remote and b == 0:
            down.cross(chunks - 1, level_of(chunks - 1))
            up.side(chunks - 1)
            own_rail(chunks - 2)
    if remote:
        up.cross(chunks - 1, 0)
        down.last(chunks - 1, level_of(chunks - 1))
        own_rail(chunks - 1)
        for i in range(4):
            send_rail(i).wait()
        up.finish(level_of)
        down.finish(level_of)


def mlp(remote, mid, cot, wu, wd, table):
    count, span, width = mid.shape
    tokens = count * span
    if remote:
        rows, depth = wu.shape[0] // 32, wd.shape[0] // 32
        outs = [jax.ShapeDtypeStruct((rows, wu.shape[1]), F32), jax.ShapeDtypeStruct((depth, width), F32)]
        half = width // 2
        extra = [
            pltpu.VMEM((4, 4, 2, depth, width), BF),
            pltpu.VMEM((4, 4, 4, 2 * rows, width), BF),
            pltpu.VMEM((4, 2 * rows, half), F32),
        ]
        extra += [pltpu.VMEM((4, 4, depth, width), BF), pltpu.VMEM((4, 2, depth, width), BF)]
        extra += [pltpu.VMEM((4, depth, width), BF)] * 3 + [pltpu.VMEM((4, 3, depth, width), BF)]
        extra += [pltpu.VMEM((4, 4, 4, 2 * rows, half), BF), pltpu.VMEM((4, 2, 4, 2 * rows, half), BF)]
        extra += [pltpu.VMEM((4, 4, 2 * rows, half), BF)] * 2 + [pltpu.VMEM((4, 3, 2 * rows, half), BF)] * 2
        extra += [pltpu.SemaphoreType.DMA((2, 7, 2, 4)), pltpu.SemaphoreType.DMA((2, 4))]
        params = dict(collective_id=2, has_side_effects=True)
    else:
        outs = [jax.ShapeDtypeStruct(wu.shape, BF), jax.ShapeDtypeStruct(wd.shape, BF)]
        extra, params = [], {}
    vmem = pl.BlockSpec(memory_space=pltpu.VMEM)
    hbm = pl.BlockSpec(memory_space=pl.ANY)
    return pl.pallas_call(
        partial(mlp_kernel, remote),
        out_shape=(
            jax.ShapeDtypeStruct(mid.shape, BF),
            jax.ShapeDtypeStruct(mid.shape, BF),
            jax.ShapeDtypeStruct((16, width), F32),
            *outs,
        ),
        in_specs=[vmem, vmem, hbm, hbm, vmem],
        out_specs=(vmem,) * 5,
        scratch_shapes=[
            pltpu.VMEM((tokens, width), BF),
            pltpu.VMEM((2, tokens, width), F32),
            pltpu.VMEM((tokens, width), BF),
            pltpu.VMEM((tokens, width), BF),
            pltpu.VMEM((2, width, width), BF),
            pltpu.VMEM((2, width, width), BF),
            pltpu.SemaphoreType.DMA((2, 2)),
            *extra,
        ],
        compiler_params=pltpu.CompilerParams(vmem_limit_bytes=62 * 2**20, **params),
        name="mlp",
    )(mid, cot.reshape(tokens, width), wu, wd, table)


def local(
    small, patches, segment_ids, selected, cotangent, ln1_gain, ln1_bias, w_router, w_query, b_query,
    w_key, w_value, b_value, w_out, b_out, ln2_gain, ln2_bias, w_up, b_up, w_down, b_down,
):
    length, width = patches.shape[1:]
    span = up_to(length, 16)
    vectors = (ln1_gain, ln1_bias, w_router, b_query, b_value, b_out, ln2_gain, ln2_bias, b_down)
    matrices = (w_query, w_key, w_value, w_out, w_up, w_down)
    if small:
        attn_w, up_w, down_w, table, x, cot = gather_all(vectors, b_up, matrices, (patches, cotangent), span)
        attn_w = attn_w.reshape(-1, attn_w.shape[2])
        up_w = up_w.reshape(-1, up_w.shape[2])
        down_w = down_w.reshape(-1, down_w.shape[3])
    else:
        whole = [lax.all_gather(v, AXES, axis=0, tiled=True) for v in vectors + (b_up,)]
        table = jnp.concatenate(
            [jnp.stack(whole[:VECTORS]), whole[VECTORS].reshape(4, width), jnp.zeros((3, width), BF)]
        ).astype(F32)
        attn_w = jnp.concatenate([lax.all_gather(w, AXES, axis=0, tiled=True) for w in matrices[:4]], axis=1)
        up_w = lax.all_gather(w_up, AXES, axis=0, tiled=True)
        down_w = lax.all_gather(w_down, AXES, axis=0, tiled=True)
        x, cot = [jnp.pad(v, ((0, 0), (0, span - length), (0, 0))) for v in (patches, cotangent)]
    mid, *kept = attend(x, segment_ids, selected, attn_w, table)
    mixed, grad_mid, sums_mlp, grad_u, grad_d = mlp(small, mid, cot, up_w, down_w, table)
    grad_x, mixed, grad_a, sums_attn = attend_back(mixed, grad_mid, segment_ids, selected, attn_w, table, kept)
    if small:
        own_a, own_v, own_b = scatter_all(grad_a.reshape(16, -1, grad_a.shape[1]), sums_mlp, sums_attn)
        own_m = jnp.split(own_a, 4, axis=1) + [grad_u, grad_d]
        own = [own_v[i, : ln1_gain.shape[0]] for i in range(VECTORS)]
        own_up_b = own_b[0, : b_up.shape[0]]
    else:
        sums = sums_mlp + sums_attn
        own = [lax.psum_scatter(sums[i], AXES, scatter_dimension=0, tiled=True) for i in range(VECTORS)]
        own_up_b = lax.psum_scatter(
            sums[VECTORS : VECTORS + 4].reshape(-1), AXES, scatter_dimension=0, tiled=True
        )
        own_m = [
            lax.psum_scatter(g.astype(F32), AXES, scatter_dimension=0, tiled=True)
            for g in jnp.split(grad_a, 4, axis=1) + [grad_u, grad_d]
        ]
    return (
        mixed, grad_x, own[0], own[1], own[2], own_m[0], own[3], own_m[1], own_m[2], own[4],
        own_m[3], own[5], own[6], own[7], own_m[4], own_up_b, own_m[5], own[8],
    )


def solution(mesh):
    flat, rows2, rows3 = P(AXES), P(AXES, None), P(AXES, None, None)
    vec, mat = flat, rows2
    small = mesh.shape["dp"] == 4 and mesh.shape["fsdp"] == 8
    return jax.shard_map(
        partial(local, small),
        mesh=mesh,
        in_specs=(
            rows3, rows2, rows2, rows3, vec, vec, vec, mat, vec, mat, mat, vec, mat, vec, vec, vec, mat, vec, mat, vec,
        ),
        out_specs=(
            rows3, rows3, vec, vec, vec, mat, vec, mat, mat, vec, mat, vec, vec, vec, mat, vec, mat, vec,
        ),
        check_vma=False,
    )
```

```python
from functools import partial
import math

import jax
import jax.numpy as jnp
from jax import lax
from jax.experimental import pallas as pl
from jax.experimental.pallas import tpu as pltpu
from jax.sharding import PartitionSpec as P

AXES = ("dp", "fsdp")
MESH = pl.DeviceIdType.MESH
BF = jnp.bfloat16
F32 = jnp.float32


class Place:
    def __init__(self):
        self.z = lax.axis_index("dp")
        self.f = lax.axis_index("fsdp")
        self.c = lax.rem(self.f, 2)
        self.x = lax.rem(self.f // 2, 2)
        self.y = self.f // 4
        self.chip = self.z * 4 + self.y * 2 + self.x
        self.chip_x = self.z * 4 + self.y * 2 + (1 - self.x)
        self.chip_y = self.z * 4 + (1 - self.y) * 2 + self.x
        self.to_core = (self.z, self.y * 4 + self.x * 2 + (1 - self.c))
        self.to_x = (self.z, self.y * 4 + (1 - self.x) * 2 + self.c)
        self.to_y = (self.z, (1 - self.y) * 4 + self.x * 2 + self.c)

    def to_z(self, step):
        return (lax.rem(self.z + step + 4, 4), self.f)


def greet(place):
    bar = pltpu.get_barrier_semaphore()
    others = [place.to_core, place.to_x, place.to_y] + [place.to_z(s) for s in (1, 2, 3)]
    for other in others:
        pl.semaphore_signal(bar, inc=1, device_id=other, device_id_type=MESH)
    pl.semaphore_wait(bar, len(others))


def push(src, dst, send, recv, to):
    return pltpu.make_async_remote_copy(
        src_ref=src, dst_ref=dst, send_sem=send, recv_sem=recv, device_id=to, device_id_type=MESH
    )


class Gather:
    def __init__(self, place, j, block, level, plane_first, sems):
        self.p, self.j, self.block, self.level, self.sems = place, j, block, level, sems
        self.plane_first = plane_first

    def copy(self, kind, i, ref, to):
        return push(ref, ref, self.sems.at[2 * kind, self.j, i], self.sems.at[2 * kind + 1, self.j, i], to)

    def piece(self, l):
        if self.plane_first:
            return self.level(l, self.p.c)
        return self.block(l * 4 + self.p.y * 2 + self.p.x)

    def up(self, k):
        return self.copy(0, k, self.piece(lax.rem(self.p.z - k + 4, 4)), self.p.to_z(1))

    def up_in(self, k):
        return self.copy(0, k, self.piece(lax.rem(self.p.z - k + 3, 4)), self.p.to_z(1))

    def down(self, k):
        return self.copy(1, k, self.piece(lax.rem(self.p.z + k, 4)), self.p.to_z(3))

    def down_in(self, k):
        return self.copy(1, k, self.piece(lax.rem(self.p.z + k + 1, 4)), self.p.to_z(3))

    def xs(self, l):
        return self.copy(2, l, self.block(l * 4 + self.p.y * 2 + self.p.x), self.p.to_x)

    def ys(self, l):
        return self.copy(3, l, self.block(l * 4 + self.p.y * 2 + self.p.x), self.p.to_y)

    def side_in(self, l, y_side):
        p = self.p
        chip = l * 4 + (p.y + y_side - 2 * p.y * y_side) * 2 + (p.x + (1 - y_side) - 2 * p.x * (1 - y_side))
        return self.copy(2 + y_side, l, self.block(chip), p.to_x)

    def forward(self, l):
        p = self.p
        chip = l * 4 + jnp.where(p.c == 0, (1 - p.y) * 2 + p.x, p.y * 2 + 1 - p.x)
        to = (p.z, jnp.where(p.c == 0, p.y * 4 + (1 - p.x) * 2 + p.c, (1 - p.y) * 4 + p.x * 2 + p.c))
        return self.copy(4, l, self.block(chip), to)

    def forward_in(self, l):
        return self.copy(4, l, self.block(l * 4 + (1 - self.p.y) * 2 + 1 - self.p.x), self.p.to_x)

    def cs(self, l):
        return self.copy(5, l, self.level(l, self.p.c), self.p.to_core)

    def cs_in(self, l):
        return self.copy(5, l, self.level(l, 1 - self.p.c), self.p.to_core)

    def sides(self, l):
        self.xs(l).start()
        self.ys(l).start()

    def ends(self, k):
        z = self.p.z

        @pl.when((z >= k) & (z < 3))
        def _():
            self.up(k).start()

        @pl.when((z + k <= 3) & (z > 0))
        def _():
            self.down(k).start()

    def begin(self):
        if not self.plane_first:
            self.ends(0)
        self.sides(self.p.z)

    def along_z(self, k, onward=True):
        z = self.p.z

        @pl.when(z > k)
        def _():
            self.up_in(k).wait_recv()

        @pl.when(z + k < 3)
        def _():
            self.down_in(k).wait_recv()

        if k < 2:
            self.ends(k + 1)
        if onward:
            self.each(k + 1, (lambda l: self.cs(l).start()) if self.plane_first else self.sides)

    def each(self, k, what):
        z = self.p.z
        if k == 0:
            what(z)
            return

        @pl.when(z >= k)
        def _():
            what(z - k)

        @pl.when(z + k <= 3)
        def _():
            what(z + k)

    def turn(self, l):
        self.side_in(l, 1 - self.p.c).wait_recv()
        self.forward(l).start()
        self.side_in(l, self.p.c).wait_recv()

    def across(self, l):
        self.forward_in(l).wait_recv()
        if self.plane_first:
            self.ends(0)
        self.cs(l).start()

    def finish(self):
        z = self.p.z
        self.finish_z()
        for l in range(4):
            if self.plane_first:
                continue
            self.xs(l).wait_send()
            self.ys(l).wait_send()
            self.forward(l).wait_send()
        if self.plane_first:
            self.xs(z).wait_send()
            self.ys(z).wait_send()
            self.forward(z).wait_send()
        for l in range(4):
            self.cs(l).wait_send()
            self.cs_in(l).wait_recv()

    def finish_z(self):
        z = self.p.z
        for k in range(3):

            @pl.when((z >= k) & (z < 3))
            def _():
                self.up(k).wait_send()

            @pl.when((z + k <= 3) & (z > 0))
            def _():
                self.down(k).wait_send()


VECTORS = 9
TILE = 128


def vector_steps(p, values, out_ref, hold, landed, sems):
    send, recv = sems.at[0], sems.at[1]
    state = {}

    def begin():
        state["value"] = values()
        hold[0] = state["value"]
        push(hold.at[0], landed.at[0], send.at[0], recv.at[0], p.to_core).start()

    def then(i, to, after):
        def step():
            push(hold.at[i], landed.at[i], send.at[i], recv.at[i], to).wait()
            hold[i + 1] = hold[i] + landed[i]
            after()
        return step

    def next_side():
        push(hold.at[1], landed.at[1], send.at[1], recv.at[1], p.to_x).start()

    def next_other():
        push(hold.at[2], landed.at[2], send.at[2], recv.at[2], p.to_y).start()

    def line(s):
        return push(hold.at[3], landed.at[2 + s], send.at[2 + s], recv.at[2 + s], p.to_z(s))

    def next_line():
        for s in (1, 2, 3):
            line(s).start()

    def last():
        for s in (1, 2, 3):
            line(s).wait()
        out_ref[...] = hold[3] + landed[3] + landed[4] + landed[5]

    return [begin, then(0, p.to_core, next_side), then(1, p.to_x, next_other), then(2, p.to_y, next_line), last]


def cut(cols, share):
    first = int(round(cols * (1 - share) / TILE)) * TILE
    return first


PLANE_SHARE = 0.12


def gather_kernel(*refs):
    vectors, b_up = refs[:VECTORS], refs[VECTORS]
    wq, wk, wv, wo, wu, wd = refs[VECTORS + 1 : VECTORS + 7]
    rows_in = refs[VECTORS + 7 : VECTORS + 9]
    out_a, out_u, out_d, out_v = refs[VECTORS + 9 : VECTORS + 13]
    rows_out = refs[VECTORS + 13 : VECTORS + 15]
    rows_held = refs[VECTORS + 15 : VECTORS + 17]
    held, give, take, packed, hold, landed, sems, pair_sems, own_sems, vec_sems = refs[VECTORS + 17 :]
    p = Place()
    width = wq.shape[1]
    rail = 2 * width
    rows = wq.shape[0]
    lower = p.c == 0
    loads = [pltpu.make_async_copy(w, held.at[0, :, pl.ds(i * width, width)], own_sems.at[3 + i]) for i, w in enumerate((wq, wk, wv, wo))]
    loads.append(pltpu.make_async_copy(wu, held.at[1], own_sems.at[7]))
    own_d = pltpu.make_async_copy(wd, out_d.at[p.z], own_sems.at[2])
    moves = [pltpu.make_async_copy(a, b, own_sems.at[8 + i]) for i, (a, b) in enumerate(zip(rows_in, rows_held))]
    for cp in loads + moves:
        cp.start()
    own_d.start()
    greet(p)
    for cp in loads:
        cp.wait()
    mine = pl.ds(pl.multiple_of(p.c * rail, TILE), rail)
    other = pl.ds(pl.multiple_of((1 - p.c) * rail, TILE), rail)
    pair = []
    for i in range(2):
        give[i] = held[i, :, other].astype(F32)
        pair.append(push(give.at[i], take.at[i], pair_sems.at[0, i], pair_sems.at[1, i], p.to_core))
        pair[i].start()
    jobs = []

    def add_jobs(out, rail_cols, columns_by_rail):
        first = cut(rail_cols, PLANE_SHARE)
        for start, size, plane in ((0, first, False), (first, rail_cols - first, True)):
            if size == 0:
                continue
            if columns_by_rail:
                def lanes(c, start=start, size=size):
                    return pl.ds(pl.multiple_of(c * rail_cols + start, TILE), size)
                block = lambda chip, out=out, lanes=lanes: out.at[chip, :, lanes(p.c)]
                level = lambda l, c, out=out, lanes=lanes: out.at[pl.ds(l * 4, 4), :, lanes(c)]
            else:
                lane = pl.ds(start, size)
                block = lambda chip, out=out, lane=lane: out.at[chip, p.c, :, lane]
                level = lambda l, c, out=out, lane=lane: out.at[pl.ds(l * 4, 4), c, :, lane]
            jobs.append(Gather(p, len(jobs), block, level, plane, sems))

    add_jobs(out_a, rail, True)
    add_jobs(out_u, rail, True)
    per = len(jobs) // 2
    for i, out in enumerate((out_a, out_u)):
        pair[i].wait()
        own = held[i, :, mine].astype(F32)
        got = take[i]
        packed[i] = jnp.concatenate([jnp.where(lower, own, got), jnp.where(lower, got, own)], axis=0).astype(BF)
        cp = pltpu.make_async_copy(packed.at[i], out.at[p.chip, :, mine], own_sems.at[i])
        cp.start()
        cp.wait()
        for job in jobs[i * per : (i + 1) * per][::-1]:
            job.begin()
    rows_d = Gather(p, len(jobs), lambda chip: out_d.at[chip // 4], None, False, sems)
    own_d.wait()
    rows_d.ends(0)
    device = p.z * 8 + p.f

    def spread(ref):
        count = ref.shape[1]
        total = count * 32
        lane = lax.broadcasted_iota(jnp.int32, (count, total), 1)
        row = lax.broadcasted_iota(jnp.int32, (count, total), 0)
        place = (lane == row + device * count).astype(BF)
        return jnp.dot(ref[...], place, preferred_element_type=F32)

    def values():
        rows_of = [spread(v) for v in vectors]
        up = spread(b_up)
        rows_of += [up[:, i * width : (i + 1) * width] for i in range(4)]
        rows_of.append(jnp.zeros((3, width), F32))
        return jnp.concatenate(rows_of, axis=0)

    steps = vector_steps(p, values, out_v, hold, landed, vec_sems)
    steps[0]()
    plane = [job for job in jobs if job.plane_first]
    line = [job for job in jobs if not job.plane_first]
    for job in plane:
        job.turn(p.z)
    length, count = rows_in[0].shape[0], rows_in[0].shape[1]
    span = rows_out[0].shape[1]
    low = length // 16 * 16

    def lay_out(i, r):
        if r == 0:
            moves[i].wait()
        rows_out[i][r, low:span, :] = jnp.zeros((span - low, width), BF)
        rows_out[i][r, 0:length, :] = rows_held[i][:, r, :]

    work = [(i, r) for i in range(2) for r in range(count)]
    lay_out(*work[0])
    steps[1]()
    for job in plane:
        job.across(p.z)
    for r in range(1, count):
        lay_out(*work[r])
    for k in range(4):
        if k < 3:
            for job in line + plane:
                job.along_z(k)
            rows_d.along_z(k, False)
            steps[k + 2]()
        for job in line:
            job.each(k, job.turn)
        if k == 0:
            for item in work[count:]:
                lay_out(*item)
        if k > 0:
            for job in line:
                job.each(k - 1, job.across)
    for job in line:
        job.each(3, job.across)
    rows_d.finish_z()
    for job in jobs:
        job.finish()


def gather_all(vectors, b_up, matrices, rows_in, span):
    wq, wd = matrices[0], matrices[5]
    rows, width = wq.shape
    rail = 2 * width
    depth = wd.shape[0]
    turned = [v.transpose(1, 0, 2) for v in rows_in]
    count = rows_in[0].shape[0]
    return pl.pallas_call(
        gather_kernel,
        out_shape=(
            jax.ShapeDtypeStruct((16, 2 * rows, 4 * width), BF),
            jax.ShapeDtypeStruct((16, 2 * rows, 4 * width), BF),
            jax.ShapeDtypeStruct((4, depth, width), BF),
            jax.ShapeDtypeStruct((16, width), F32),
            jax.ShapeDtypeStruct((count, span, width), BF),
            jax.ShapeDtypeStruct((count, span, width), BF),
        ),
        in_specs=[pl.BlockSpec(memory_space=pltpu.VMEM)] * (VECTORS + 1) + [pl.BlockSpec(memory_space=pl.ANY)] * 8,
        out_specs=(pl.BlockSpec(memory_space=pl.ANY),) * 3 + (pl.BlockSpec(memory_space=pltpu.VMEM),) * 3,
        scratch_shapes=[
            pltpu.VMEM(turned[0].shape, BF),
            pltpu.VMEM(turned[1].shape, BF),
            pltpu.VMEM((2, rows, 2 * rail), BF),
            pltpu.VMEM((2, rows, rail), F32),
            pltpu.VMEM((2, rows, rail), F32),
            pltpu.VMEM((2, 2 * rows, rail), BF),
            pltpu.VMEM((4, 16, width), F32),
            pltpu.VMEM((6, 16, width), F32),
            pltpu.SemaphoreType.DMA((12, 6, 4)),
            pltpu.SemaphoreType.DMA((2, 2)),
            pltpu.SemaphoreType.DMA((10,)),
            pltpu.SemaphoreType.DMA((2, 6)),
        ],
        compiler_params=pltpu.CompilerParams(collective_id=0, has_side_effects=True, vmem_limit_bytes=60 * 2**20),
        name="gather_weights",
    )(*[v[None] for v in vectors], b_up[None], *matrices, *turned)


class Scatter:
    def __init__(self, place, j, level, bufs, sems):
        self.p, self.j, self.level, self.sems = place, j, level, sems
        self.acc, self.got, self.one, self.two, self.give, self.line, self.low, self.fin = bufs
        p = place
        rail0 = p.c == 0
        self.me = p.y * 2 + p.x
        self.first = jnp.where(rail0, p.y * 2 + 1 - p.x, (1 - p.y) * 2 + p.x)
        self.second = jnp.where(rail0, (1 - p.y) * 2 + p.x, p.y * 2 + 1 - p.x)
        self.diag = (1 - p.y) * 2 + 1 - p.x
        self.to_first = (p.z, self.first * 2 + p.c)
        self.to_second = (p.z, self.second * 2 + p.c)

    def move(self, kind, l, src, dst, to):
        return push(src, dst, self.sems.at[0, kind, self.j, l], self.sems.at[1, kind, self.j, l], to)

    def own(self, l):
        return pltpu.make_async_copy(self.level(l, self.p.c), self.acc.at[l], self.sems.at[0, 0, self.j, l])

    def core(self, l):
        return self.move(1, l, self.level(l, 1 - self.p.c), self.got.at[l], self.p.to_core)

    def step1(self, l, slot):
        block = self.first if slot == 0 else self.diag
        return self.move(2 + slot, l, self.acc.at[l, block], self.one.at[l, slot], self.to_first)

    def step2(self, l):
        return self.move(4, l, self.give.at[l], self.two.at[l], self.to_second)

    def along(self, l, s):
        return self.move(5, s, self.line.at[l], self.low.at[s], self.p.to_z(s))

    def begin(self, l):
        self.core(l).start()
        self.own(l).start()

    def pair(self, l):
        self.own(l).wait()
        self.core(l).wait_recv()
        self.acc[l] = (self.acc[l].astype(F32) + self.got[l].astype(F32)).astype(BF)
        self.step1(l, 0).start()
        self.step1(l, 1).start()

    def side(self, l):
        self.step1(l, 1).wait_recv()
        self.give[l] = (self.acc[l, self.second].astype(F32) + self.one[l, 1].astype(F32)).astype(BF)
        self.step2(l).start()

    def plane_sum(self, l):
        return self.acc[l, self.me].astype(F32) + self.one[l, 0].astype(F32) + self.two[l].astype(F32)

    def plane(self, l):
        self.step1(l, 0).wait_recv()
        self.step2(l).wait_recv()
        self.line[l] = self.plane_sum(l).astype(BF)
        self.along(l, lax.rem(l - self.p.z + 4, 4)).start()

    def last(self):
        z = self.p.z
        self.step1(z, 0).wait_recv()
        self.step2(z).wait_recv()
        self.fin[...] = self.plane_sum(z)
        for s in (1, 2, 3):
            self.along(z, s).wait_recv()
            self.fin[...] += self.low[s].astype(F32)

    def finish(self):
        for l in range(4):
            self.core(l).wait_send()
            self.step1(l, 0).wait_send()
            self.step1(l, 1).wait_send()
            self.step2(l).wait_send()
        for s in (1, 2, 3):
            self.along(self.p.z, s).wait_send()


def level_order(p):
    low = p.z < 2
    zz = jnp.where(low, p.z, 3 - p.z)
    order = [3, 2, 1 - zz, zz]
    return [jnp.where(low, l, 3 - l) for l in order]


PARTS = 1


def scatter_kernel(ga, vec_m, vec_a, u_so_far, d_so_far, two_d, mine_d, two_u, mine_u, *refs):
    out_a, out_v, out_b, out_u, out_d = refs[0:5]
    hold, landed, total, sems, last_sems, vec_sems = refs[5 + 8 * PARTS : 11 + 8 * PARTS]
    line_d, far_d, line_u, far_u, fin_u, tail_sems = refs[11 + 8 * PARTS :]
    p = Place()
    rail = ga.shape[2] // 2
    part = rail // PARTS
    rows = ga.shape[1] // 2

    def lanes_of(i, c):
        return pl.ds(pl.multiple_of(c * rail + i * part, TILE), part)

    jobs = [
        Scatter(
            p, i, lambda l, c, i=i: ga.at[pl.ds(l * 4, 4), :, lanes_of(i, c)], refs[5 + 8 * i : 13 + 8 * i], sems
        )
        for i in range(PARTS)
    ]
    out_u[...] = u_so_far[...]
    out_d[...] = d_so_far[...]
    greet(p)
    order = level_order(p)
    items = [(job, l) for l in order for job in jobs]
    for job, l in items:
        job.begin(l)
    owner = level_of(3)
    sum_d = mine_d[...] + two_d[...].astype(F32)
    line_d[...] = sum_d.astype(BF)

    def tail(kind, s):
        src, dst = (line_d, far_d.at[s - 1]) if kind == 0 else (line_u.at[s - 1], far_u.at[s - 1])
        return push(src, dst, tail_sems.at[0, kind, s], tail_sems.at[1, kind, s], p.to_z(s))

    def sum_u(l):
        return mine_u[l] + two_u[l].astype(F32)

    for s in (1, 2, 3):
        pl.when(lax.rem(p.z + s, 4) == owner)(lambda s=s: tail(0, s).start())
        line_u[s - 1] = sum_u(lax.rem(p.z + s, 4)).astype(BF)
        tail(1, s).start()
    steps = vector_steps(p, lambda: vec_m[...] + vec_a[...], total, hold, landed, vec_sems)
    number = len(items)
    for n in range(number + 2):
        if n < number:
            items[n][0].pair(items[n][1])
        if 1 <= n <= number:
            items[n - 1][0].side(items[n - 1][1])
        if 2 <= n:
            job, l = items[n - 2]
            if n - 2 < number - PARTS:
                job.plane(l)
            else:
                job.last()
        if n < 5:
            steps[n]()
    sends = []
    for i, job in enumerate(jobs):
        lane = lanes_of(i, p.c)
        cp = push(
            job.fin.at[pl.ds(pl.multiple_of((1 - p.c) * rows, 8), rows)], out_a.at[:, lane],
            last_sems.at[0, i], last_sems.at[1, i], p.to_core,
        )
        cp.start()
        sends.append(cp)
        out_a[:, lane] = job.fin[pl.ds(pl.multiple_of(p.c * rows, 8), rows), :]
    fin_u[...] = sum_u(p.z)
    for s in (1, 2, 3):
        tail(1, s).wait()
        fin_u[...] += far_u[s - 1].astype(F32)
    half = fin_u.shape[1]
    lane = pl.ds(pl.multiple_of(owner * 2 * half + p.c * half, TILE), half)
    cp = push(
        fin_u.at[pl.ds(pl.multiple_of((1 - p.c) * rows, 8), rows)], out_u.at[:, lane],
        tail_sems.at[0, 0, 0], tail_sems.at[1, 0, 0], p.to_core,
    )
    cp.start()
    sends.append(cp)
    out_u[:, lane] = fin_u[pl.ds(pl.multiple_of(p.c * rows, 8), rows), :]

    @pl.when(p.z == owner)
    def _():
        out_d[...] = sum_d
        for s in (1, 2, 3):
            tail(0, s).wait_recv()
            out_d[...] += far_d[s - 1].astype(F32)

    for s in (1, 2, 3):
        pl.when(lax.rem(p.z + s, 4) == owner)(lambda s=s: tail(0, s).wait_send())
    device = p.z * 8 + p.f
    width = total.shape[1]
    share = width // 32
    out_v[...] = pltpu.roll(total[...], lax.rem(width - device * share, width), 1)[:, :TILE]
    row = VECTORS + device // 8
    up = jnp.sum(jnp.where(lax.broadcasted_iota(jnp.int32, total.shape, 0) == row, total[...], 0.0), axis=0, keepdims=True)
    up = jnp.broadcast_to(up, (8, width))
    out_b[...] = pltpu.roll(up, lax.rem(width - lax.rem(device, 8) * 4 * share, width), 1)[:, :TILE]
    for job in jobs:
        job.finish()
    for cp in sends:
        cp.wait()


def scatter_all(ga, vec_m, vec_a, u_so_far, d_so_far, two_d, mine_d, two_u, mine_u):
    rows = ga.shape[1] // 2
    cols = ga.shape[2]
    width = vec_m.shape[1]
    block = (2 * rows, cols // 2 // PARTS)
    bufs = [
        pltpu.VMEM((4, 4) + block, BF),
        pltpu.VMEM((4, 4) + block, BF),
        pltpu.VMEM((4, 2) + block, BF),
        pltpu.VMEM((4,) + block, BF),
        pltpu.VMEM((4,) + block, BF),
        pltpu.VMEM((4,) + block, BF),
        pltpu.VMEM((4,) + block, BF),
        pltpu.VMEM(block, F32),
    ]
    vmem, hbm = pl.BlockSpec(memory_space=pltpu.VMEM), pl.BlockSpec(memory_space=pl.ANY)
    return pl.pallas_call(
        scatter_kernel,
        out_shape=(
            jax.ShapeDtypeStruct((rows, cols), F32),
            jax.ShapeDtypeStruct((16, TILE), F32),
            jax.ShapeDtypeStruct((8, TILE), F32),
            jax.ShapeDtypeStruct(u_so_far.shape, F32),
            jax.ShapeDtypeStruct(d_so_far.shape, F32),
        ),
        in_specs=[hbm] + [vmem] * 8,
        out_specs=(vmem,) * 5,
        scratch_shapes=[
            *(bufs * PARTS),
            pltpu.VMEM((4, 16, width), F32),
            pltpu.VMEM((6, 16, width), F32),
            pltpu.VMEM((16, width), F32),
            pltpu.SemaphoreType.DMA((2, 6, PARTS, 4)),
            pltpu.SemaphoreType.DMA((2, PARTS)),
            pltpu.SemaphoreType.DMA((2, 6)),
            pltpu.VMEM(two_d.shape, BF),
            pltpu.VMEM((3,) + two_d.shape, BF),
            pltpu.VMEM((3,) + two_u.shape[1:], BF),
            pltpu.VMEM((3,) + two_u.shape[1:], BF),
            pltpu.VMEM(two_u.shape[1:], F32),
            pltpu.SemaphoreType.DMA((2, 2, 4)),
        ],
        compiler_params=pltpu.CompilerParams(collective_id=1, has_side_effects=True, vmem_limit_bytes=60 * 2**20),
        name="scatter_gradients",
    )(ga, vec_m, vec_a, u_so_far, d_so_far, two_d, mine_d, two_u, mine_u)


def part_kernel(a, u, d, v, b, *outs):
    width = outs[0].shape[1]
    for i in range(4):
        outs[i][...] = a[:, i * width : (i + 1) * width]
    outs[4][...] = u[...]
    outs[5][...] = d[...]
    for i in range(VECTORS):
        outs[6 + i][...] = v[i : i + 1, : outs[6 + i].shape[1]]
    outs[6 + VECTORS][...] = b[0:1, : outs[6 + VECTORS].shape[1]]


def part_all(a, u, d, v, b, share, up_share):
    rows, width = a.shape[0], a.shape[1] // 4
    shapes = [(rows, width)] * 4 + [u.shape, d.shape] + [(1, share)] * VECTORS + [(1, up_share)]
    vmem = pl.BlockSpec(memory_space=pltpu.VMEM)
    outs = pl.pallas_call(
        part_kernel,
        out_shape=tuple(jax.ShapeDtypeStruct(s, F32) for s in shapes),
        in_specs=[vmem] * 5,
        out_specs=(vmem,) * len(shapes),
        name="part_gradients",
    )(a, u, d, v, b)
    return outs[:6], [w.reshape(-1) for w in outs[6:]]


HEAD = 64
EPSILON = 1e-06
LANES = 128
FAR = -1e30
GAIN1, BIAS1, ROUTER, B_QUERY, B_VALUE, B_OUT, GAIN2, BIAS2, B_DOWN, B_UP = range(10)


def dot(a, b):
    return lax.dot_general(a, b, (((1,), (0,)), ((), ())), preferred_element_type=F32)


def dot_nt(a, b):
    return lax.dot_general(a, b, (((1,), (1,)), ((), ())), preferred_element_type=F32)


def dot_tn(a, b):
    return lax.dot_general(a, b, (((0,), (0,)), ((), ())), preferred_element_type=F32)


def up_to(count, step):
    return (count + step - 1) // step * step


def iota(shape, dim):
    return lax.broadcasted_iota(jnp.int32, shape, dim)


def normalized(x):
    centred = x - jnp.mean(x, axis=-1, keepdims=True)
    scale = lax.rsqrt(jnp.mean(centred * centred, axis=-1, keepdims=True) + EPSILON)
    return centred * scale, scale


def norm_back(n, scale, gain, e):
    eg = e * gain
    return scale * (eg - jnp.mean(eg, axis=-1, keepdims=True) - n * jnp.mean(eg * n, axis=-1, keepdims=True))


def column_of(row, size):
    eye = iota((size, size), 0) == iota((size, size), 1)
    return jnp.sum(jnp.where(eye, jnp.broadcast_to(row, (size, size)), 0.0), axis=1, keepdims=True)


def order_of(picked_ref, order_ref):
    cap = picked_ref.shape[1]
    before = jnp.where(iota((cap, cap), 0) < iota((cap, cap), 1), 1.0, 0.0).astype(BF)
    order_ref[...] = dot(picked_ref[...].astype(BF), before)


def pad_rows(selected, segment, picked_ref, marks_ref):
    count, length = selected.shape
    picked_ref[...] = jnp.zeros_like(picked_ref)
    picked_ref[0:count, 0:length] = selected[...].astype(F32)
    if marks_ref is not None:
        marks_ref[...] = jnp.zeros_like(marks_ref)
        marks_ref[0:count, 0:length] = segment[...].astype(F32)


def row_of(ref, r):
    return jnp.sum(jnp.where(iota(ref.shape, 0) == r, ref[...], 0.0), axis=0, keepdims=True)


def to_picked(order, picked, size):
    cap = order.shape[1]
    hit = (order == iota((size, cap), 0).astype(F32)) & (picked > 0.5)
    return jnp.where(hit, 1.0, 0.0)


def from_picked(order, picked, size):
    cap = order.shape[1]
    place = column_of(jnp.where(picked > 0.5, order, -1.0), cap)
    return jnp.where(place == iota((cap, size), 1).astype(F32), 1.0, 0.0).astype(BF)


def sizes(cap):
    half = up_to(cap // 2, HEAD)
    return [(half, up_to(half, LANES)), (cap, cap)]


def loop(count, what):
    lax.fori_loop(0, count, lambda i, c: (what(i), c)[1], 0)


def lanes(i, size):
    return pl.ds(pl.multiple_of(i * size, LANES), size)


def each_size(count, cap, what):
    low = 0
    for rows, keys in sizes(cap):

        @pl.when((count > low) & (count <= rows))
        def _(rows=rows, keys=keys):
            what(rows, keys)

        low = rows


def forbidden(hit, marks, count, size):
    segment_of = dot_nt(jnp.broadcast_to(marks, (8, marks.shape[1])).astype(BF), hit.astype(BF))[0:1]
    segment_of = jnp.where(iota((1, size), 1) < count, segment_of, 99.0)
    column = jnp.sum(hit * marks, axis=1, keepdims=True)
    column = jnp.where(iota((size, 1), 0) < count, column, 99.0)
    return jnp.where(column == segment_of, 0.0, FAR)


def two_heads(pair):
    first = iota(pair.shape, 1) < HEAD
    zero = jnp.zeros_like(pair)
    return jnp.concatenate([jnp.where(first, pair, zero), jnp.where(first, zero, pair)], axis=0)


def one_pair(turned):
    size = turned.shape[1] // 2
    return jnp.concatenate([turned[:HEAD, :size], turned[HEAD:, size:]], axis=0).T


def attend_kernel(r, x, segment, selected, wa, table, *refs):
    outs, kept = refs[-22:-14], refs[-14:-6]
    mid, xc, h, qkv, attn, branch, logs, gates = kept
    xs, picked, marks, order, bar, sems = refs[-6:]
    cap = xs.shape[0]
    span, width = x.shape[1], x.shape[2]
    pad_rows(selected, segment, picked, marks)
    order_of(picked, order)
    sel, place, mark = [ref[r : r + 1, :] for ref in (picked, order, marks)]
    count = jnp.sum(sel).astype(jnp.int32)
    xs[span:cap, :] = jnp.zeros((cap - span, width), BF)
    xs[0:span, :] = x[r]
    mid[...] = x[r].astype(F32)

    def leave(i, size):
        src, dst = kept[i], outs[i].at[r]
        if i not in (0, 6):
            src, dst = src.at[0:size], dst.at[0:size]
        return pltpu.make_async_copy(src, dst, sems.at[i])

    def work(rows, keys):
        hit = to_picked(place, sel, keys)
        block = forbidden(hit, mark, count, keys)
        bar[0:keys, 0:keys] = block
        bar[0:keys, keys : 2 * keys] = block
        x_in = dot(hit[:rows].astype(BF), xs[...])
        xc[0:rows, :] = x_in.astype(BF)
        n, _ = normalized(x_in)
        h_in = (n * table[GAIN1 : GAIN1 + 1, :] + table[BIAS1 : BIAS1 + 1, :]).astype(BF)
        h[0:rows, :] = h_in
        gate = jax.nn.sigmoid(jnp.sum(h_in.astype(F32) * table[ROUTER : ROUTER + 1, :], axis=1, keepdims=True))
        for i, b in enumerate((B_QUERY, None, B_VALUE)):
            part = dot(h_in, wa[:, i * width : (i + 1) * width])
            if b is not None:
                part = part + table[b : b + 1, :]
            qkv[0:rows, i * width : (i + 1) * width] = part.astype(BF)
        if keys > rows:
            qkv[rows:keys, :] = jnp.zeros((keys - rows, 3 * width), BF)
        for i in (1, 2, 3):
            leave(i, keys).start()

        def pair(i, carry):
            lane = i * LANES
            q = qkv[0:keys, pl.ds(pl.multiple_of(lane, LANES), LANES)]
            k = qkv[0:keys, pl.ds(pl.multiple_of(lane + width, LANES), LANES)]
            v = qkv[0:keys, pl.ds(pl.multiple_of(lane + 2 * width, LANES), LANES)]
            s = dot_nt(k, two_heads(q * BF(HEAD**-0.5))) + bar[0:keys, 0 : 2 * keys]
            top = jnp.max(s, axis=0, keepdims=True)
            e = jnp.exp(s - top)
            total = jnp.sum(e, axis=0, keepdims=True)
            out = one_pair(dot_tn(v, e.astype(BF)) * (1.0 / total))
            attn[0:keys, pl.ds(pl.multiple_of(lane, LANES), LANES)] = out.astype(BF)
            logs[i, 0:1, 0 : 2 * keys] = top + jnp.log(total)
            return carry

        lax.fori_loop(0, width // LANES, pair, 0)
        gates[0:rows, :] = jnp.broadcast_to(gate, (rows, LANES))
        for i in (4, 6, 7):
            leave(i, keys).start()
        out = dot(attn[0:rows, :], wa[:, 3 * width :]) + table[B_OUT : B_OUT + 1, :]
        branch[0:rows, :] = out.astype(BF)
        leave(5, keys).start()
        back = from_picked(place, sel, keys)[:span, :rows]
        mid[...] += dot(back, (out * gate).astype(BF))
        for i in range(1, 8):
            leave(i, keys).wait()

    each_size(count, cap, work)
    leave(0, cap).start()
    leave(0, cap).wait()


def attend(r, patches, segment, selected, wa, table, kept=()):
    count, span, width = patches.shape
    cap = up_to(span, LANES)
    shapes = [
        ((span, width), F32), ((cap, width), BF), ((cap, width), BF), ((cap, 3 * width), BF), ((cap, width), BF),
        ((cap, width), BF), ((width // LANES, 1, 2 * cap), F32), ((cap, LANES), F32),
    ]
    vmem, hbm = pl.BlockSpec(memory_space=pltpu.VMEM), pl.BlockSpec(memory_space=pl.ANY)
    return pl.pallas_call(
        partial(attend_kernel, r),
        out_shape=tuple(jax.ShapeDtypeStruct((count,) + s, d) for s, d in shapes),
        in_specs=[vmem] * 5 + [hbm] * len(kept),
        out_specs=(hbm,) * 8,
        scratch_shapes=[pltpu.VMEM(s, d) for s, d in shapes] + [
            pltpu.VMEM((cap, width), BF),
            pltpu.VMEM((8, cap), F32),
            pltpu.VMEM((8, cap), F32),
            pltpu.VMEM((8, cap), F32),
            pltpu.VMEM((cap, 2 * cap), F32),
            pltpu.SemaphoreType.DMA((8,)),
        ],
        input_output_aliases={5 + i: i for i in range(len(kept))},
        cost_estimate=pl.CostEstimate(flops=4 * 10**9, bytes_accessed=10**7, transcendentals=10**6),
        compiler_params=pltpu.CompilerParams(vmem_limit_bytes=60 * 2**20),
        name="attend",
    )(patches, segment, selected, wa, table, *kept)


def attend_back_kernel(
    mixed, gm, segment, selected, wa, table, xc, h, qkv, attn, branch, logs, gates,
    rows_x, rows_mixed, grad_a, sums, grad_x, high, picked, marks, order, bar, ga, dqkv,
):
    cap = high.shape[0]
    span, width = gm.shape[1], gm.shape[2]
    pad_rows(selected, segment, picked, marks)
    order_of(picked, order)
    high[...] = jnp.zeros_like(high)
    grad_a[...] = jnp.zeros_like(grad_a)
    sums[...] = jnp.zeros_like(sums)

    def add(i, v):
        sums[i : i + 1, :] += jnp.sum(v, axis=0, keepdims=True)

    def add_weight(i, j, v):
        at = slice(i * width, j * width)
        grad_a[:, at] = (grad_a[:, at].astype(F32) + v).astype(BF)

    def row(r, carry):
        sel, place, mark = row_of(picked, r), row_of(order, r), row_of(marks, r)
        count = jnp.sum(sel).astype(jnp.int32)
        high[0:span, :] = gm[r]

        @pl.when(count == 0)
        def _():
            grad_x[r] = gm[r]

        def work(rows, keys):
            hit = to_picked(place, sel, keys)
            block = forbidden(hit, mark, count, keys)
            bar[0:keys, 0:keys] = block
            bar[0:keys, keys : 2 * keys] = block
            take = hit[:rows].astype(BF)
            g = dot(take, high[...])
            gate = gates[r, 0:rows, 0:1]
            grad_logit = jnp.sum(g * branch[r, 0:rows, :].astype(F32), axis=1, keepdims=True) * gate * (1.0 - gate)
            gb = g * gate
            add(B_OUT, gb.astype(BF).astype(F32))
            gb = gb.astype(BF)
            add_weight(3, 4, dot_tn(attn[r, 0:rows, :], gb))
            ga[0:rows, :] = dot_nt(gb, wa[:, 3 * width :]).astype(BF)
            if keys > rows:
                ga[rows:keys, :] = jnp.zeros((keys - rows, width), BF)

            def pair(i, carry):
                at = pl.ds(pl.multiple_of(i * LANES, LANES), LANES)
                at_k = pl.ds(pl.multiple_of(i * LANES + width, LANES), LANES)
                at_v = pl.ds(pl.multiple_of(i * LANES + 2 * width, LANES), LANES)
                q2 = two_heads(qkv[r, 0:keys, at] * BF(HEAD**-0.5))
                k = qkv[r, 0:keys, at_k]
                v = qkv[r, 0:keys, at_v]
                g2 = two_heads(ga[0:keys, at])
                p = jnp.exp(dot_nt(k, q2) + bar[0:keys, 0 : 2 * keys] - logs[r, i, 0:1, 0 : 2 * keys])
                dp = dot_nt(v, g2)
                ds = (p * (dp - jnp.sum(p * dp, axis=0, keepdims=True))).astype(BF)
                dqkv[0:keys, at] = one_pair(dot_tn(k, ds) * HEAD**-0.5).astype(BF)
                dqkv[0:keys, at_k] = dot(ds, q2).astype(BF)
                dqkv[0:keys, at_v] = dot(p.astype(BF), g2).astype(BF)
                return carry

            lax.fori_loop(0, width // LANES, pair, 0)
            add(B_QUERY, dqkv[0:rows, 0:width].astype(F32))
            add(B_VALUE, dqkv[0:rows, 2 * width :].astype(F32))
            h_in = h[r, 0:rows, :]
            add(ROUTER, h_in.astype(F32) * grad_logit)
            add_weight(0, 3, dot_tn(h_in, dqkv[0:rows, :]))
            gh = dot_nt(dqkv[0:rows, :], wa[:, : 3 * width]) + grad_logit * table[ROUTER : ROUTER + 1, :]
            n, scale = normalized(xc[r, 0:rows, :].astype(F32))
            add(GAIN1, n * gh)
            add(BIAS1, gh)
            dx = norm_back(n, scale, table[GAIN1 : GAIN1 + 1, :], gh).astype(BF)
            back = from_picked(place, sel, keys)[:span, :rows]
            grad_x[r] = (gm[r].astype(F32) + dot(back, dx)).astype(BF)

        each_size(count, cap, work)
        return carry

    lax.fori_loop(0, gm.shape[0], row, 0)
    for r in range(gm.shape[0]):
        rows_x[:, r, :] = grad_x[r, 0 : rows_x.shape[0], :]
        rows_mixed[:, r, :] = mixed[r, 0 : rows_x.shape[0], :]


def attend_back(mixed, gm, segment, selected, wa, table, kept):
    count, span, width = gm.shape
    cap = up_to(span, LANES)
    rows_out = jax.ShapeDtypeStruct((segment.shape[1], count, width), BF)
    rows_x, rows_mixed, grad_a, sums = pl.pallas_call(
        attend_back_kernel,
        out_shape=(
            rows_out,
            rows_out,
            jax.ShapeDtypeStruct(wa.shape, BF),
            jax.ShapeDtypeStruct((16, width), F32),
        ),
        in_specs=[pl.BlockSpec(memory_space=pltpu.VMEM)] * 13,
        out_specs=(pl.BlockSpec(memory_space=pltpu.VMEM),) * 4,
        scratch_shapes=[
            pltpu.VMEM(gm.shape, BF),
            pltpu.VMEM((cap, width), BF),
            pltpu.VMEM((8, cap), F32),
            pltpu.VMEM((8, cap), F32),
            pltpu.VMEM((8, cap), F32),
            pltpu.VMEM((cap, 2 * cap), F32),
            pltpu.VMEM((cap, width), BF),
            pltpu.VMEM((cap, 3 * width), BF),
        ],
        cost_estimate=pl.CostEstimate(flops=10**10, bytes_accessed=3 * 10**7, transcendentals=10**6),
        compiler_params=pltpu.CompilerParams(vmem_limit_bytes=60 * 2**20),
        name="attend_back",
    )(mixed, gm, segment, selected, wa, table, *kept)
    return rows_x.transpose(1, 0, 2), rows_mixed.transpose(1, 0, 2), grad_a, sums


def gelu_parts(p):
    z = jnp.abs(p)
    e = jnp.exp(-0.5 * p * p)
    t = 1.0 / (1.0 + (0.3275911 * 0.5**0.5) * z)
    poly = ((((1.061405429 * t - 1.453152027) * t + 1.421413741) * t - 0.284496736) * t + 0.254829592) * t
    tail = 0.5 * poly * e
    phi = jnp.where(p > 0, 1.0 - tail, tail)
    return phi, phi + p * (e * 0.3989422804014327)


BLOCK = 592


class ChunkScatter:
    def __init__(self, p, kind, whole, bufs, fin, sems):
        self.p, self.kind, self.whole, self.fin, self.sems = p, kind, whole, fin, sems
        self.got, self.one, self.give, self.two, self.line, self.far = bufs
        rail0 = p.c == 0
        self.me = p.y * 2 + p.x
        self.first = jnp.where(rail0, p.y * 2 + 1 - p.x, (1 - p.y) * 2 + p.x)
        self.second = jnp.where(rail0, (1 - p.y) * 2 + p.x, p.y * 2 + 1 - p.x)
        self.diag = (1 - p.y) * 2 + 1 - p.x
        self.to_first = (p.z, self.first * 2 + p.c)
        self.to_second = (p.z, self.second * 2 + p.c)

    def move(self, stage, j, src, dst, to):
        return push(src, dst, self.sems.at[0, stage, self.kind, j], self.sems.at[1, stage, self.kind, j], to)

    def rail(self, j, c):
        if self.kind == 0:
            return self.whole.at[j, :, c]
        return self.whole.at[j, :, :, :, lanes(c, self.whole.shape[4] // 2)]

    def block(self, j, chip):
        if self.kind == 0:
            return self.whole.at[j, chip, self.p.c]
        return self.whole.at[j, :, chip, :, lanes(self.p.c, self.whole.shape[4] // 2)]

    def core(self, j):
        return self.move(0, j, self.rail(j, 1 - self.p.c), self.got.at[j], self.p.to_core)

    def step1(self, j, slot):
        return self.move(1 + slot, j, self.block(j, self.diag if slot else self.first), self.one.at[j, slot], self.to_first)

    def step2(self, j):
        return self.move(3, j, self.give.at[j], self.two.at[j], self.to_second)

    def begin(self, j):
        self.core(j).start()

    def pair(self, j):
        self.core(j).wait_recv()
        mine = self.rail(j, self.p.c)
        mine[...] = (mine[...].astype(F32) + self.got[j].astype(F32)).astype(BF)
        self.step1(j, 1).start()
        self.step1(j, 0).start()

    def side(self, j):
        self.step1(j, 1).wait_recv()
        self.give[j] = (self.block(j, self.second)[...].astype(F32) + self.one[j, 1].astype(F32)).astype(BF)
        self.step2(j).start()

    def along(self, j, s):
        if self.kind == 0:
            src = self.line.at[j]
        else:
            src = self.line.at[j, s - 1]
        return self.move(3 + s, j, src, self.far.at[j, s - 1], self.p.to_z(s))

    def plane_sum(self, j, l):
        if self.kind == 0:
            return self.block(j, self.me)[...].astype(F32) + self.one[j, 0].astype(F32) + self.two[j].astype(F32)
        own = self.whole[j, l, self.me, :, lanes(self.p.c, self.whole.shape[4] // 2)]
        return own.astype(F32) + self.one[j, 0, l].astype(F32) + self.two[j, l].astype(F32)

    def cross(self, j, owner):
        z = self.p.z
        self.step1(j, 0).wait_recv()
        self.step2(j).wait_recv()
        if self.kind == 0:
            self.line[j] = self.plane_sum(j, 0).astype(BF)
            for s in (1, 2, 3):

                @pl.when(lax.rem(z + s, 4) == owner)
                def _(s=s):
                    self.along(j, s).start()

            return
        for s in (1, 2, 3):
            self.line[j, s - 1] = self.plane_sum(j, lax.rem(z + s, 4)).astype(BF)
            self.along(j, s).start()

    def last(self, j, owner):
        if self.kind == 0:

            @pl.when(self.p.z == owner)
            def _():
                total = self.plane_sum(j, 0)
                for s in (1, 2, 3):
                    self.along(j, s).wait_recv()
                    total = total + self.far[j, s - 1].astype(F32)
                self.fin[...] = total

            return
        total = self.plane_sum(j, self.p.z)
        for s in (1, 2, 3):
            self.along(j, s).wait_recv()
            total = total + self.far[j, s - 1].astype(F32)
        self.fin[j] = total

    def hand_over(self, j, give, mine):
        self.step1(j, 1).wait_recv()
        give[...] = (self.block(j, self.second)[...].astype(F32) + self.one[j, 1].astype(F32)).astype(BF)
        self.step1(j, 0).wait_recv()
        mine[...] = self.block(j, self.me)[...].astype(F32) + self.one[j, 0].astype(F32)

    def finish(self, owner_of, handed):
        def left(j):
            self.core(j).wait_send()
            self.step1(j, 0).wait_send()
            self.step1(j, 1).wait_send()

        left(handed)

        def one(j):
            left(j)
            self.step2(j).wait_send()
            for s in (1, 2, 3):
                if self.kind == 0:

                    @pl.when(lax.rem(self.p.z + s, 4) == owner_of(j))
                    def _(s=s):
                        self.along(j, s).wait_send()

                else:
                    self.along(j, s).wait_send()

        loop(handed, one)


def level_of(i):
    return jnp.where(i == 0, 0, jnp.where(i == 1, 3, i - 1))


def mlp_kernel(remote, mid, g, wu, wd, table, *refs):
    if remote:
        parts_d, refs = (wd,) + refs[:3], refs[3:]
    mlp_body(remote, mid, g, wu, parts_d if remote else (wd,), table, *refs)


def mlp_body(remote, mid, g, wu, parts_d, table, mixed, gm, sums, out_u, out_d, *refs):
    if remote:
        handed, refs = refs[:4], refs[4:]
    u, acc, act, gp, hold_u, hold_d, weight_sems = refs[:7]
    count, span, width = mid.shape
    tokens = count * span
    chunk = width
    chunks = 4 if remote else parts_d[0].shape[0] // chunk
    blocks = tokens // BLOCK
    per = span // BLOCK
    if remote:
        grad_d, grad_u, fin_u = refs[7:10]
        bufs_d, bufs_u = refs[10:16], refs[16:22]
        sems, last_sems, part_sems = refs[22:]
        p = Place()
        greet(p)
        down = ChunkScatter(p, 0, grad_d, bufs_d, out_d, sems)
        up = ChunkScatter(p, 1, grad_u, bufs_u, fin_u, sems)
        rail = width // 2
        rows = out_u.shape[0]

    def row(i):
        return table[i : i + 1, :]

    def each_block(what):
        loop(blocks, lambda b: what(b, pl.ds(pl.multiple_of(b * BLOCK, 16), BLOCK)))

    def mid_of(b):
        return mid[b // per, pl.ds(pl.multiple_of(lax.rem(b, per) * BLOCK, 16), BLOCK), :]

    def load(i):
        j, slot = level_of(i), lax.rem(i, 2)
        up_part = pltpu.make_async_copy(wu.at[:, lanes(j, chunk)], hold_u.at[slot], weight_sems.at[0, slot])
        if remote:
            return (up_part,)
        rows_d = parts_d[0].at[pl.ds(pl.multiple_of(j * chunk, 16), chunk)]
        return up_part, pltpu.make_async_copy(rows_d, hold_d.at[slot], weight_sems.at[1, slot])

    def weights(i):
        if remote:
            return hold_u[lax.rem(i, 2)], hold_d[i].reshape(chunk, width)
        return hold_u[lax.rem(i, 2)], hold_d[lax.rem(i, 2)]

    for cp in load(0):
        cp.start()
    if remote:
        chips = (p.y * 2 + p.x, p.y * 2 + 1 - p.x, (1 - p.y) * 2 + p.x, (1 - p.y) * 2 + 1 - p.x)

        def keep(i, n):
            return pltpu.make_async_copy(parts_d[n].at[level_of(i)], hold_d.at[i, chips[n], p.c], part_sems.at[2, i, n])

        def share(i, n):
            return push(
                parts_d[n].at[level_of(i)], hold_d.at[i, chips[n], p.c], part_sems.at[0, i, n], part_sems.at[1, i, n], p.to_core
            )

        for i in range(chunks):
            for n in range(4):
                keep(i, n).start()
                share(i, n).start()
    sums[...] = jnp.zeros_like(sums)
    acc[...] = jnp.zeros_like(acc)
    def start(b, at):
        n, _ = normalized(mid_of(b))
        u[at, :] = (n * row(GAIN2) + row(BIAS2)).astype(BF)
        sums[B_DOWN : B_DOWN + 1, :] += jnp.sum(g[at, :].astype(F32), axis=0, keepdims=True)

    each_block(start)

    def send_rail(i):
        lane = pl.ds(pl.multiple_of(level_of(i) * chunk + p.c * rail, TILE), rail)
        return push(
            fin_u.at[i, pl.ds(pl.multiple_of((1 - p.c) * rows, 8), rows)], out_u.at[:, lane],
            last_sems.at[0, i], last_sems.at[1, i], p.to_core,
        )

    def own_rail(i):
        up.last(i, 0)
        send_rail(i).start()
        lane = pl.ds(pl.multiple_of(level_of(i) * chunk + p.c * rail, TILE), rail)
        out_u[:, lane] = fin_u[i, pl.ds(pl.multiple_of(p.c * rows, 8), rows), :]

    def from_chunk(i, back, what):
        if remote:
            pl.when(i >= back)(lambda: what(i - back))

    def one_chunk(i):
        j, slot = level_of(i), lax.rem(i, 2)
        for cp in load(i):
            cp.wait()
        if remote:
            for n in range(4):
                keep(i, n).wait()
                share(i, n).wait_recv()

        @pl.when(i + 1 < chunks)
        def _():
            for cp in load(i + 1):
                cp.start()

        def hidden(b, at):
            in_u, in_d = weights(i)
            pre = dot(u[at, :], in_u) + table[pl.ds(B_UP + j, 1), :]
            phi, slope = gelu_parts(pre)
            act[at, :] = (pre * phi).astype(BF)
            grad_pre = (slope * dot_nt(g[at, :], in_d)).astype(BF)
            gp[at, :] = grad_pre
            sums[pl.ds(B_UP + j, 1), :] += jnp.sum(grad_pre.astype(F32), axis=0, keepdims=True)

        each_block(hidden)
        from_chunk(i, 1, lambda k: down.cross(k, level_of(k)))
        from_chunk(i, 1, lambda k: up.side(k))
        from_chunk(i, 2, own_rail)
        part = dot_tn(act[...], g[...]).astype(BF)
        if remote:
            grad_d[i] = part.reshape(grad_d.shape[1:])
            down.begin(i)
        else:
            out_d[pl.ds(pl.multiple_of(j * chunk, 16), chunk), :] = part
        part = dot_tn(u[...], gp[...]).astype(BF)
        if remote:
            grad_u[i] = part.reshape(grad_u.shape[1:])
            up.begin(i)
            down.pair(i)
        else:
            out_u[:, lanes(j, chunk)] = part
        from_chunk(i, 1, lambda k: up.cross(k, 0))

        def total(b, at):
            in_u, in_d = weights(i)
            acc[0, at, :] += dot(act[at, :], in_d)
            acc[1, at, :] += dot_nt(gp[at, :], in_u)

        for b in range(blocks):
            total(b, pl.ds(b * BLOCK, BLOCK))
            if remote and b == 0:
                up.pair(i)
        if remote:
            pl.when(i + 1 < chunks)(lambda: down.side(i))
        from_chunk(i, 1, lambda k: down.last(k, level_of(k)))

    loop(chunks, one_chunk)

    def end(b, at):
        m = mid_of(b)
        out = (m + acc[0, at, :] + row(B_DOWN)).astype(BF)
        mixed[b] = out
        n, scale = normalized(m)
        e = acc[1, at, :]
        sums[GAIN2 : GAIN2 + 1, :] += jnp.sum(n * e, axis=0, keepdims=True)
        sums[BIAS2 : BIAS2 + 1, :] += jnp.sum(e, axis=0, keepdims=True)
        gm[b] = (g[at, :].astype(F32) + norm_back(n, scale, row(GAIN2), e)).astype(BF)

    for b in range(blocks):
        end(b, pl.ds(b * BLOCK, BLOCK))
        if remote and b == 0:
            own_rail(chunks - 2)
    if remote:
        down.hand_over(chunks - 1, *handed[:2])
        up.hand_over(chunks - 1, *handed[2:])
        for i in range(chunks - 1):
            send_rail(i).wait()
        up.finish(level_of, chunks - 1)
        down.finish(level_of, chunks - 1)
        for i in range(chunks):
            for n in range(4):
                share(i, n).wait_send()


def mlp(remote, mid, cot, wu, parts_d, table):
    count, span, width = mid.shape
    tokens = count * span
    if remote:
        rows, depth = wu.shape[0] // 32, parts_d[0].shape[1]
        outs = [jax.ShapeDtypeStruct((rows, wu.shape[1]), F32), jax.ShapeDtypeStruct((depth, width), F32)]
        half = width // 2
        for shape in ((depth, width), (4, 2 * rows, half)):
            outs += [jax.ShapeDtypeStruct(shape, BF), jax.ShapeDtypeStruct(shape, F32)]
        extra = [
            pltpu.VMEM((4, 4, 2, depth, width), BF),
            pltpu.VMEM((4, 4, 4, 2 * rows, width), BF),
            pltpu.VMEM((4, 2 * rows, half), F32),
        ]
        extra += [pltpu.VMEM((4, 4, depth, width), BF), pltpu.VMEM((4, 2, depth, width), BF)]
        extra += [pltpu.VMEM((4, depth, width), BF)] * 3 + [pltpu.VMEM((4, 3, depth, width), BF)]
        extra += [pltpu.VMEM((4, 4, 4, 2 * rows, half), BF), pltpu.VMEM((4, 2, 4, 2 * rows, half), BF)]
        extra += [pltpu.VMEM((4, 4, 2 * rows, half), BF)] * 2 + [pltpu.VMEM((4, 3, 2 * rows, half), BF)] * 2
        extra += [pltpu.SemaphoreType.DMA((2, 7, 2, 4)), pltpu.SemaphoreType.DMA((2, 4)), pltpu.SemaphoreType.DMA((3, 4, 4))]
        hold_d = pltpu.VMEM((4, 4, 2, depth, width), BF)
        params = dict(collective_id=2, has_side_effects=True)
    else:
        outs = [jax.ShapeDtypeStruct(wu.shape, BF), jax.ShapeDtypeStruct(parts_d[0].shape, BF)]
        extra, params = [], {}
        hold_d = pltpu.VMEM((2, width, width), BF)
    vmem = pl.BlockSpec(memory_space=pltpu.VMEM)
    hbm = pl.BlockSpec(memory_space=pl.ANY)
    return pl.pallas_call(
        partial(mlp_kernel, remote),
        out_shape=(
            jax.ShapeDtypeStruct(mid.shape, BF),
            jax.ShapeDtypeStruct(mid.shape, BF),
            jax.ShapeDtypeStruct((16, width), F32),
            *outs,
        ),
        in_specs=[vmem, vmem, hbm, hbm, vmem] + [hbm] * (len(parts_d) - 1),
        out_specs=(vmem,) * (3 + len(outs)),
        scratch_shapes=[
            pltpu.VMEM((tokens, width), BF),
            pltpu.VMEM((2, tokens, width), F32),
            pltpu.VMEM((tokens, width), BF),
            pltpu.VMEM((tokens, width), BF),
            pltpu.VMEM((2, width, width), BF),
            hold_d,
            pltpu.SemaphoreType.DMA((2, 2)),
            *extra,
        ],
        compiler_params=pltpu.CompilerParams(vmem_limit_bytes=62 * 2**20, **params),
        name="mlp",
    )(mid, cot.reshape(tokens, width), wu, parts_d[0], table, *parts_d[1:])


def local(
    small, patches, segment_ids, selected, cotangent, ln1_gain, ln1_bias, w_router, w_query, b_query,
    w_key, w_value, b_value, w_out, b_out, ln2_gain, ln2_bias, w_up, b_up, w_down, b_down,
):
    length, width = patches.shape[1:]
    span = up_to(length, 16)
    vectors = (ln1_gain, ln1_bias, w_router, b_query, b_value, b_out, ln2_gain, ln2_bias, b_down)
    matrices = (w_query, w_key, w_value, w_out, w_up, w_down)
    if small:
        attn_w, up_w, down_z, table, x, cot = gather_all(vectors, b_up, matrices, (patches, cotangent), span)
        attn_w = attn_w.reshape(-1, attn_w.shape[2])
        up_w = up_w.reshape(-1, up_w.shape[2])
        down_x = lax.ppermute(down_z, "fsdp", [(i, i ^ 2) for i in range(8)])
        down_y = lax.ppermute(down_z, "fsdp", [(i, i ^ 4) for i in range(8)])
    else:
        whole = [lax.all_gather(v, AXES, axis=0, tiled=True) for v in vectors + (b_up,)]
        table = jnp.concatenate(
            [jnp.stack(whole[:VECTORS]), whole[VECTORS].reshape(4, width), jnp.zeros((3, width), BF)]
        ).astype(F32)
        attn_w = jnp.concatenate([lax.all_gather(w, AXES, axis=0, tiled=True) for w in matrices[:4]], axis=1)
        up_w = lax.all_gather(w_up, AXES, axis=0, tiled=True)
        down_w = lax.all_gather(w_down, AXES, axis=0, tiled=True)
        x, cot = [jnp.pad(v, ((0, 0), (0, span - length), (0, 0))) for v in (patches, cotangent)]
    kept = ()
    for r in range(x.shape[0]):
        kept = attend(r, x, segment_ids, selected, attn_w, table, kept)
        if small and r == 0:
            down_x, down_y, _ = lax.optimization_barrier((down_x, down_y, kept[6]))
            turn = jnp.where(lax.rem(lax.axis_index("fsdp"), 2) == 0, down_y, down_x)
            down_d = lax.ppermute(turn, "fsdp", [(i, i ^ (4 if i % 2 else 2)) for i in range(8)])
    mid, *kept = kept
    down_parts = (down_z, down_x, down_y, down_d) if small else (down_w,)
    mixed, grad_mid, sums_mlp, grad_u, grad_d, *handed = mlp(small, mid, cot, up_w, down_parts, table)
    if small:
        give_d, mine_d, give_u, mine_u = handed
        second = [(i, i ^ (2 if i % 2 else 4)) for i in range(8)]
        two_d, two_u = lax.ppermute(give_d, "fsdp", second), lax.ppermute(give_u, "fsdp", second)
    grad_x, mixed, grad_a, sums_attn = attend_back(mixed, grad_mid, segment_ids, selected, attn_w, table, kept)
    if small:
        own_a, own_v, own_b, grad_u, grad_d = scatter_all(
            grad_a.reshape(16, -1, grad_a.shape[1]), sums_mlp, sums_attn, grad_u, grad_d, two_d, mine_d, two_u, mine_u
        )
        own_m, (*own, own_up_b) = part_all(own_a, grad_u, grad_d, own_v, own_b, ln1_gain.shape[0], b_up.shape[0])
    else:
        sums = sums_mlp + sums_attn
        own = [lax.psum_scatter(sums[i], AXES, scatter_dimension=0, tiled=True) for i in range(VECTORS)]
        own_up_b = lax.psum_scatter(
            sums[VECTORS : VECTORS + 4].reshape(-1), AXES, scatter_dimension=0, tiled=True
        )
        own_m = [
            lax.psum_scatter(g.astype(F32), AXES, scatter_dimension=0, tiled=True)
            for g in jnp.split(grad_a, 4, axis=1) + [grad_u, grad_d]
        ]
    return (
        mixed, grad_x, own[0], own[1], own[2], own_m[0], own[3], own_m[1], own_m[2], own[4],
        own_m[3], own[5], own[6], own[7], own_m[4], own_up_b, own_m[5], own[8],
    )


def solution(mesh):
    flat, rows2, rows3 = P(AXES), P(AXES, None), P(AXES, None, None)
    vec, mat = flat, rows2
    small = mesh.shape["dp"] == 4 and mesh.shape["fsdp"] == 8
    return jax.shard_map(
        partial(local, small),
        mesh=mesh,
        in_specs=(
            rows3, rows2, rows2, rows3, vec, vec, vec, mat, vec, mat, mat, vec, mat, vec, vec, vec, mat, vec, mat, vec,
        ),
        out_specs=(
            rows3, rows3, vec, vec, vec, mat, vec, mat, mat, vec, mat, vec, vec, vec, mat, vec, mat, vec,
        ),
        check_vma=False,
    )
```

```python
from functools import partial
import math

import jax
import jax.numpy as jnp
from jax import lax
from jax.experimental import pallas as pl
from jax.experimental.pallas import tpu as pltpu
from jax.sharding import PartitionSpec as P

AXES = ("dp", "fsdp")
MESH = pl.DeviceIdType.MESH
BF = jnp.bfloat16
F32 = jnp.float32


class Place:
    def __init__(self):
        self.z = lax.axis_index("dp")
        self.f = lax.axis_index("fsdp")
        self.c = lax.rem(self.f, 2)
        self.x = lax.rem(self.f // 2, 2)
        self.y = self.f // 4
        self.chip = self.z * 4 + self.y * 2 + self.x
        self.chip_x = self.z * 4 + self.y * 2 + (1 - self.x)
        self.chip_y = self.z * 4 + (1 - self.y) * 2 + self.x
        self.to_core = (self.z, self.y * 4 + self.x * 2 + (1 - self.c))
        self.to_x = (self.z, self.y * 4 + (1 - self.x) * 2 + self.c)
        self.to_y = (self.z, (1 - self.y) * 4 + self.x * 2 + self.c)

    def to_z(self, step):
        return (lax.rem(self.z + step + 4, 4), self.f)


def greet(place):
    bar = pltpu.get_barrier_semaphore()
    others = [place.to_core, place.to_x, place.to_y] + [place.to_z(s) for s in (1, 2, 3)]
    for other in others:
        pl.semaphore_signal(bar, inc=1, device_id=other, device_id_type=MESH)
    pl.semaphore_wait(bar, len(others))


def push(src, dst, send, recv, to):
    return pltpu.make_async_remote_copy(
        src_ref=src, dst_ref=dst, send_sem=send, recv_sem=recv, device_id=to, device_id_type=MESH
    )


class Gather:
    def __init__(self, place, j, block, level, plane_first, sems):
        self.p, self.j, self.block, self.level, self.sems = place, j, block, level, sems
        self.plane_first = plane_first

    def copy(self, kind, i, ref, to):
        return push(ref, ref, self.sems.at[2 * kind, self.j, i], self.sems.at[2 * kind + 1, self.j, i], to)

    def piece(self, l):
        if self.plane_first:
            return self.level(l, self.p.c)
        return self.block(l * 4 + self.p.y * 2 + self.p.x)

    def up(self, k):
        return self.copy(0, k, self.piece(lax.rem(self.p.z - k + 4, 4)), self.p.to_z(1))

    def up_in(self, k):
        return self.copy(0, k, self.piece(lax.rem(self.p.z - k + 3, 4)), self.p.to_z(1))

    def down(self, k):
        return self.copy(1, k, self.piece(lax.rem(self.p.z + k, 4)), self.p.to_z(3))

    def down_in(self, k):
        return self.copy(1, k, self.piece(lax.rem(self.p.z + k + 1, 4)), self.p.to_z(3))

    def xs(self, l):
        return self.copy(2, l, self.block(l * 4 + self.p.y * 2 + self.p.x), self.p.to_x)

    def ys(self, l):
        return self.copy(3, l, self.block(l * 4 + self.p.y * 2 + self.p.x), self.p.to_y)

    def side_in(self, l, y_side):
        p = self.p
        chip = l * 4 + (p.y + y_side - 2 * p.y * y_side) * 2 + (p.x + (1 - y_side) - 2 * p.x * (1 - y_side))
        return self.copy(2 + y_side, l, self.block(chip), p.to_x)

    def forward(self, l):
        p = self.p
        chip = l * 4 + jnp.where(p.c == 0, (1 - p.y) * 2 + p.x, p.y * 2 + 1 - p.x)
        to = (p.z, jnp.where(p.c == 0, p.y * 4 + (1 - p.x) * 2 + p.c, (1 - p.y) * 4 + p.x * 2 + p.c))
        return self.copy(4, l, self.block(chip), to)

    def forward_in(self, l):
        return self.copy(4, l, self.block(l * 4 + (1 - self.p.y) * 2 + 1 - self.p.x), self.p.to_x)

    def cs(self, l):
        return self.copy(5, l, self.level(l, self.p.c), self.p.to_core)

    def cs_in(self, l):
        return self.copy(5, l, self.level(l, 1 - self.p.c), self.p.to_core)

    def sides(self, l):
        self.xs(l).start()
        self.ys(l).start()

    def ends(self, k):
        z = self.p.z

        @pl.when((z >= k) & (z < 3))
        def _():
            self.up(k).start()

        @pl.when((z + k <= 3) & (z > 0))
        def _():
            self.down(k).start()

    def begin(self):
        if not self.plane_first:
            self.ends(0)
        self.sides(self.p.z)

    def along_z(self, k, onward=True):
        z = self.p.z

        @pl.when(z > k)
        def _():
            self.up_in(k).wait_recv()

        @pl.when(z + k < 3)
        def _():
            self.down_in(k).wait_recv()

        if k < 2:
            self.ends(k + 1)
        if onward:
            self.each(k + 1, (lambda l: self.cs(l).start()) if self.plane_first else self.sides)

    def each(self, k, what):
        z = self.p.z
        if k == 0:
            what(z)
            return

        @pl.when(z >= k)
        def _():
            what(z - k)

        @pl.when(z + k <= 3)
        def _():
            what(z + k)

    def turn(self, l):
        self.side_in(l, 1 - self.p.c).wait_recv()
        self.forward(l).start()
        self.side_in(l, self.p.c).wait_recv()

    def across(self, l):
        self.forward_in(l).wait_recv()
        if self.plane_first:
            self.ends(0)
        self.cs(l).start()

    def finish(self):
        z = self.p.z
        self.finish_z()
        for l in range(4):
            if self.plane_first:
                continue
            self.xs(l).wait_send()
            self.ys(l).wait_send()
            self.forward(l).wait_send()
        if self.plane_first:
            self.xs(z).wait_send()
            self.ys(z).wait_send()
            self.forward(z).wait_send()
        for l in range(4):
            self.cs(l).wait_send()
            self.cs_in(l).wait_recv()

    def finish_z(self):
        z = self.p.z
        for k in range(3):

            @pl.when((z >= k) & (z < 3))
            def _():
                self.up(k).wait_send()

            @pl.when((z + k <= 3) & (z > 0))
            def _():
                self.down(k).wait_send()


VECTORS = 9
TILE = 128


def vector_steps(p, values, out_ref, hold, landed, sems):
    send, recv = sems.at[0], sems.at[1]
    state = {}

    def begin():
        state["value"] = values()
        hold[0] = state["value"]
        push(hold.at[0], landed.at[0], send.at[0], recv.at[0], p.to_core).start()

    def then(i, to, after):
        def step():
            push(hold.at[i], landed.at[i], send.at[i], recv.at[i], to).wait()
            hold[i + 1] = hold[i] + landed[i]
            after()
        return step

    def next_side():
        push(hold.at[1], landed.at[1], send.at[1], recv.at[1], p.to_x).start()

    def next_other():
        push(hold.at[2], landed.at[2], send.at[2], recv.at[2], p.to_y).start()

    def line(s):
        return push(hold.at[3], landed.at[2 + s], send.at[2 + s], recv.at[2 + s], p.to_z(s))

    def next_line():
        for s in (1, 2, 3):
            line(s).start()

    def last():
        for s in (1, 2, 3):
            line(s).wait()
        out_ref[...] = hold[3] + landed[3] + landed[4] + landed[5]

    return [begin, then(0, p.to_core, next_side), then(1, p.to_x, next_other), then(2, p.to_y, next_line), last]


def cut(cols, share):
    first = int(round(cols * (1 - share) / TILE)) * TILE
    return first


import os
PLANE_SHARE = 0.0


def gather_kernel(*refs):
    vectors, b_up = refs[:VECTORS], refs[VECTORS]
    wq, wk, wv, wo, wu, wd = refs[VECTORS + 1 : VECTORS + 7]
    rows_in = refs[VECTORS + 7 : VECTORS + 9]
    out_a, out_u, out_d, out_v = refs[VECTORS + 9 : VECTORS + 13]
    rows_out = refs[VECTORS + 13 : VECTORS + 15]
    rows_held = refs[VECTORS + 15 : VECTORS + 17]
    held, give, take, packed, hold, landed, sems, pair_sems, own_sems, vec_sems = refs[VECTORS + 17 :]
    p = Place()
    width = wq.shape[1]
    rail = 2 * width
    rows = wq.shape[0]
    lower = p.c == 0
    loads = [pltpu.make_async_copy(w, held.at[0, :, pl.ds(i * width, width)], own_sems.at[3 + i]) for i, w in enumerate((wq, wk, wv, wo))]
    loads.append(pltpu.make_async_copy(wu, held.at[1], own_sems.at[7]))
    own_d = pltpu.make_async_copy(wd, out_d.at[p.z], own_sems.at[2])
    moves = [pltpu.make_async_copy(a, b, own_sems.at[8 + i]) for i, (a, b) in enumerate(zip(rows_in, rows_held))]
    for cp in loads + moves:
        cp.start()
    own_d.start()
    greet(p)
    for cp in loads:
        cp.wait()
    mine = pl.ds(pl.multiple_of(p.c * rail, TILE), rail)
    other = pl.ds(pl.multiple_of((1 - p.c) * rail, TILE), rail)
    pair = []
    for i in range(2):
        give[i] = held[i, :, other].astype(F32)
        pair.append(push(give.at[i], take.at[i], pair_sems.at[0, i], pair_sems.at[1, i], p.to_core))
        pair[i].start()
    jobs = []

    def add_jobs(out, rail_cols, columns_by_rail):
        first = cut(rail_cols, PLANE_SHARE)
        for start, size, plane in ((0, first, False), (first, rail_cols - first, True)):
            if size == 0:
                continue
            if columns_by_rail:
                def lanes(c, start=start, size=size):
                    return pl.ds(pl.multiple_of(c * rail_cols + start, TILE), size)
                block = lambda chip, out=out, lanes=lanes: out.at[chip, :, lanes(p.c)]
                level = lambda l, c, out=out, lanes=lanes: out.at[pl.ds(l * 4, 4), :, lanes(c)]
            else:
                lane = pl.ds(start, size)
                block = lambda chip, out=out, lane=lane: out.at[chip, p.c, :, lane]
                level = lambda l, c, out=out, lane=lane: out.at[pl.ds(l * 4, 4), c, :, lane]
            jobs.append(Gather(p, len(jobs), block, level, plane, sems))

    add_jobs(out_a, rail, True)
    add_jobs(out_u, rail, True)
    per = len(jobs) // 2
    for i, out in enumerate((out_a, out_u)):
        pair[i].wait()
        own = held[i, :, mine].astype(F32)
        got = take[i]
        packed[i] = jnp.concatenate([jnp.where(lower, own, got), jnp.where(lower, got, own)], axis=0).astype(BF)
        cp = pltpu.make_async_copy(packed.at[i], out.at[p.chip, :, mine], own_sems.at[i])
        cp.start()
        cp.wait()
        for job in jobs[i * per : (i + 1) * per][::-1]:
            job.begin()
    rows_d = Gather(p, len(jobs), lambda chip: out_d.at[chip // 4], None, False, sems)
    own_d.wait()
    rows_d.ends(0)
    device = p.z * 8 + p.f

    def spread(ref):
        count = ref.shape[1]
        total = count * 32
        lane = lax.broadcasted_iota(jnp.int32, (count, total), 1)
        row = lax.broadcasted_iota(jnp.int32, (count, total), 0)
        place = (lane == row + device * count).astype(BF)
        return jnp.dot(ref[...], place, preferred_element_type=F32)

    def values():
        rows_of = [spread(v) for v in vectors]
        up = spread(b_up)
        rows_of += [up[:, i * width : (i + 1) * width] for i in range(4)]
        rows_of.append(jnp.zeros((3, width), F32))
        return jnp.concatenate(rows_of, axis=0)

    steps = vector_steps(p, values, out_v, hold, landed, vec_sems)
    steps[0]()
    plane = [job for job in jobs if job.plane_first]
    line = [job for job in jobs if not job.plane_first]
    for job in plane:
        job.turn(p.z)
    length, count = rows_in[0].shape[0], rows_in[0].shape[1]
    span = rows_out[0].shape[1]
    low = length // 16 * 16

    def lay_out(i, r):
        if r == 0:
            moves[i].wait()
        rows_out[i][r, low:span, :] = jnp.zeros((span - low, width), BF)
        rows_out[i][r, 0:length, :] = rows_held[i][:, r, :]

    work = [(i, r) for i in range(2) for r in range(count)]
    lay_out(*work[0])
    steps[1]()
    for job in plane:
        job.across(p.z)
    for r in range(1, count):
        lay_out(*work[r])
    for k in range(4):
        if k < 3:
            for job in line + plane:
                job.along_z(k)
            rows_d.along_z(k, False)
            steps[k + 2]()
        for job in line:
            job.each(k, job.turn)
        if k == 0:
            for item in work[count:]:
                lay_out(*item)
        if k > 0:
            for job in line:
                job.each(k - 1, job.across)
    for job in line:
        job.each(3, job.across)
    rows_d.finish_z()
    for job in jobs:
        job.finish()


def gather_all(vectors, b_up, matrices, rows_in, span):
    wq, wd = matrices[0], matrices[5]
    rows, width = wq.shape
    rail = 2 * width
    depth = wd.shape[0]
    turned = [v.transpose(1, 0, 2) for v in rows_in]
    count = rows_in[0].shape[0]
    return pl.pallas_call(
        gather_kernel,
        out_shape=(
            jax.ShapeDtypeStruct((16, 2 * rows, 4 * width), BF),
            jax.ShapeDtypeStruct((16, 2 * rows, 4 * width), BF),
            jax.ShapeDtypeStruct((4, depth, width), BF),
            jax.ShapeDtypeStruct((16, width), F32),
            jax.ShapeDtypeStruct((count, span, width), BF),
            jax.ShapeDtypeStruct((count, span, width), BF),
        ),
        in_specs=[pl.BlockSpec(memory_space=pltpu.VMEM)] * (VECTORS + 1) + [pl.BlockSpec(memory_space=pl.ANY)] * 8,
        out_specs=(pl.BlockSpec(memory_space=pl.ANY),) * 3 + (pl.BlockSpec(memory_space=pltpu.VMEM),) * 3,
        scratch_shapes=[
            pltpu.VMEM(turned[0].shape, BF),
            pltpu.VMEM(turned[1].shape, BF),
            pltpu.VMEM((2, rows, 2 * rail), BF),
            pltpu.VMEM((2, rows, rail), F32),
            pltpu.VMEM((2, rows, rail), F32),
            pltpu.VMEM((2, 2 * rows, rail), BF),
            pltpu.VMEM((4, 16, width), F32),
            pltpu.VMEM((6, 16, width), F32),
            pltpu.SemaphoreType.DMA((12, 6, 4)),
            pltpu.SemaphoreType.DMA((2, 2)),
            pltpu.SemaphoreType.DMA((10,)),
            pltpu.SemaphoreType.DMA((2, 6)),
        ],
        compiler_params=pltpu.CompilerParams(collective_id=0, has_side_effects=True, vmem_limit_bytes=60 * 2**20),
        name="gather_weights",
    )(*[v[None] for v in vectors], b_up[None], *matrices, *turned)


class Scatter:
    def __init__(self, place, j, level, bufs, sems):
        self.p, self.j, self.level, self.sems = place, j, level, sems
        self.acc, self.got, self.one, self.two, self.give, self.line, self.low, self.fin = bufs
        p = place
        rail0 = p.c == 0
        self.me = p.y * 2 + p.x
        self.first = jnp.where(rail0, p.y * 2 + 1 - p.x, (1 - p.y) * 2 + p.x)
        self.second = jnp.where(rail0, (1 - p.y) * 2 + p.x, p.y * 2 + 1 - p.x)
        self.diag = (1 - p.y) * 2 + 1 - p.x
        self.to_first = (p.z, self.first * 2 + p.c)
        self.to_second = (p.z, self.second * 2 + p.c)

    def move(self, kind, l, src, dst, to):
        return push(src, dst, self.sems.at[0, kind, self.j, l], self.sems.at[1, kind, self.j, l], to)

    def own(self, l):
        return pltpu.make_async_copy(self.level(l, self.p.c), self.acc.at[l], self.sems.at[0, 0, self.j, l])

    def core(self, l):
        return self.move(1, l, self.level(l, 1 - self.p.c), self.got.at[l], self.p.to_core)

    def step1(self, l, slot):
        block = self.first if slot == 0 else self.diag
        return self.move(2 + slot, l, self.acc.at[l, block], self.one.at[l, slot], self.to_first)

    def step2(self, l):
        return self.move(4, l, self.give.at[l], self.two.at[l], self.to_second)

    def along(self, l, s):
        return self.move(5, s, self.line.at[l], self.low.at[s], self.p.to_z(s))

    def begin(self, l):
        self.core(l).start()
        self.own(l).start()

    def pair(self, l):
        self.own(l).wait()
        self.core(l).wait_recv()
        self.acc[l] = (self.acc[l].astype(F32) + self.got[l].astype(F32)).astype(BF)
        self.step1(l, 0).start()
        self.step1(l, 1).start()

    def side(self, l):
        self.step1(l, 1).wait_recv()
        self.give[l] = (self.acc[l, self.second].astype(F32) + self.one[l, 1].astype(F32)).astype(BF)
        self.step2(l).start()

    def plane_sum(self, l):
        return self.acc[l, self.me].astype(F32) + self.one[l, 0].astype(F32) + self.two[l].astype(F32)

    def plane(self, l):
        self.step1(l, 0).wait_recv()
        self.step2(l).wait_recv()
        self.line[l] = self.plane_sum(l).astype(BF)
        self.along(l, lax.rem(l - self.p.z + 4, 4)).start()

    def last(self):
        z = self.p.z
        self.step1(z, 0).wait_recv()
        self.step2(z).wait_recv()
        self.fin[...] = self.plane_sum(z)
        for s in (1, 2, 3):
            self.along(z, s).wait_recv()
            self.fin[...] += self.low[s].astype(F32)

    def finish(self):
        for l in range(4):
            self.core(l).wait_send()
            self.step1(l, 0).wait_send()
            self.step1(l, 1).wait_send()
            self.step2(l).wait_send()
        for s in (1, 2, 3):
            self.along(self.p.z, s).wait_send()


def level_order(p):
    low = p.z < 2
    zz = jnp.where(low, p.z, 3 - p.z)
    order = [3, 2, 1 - zz, zz]
    return [jnp.where(low, l, 3 - l) for l in order]


PARTS = 1


def scatter_kernel(ga, vec_m, vec_a, u_so_far, d_so_far, two_d, mine_d, two_u, mine_u, *refs):
    out_a, out_v, out_b, out_u, out_d = refs[0:5]
    hold, landed, total, sems, last_sems, vec_sems = refs[5 + 8 * PARTS : 11 + 8 * PARTS]
    line_d, far_d, line_u, far_u, fin_u, tail_sems = refs[11 + 8 * PARTS :]
    p = Place()
    rail = ga.shape[2] // 2
    part = rail // PARTS
    rows = ga.shape[1] // 2

    def lanes_of(i, c):
        return pl.ds(pl.multiple_of(c * rail + i * part, TILE), part)

    jobs = [
        Scatter(
            p, i, lambda l, c, i=i: ga.at[pl.ds(l * 4, 4), :, lanes_of(i, c)], refs[5 + 8 * i : 13 + 8 * i], sems
        )
        for i in range(PARTS)
    ]
    out_u[...] = u_so_far[...]
    out_d[...] = d_so_far[...]
    greet(p)
    order = level_order(p)
    items = [(job, l) for l in order for job in jobs]
    for job, l in items:
        job.begin(l)
    owner = level_of(3)
    sum_d = mine_d[...] + two_d[...].astype(F32)
    line_d[...] = sum_d.astype(BF)

    def tail(kind, s):
        src, dst = (line_d, far_d.at[s - 1]) if kind == 0 else (line_u.at[s - 1], far_u.at[s - 1])
        return push(src, dst, tail_sems.at[0, kind, s], tail_sems.at[1, kind, s], p.to_z(s))

    def sum_u(l):
        return mine_u[l] + two_u[l].astype(F32)

    for s in (1, 2, 3):
        pl.when(lax.rem(p.z + s, 4) == owner)(lambda s=s: tail(0, s).start())
        line_u[s - 1] = sum_u(lax.rem(p.z + s, 4)).astype(BF)
        tail(1, s).start()
    steps = vector_steps(p, lambda: vec_m[...] + vec_a[...], total, hold, landed, vec_sems)
    number = len(items)
    for n in range(number + 2):
        if n < number:
            items[n][0].pair(items[n][1])
        if 1 <= n <= number:
            items[n - 1][0].side(items[n - 1][1])
        if 2 <= n:
            job, l = items[n - 2]
            if n - 2 < number - PARTS:
                job.plane(l)
            else:
                job.last()
        if n < 5:
            steps[n]()
    sends = []
    for i, job in enumerate(jobs):
        lane = lanes_of(i, p.c)
        cp = push(
            job.fin.at[pl.ds(pl.multiple_of((1 - p.c) * rows, 8), rows)], out_a.at[:, lane],
            last_sems.at[0, i], last_sems.at[1, i], p.to_core,
        )
        cp.start()
        sends.append(cp)
        out_a[:, lane] = job.fin[pl.ds(pl.multiple_of(p.c * rows, 8), rows), :]
    fin_u[...] = sum_u(p.z)
    for s in (1, 2, 3):
        tail(1, s).wait()
        fin_u[...] += far_u[s - 1].astype(F32)
    half = fin_u.shape[1]
    lane = pl.ds(pl.multiple_of(owner * 2 * half + p.c * half, TILE), half)
    cp = push(
        fin_u.at[pl.ds(pl.multiple_of((1 - p.c) * rows, 8), rows)], out_u.at[:, lane],
        tail_sems.at[0, 0, 0], tail_sems.at[1, 0, 0], p.to_core,
    )
    cp.start()
    sends.append(cp)
    out_u[:, lane] = fin_u[pl.ds(pl.multiple_of(p.c * rows, 8), rows), :]

    @pl.when(p.z == owner)
    def _():
        out_d[...] = sum_d
        for s in (1, 2, 3):
            tail(0, s).wait_recv()
            out_d[...] += far_d[s - 1].astype(F32)

    for s in (1, 2, 3):
        pl.when(lax.rem(p.z + s, 4) == owner)(lambda s=s: tail(0, s).wait_send())
    device = p.z * 8 + p.f
    width = total.shape[1]
    share = width // 32
    out_v[...] = pltpu.roll(total[...], lax.rem(width - device * share, width), 1)[:, :TILE]
    row = VECTORS + device // 8
    up = jnp.sum(jnp.where(lax.broadcasted_iota(jnp.int32, total.shape, 0) == row, total[...], 0.0), axis=0, keepdims=True)
    up = jnp.broadcast_to(up, (8, width))
    out_b[...] = pltpu.roll(up, lax.rem(width - lax.rem(device, 8) * 4 * share, width), 1)[:, :TILE]
    for job in jobs:
        job.finish()
    for cp in sends:
        cp.wait()


def scatter_all(ga, vec_m, vec_a, u_so_far, d_so_far, two_d, mine_d, two_u, mine_u):
    rows = ga.shape[1] // 2
    cols = ga.shape[2]
    width = vec_m.shape[1]
    block = (2 * rows, cols // 2 // PARTS)
    bufs = [
        pltpu.VMEM((4, 4) + block, BF),
        pltpu.VMEM((4, 4) + block, BF),
        pltpu.VMEM((4, 2) + block, BF),
        pltpu.VMEM((4,) + block, BF),
        pltpu.VMEM((4,) + block, BF),
        pltpu.VMEM((4,) + block, BF),
        pltpu.VMEM((4,) + block, BF),
        pltpu.VMEM(block, F32),
    ]
    vmem, hbm = pl.BlockSpec(memory_space=pltpu.VMEM), pl.BlockSpec(memory_space=pl.ANY)
    return pl.pallas_call(
        scatter_kernel,
        out_shape=(
            jax.ShapeDtypeStruct((rows, cols), F32),
            jax.ShapeDtypeStruct((16, TILE), F32),
            jax.ShapeDtypeStruct((8, TILE), F32),
            jax.ShapeDtypeStruct(u_so_far.shape, F32),
            jax.ShapeDtypeStruct(d_so_far.shape, F32),
        ),
        in_specs=[hbm] + [vmem] * 8,
        out_specs=(vmem,) * 5,
        scratch_shapes=[
            *(bufs * PARTS),
            pltpu.VMEM((4, 16, width), F32),
            pltpu.VMEM((6, 16, width), F32),
            pltpu.VMEM((16, width), F32),
            pltpu.SemaphoreType.DMA((2, 6, PARTS, 4)),
            pltpu.SemaphoreType.DMA((2, PARTS)),
            pltpu.SemaphoreType.DMA((2, 6)),
            pltpu.VMEM(two_d.shape, BF),
            pltpu.VMEM((3,) + two_d.shape, BF),
            pltpu.VMEM((3,) + two_u.shape[1:], BF),
            pltpu.VMEM((3,) + two_u.shape[1:], BF),
            pltpu.VMEM(two_u.shape[1:], F32),
            pltpu.SemaphoreType.DMA((2, 2, 4)),
        ],
        compiler_params=pltpu.CompilerParams(collective_id=1, has_side_effects=True, vmem_limit_bytes=60 * 2**20),
        name="scatter_gradients",
    )(ga, vec_m, vec_a, u_so_far, d_so_far, two_d, mine_d, two_u, mine_u)


def part_kernel(a, u, d, v, b, *outs):
    width = outs[0].shape[1]
    for i in range(4):
        outs[i][...] = a[:, i * width : (i + 1) * width]
    outs[4][...] = u[...]
    outs[5][...] = d[...]
    for i in range(VECTORS):
        outs[6 + i][...] = v[i : i + 1, : outs[6 + i].shape[1]]
    outs[6 + VECTORS][...] = b[0:1, : outs[6 + VECTORS].shape[1]]


def part_all(a, u, d, v, b, share, up_share):
    rows, width = a.shape[0], a.shape[1] // 4
    shapes = [(rows, width)] * 4 + [u.shape, d.shape] + [(1, share)] * VECTORS + [(1, up_share)]
    vmem = pl.BlockSpec(memory_space=pltpu.VMEM)
    outs = pl.pallas_call(
        part_kernel,
        out_shape=tuple(jax.ShapeDtypeStruct(s, F32) for s in shapes),
        in_specs=[vmem] * 5,
        out_specs=(vmem,) * len(shapes),
        name="part_gradients",
    )(a, u, d, v, b)
    return outs[:6], [w.reshape(-1) for w in outs[6:]]


HEAD = 64
EPSILON = 1e-06
LANES = 128
FAR = -1e30
GAIN1, BIAS1, ROUTER, B_QUERY, B_VALUE, B_OUT, GAIN2, BIAS2, B_DOWN, B_UP = range(10)


def dot(a, b):
    return lax.dot_general(a, b, (((1,), (0,)), ((), ())), preferred_element_type=F32)


def dot_nt(a, b):
    return lax.dot_general(a, b, (((1,), (1,)), ((), ())), preferred_element_type=F32)


def dot_tn(a, b):
    return lax.dot_general(a, b, (((0,), (0,)), ((), ())), preferred_element_type=F32)


def up_to(count, step):
    return (count + step - 1) // step * step


def iota(shape, dim):
    return lax.broadcasted_iota(jnp.int32, shape, dim)


def normalized(x):
    centred = x - jnp.mean(x, axis=-1, keepdims=True)
    scale = lax.rsqrt(jnp.mean(centred * centred, axis=-1, keepdims=True) + EPSILON)
    return centred * scale, scale


def norm_back(n, scale, gain, e):
    eg = e * gain
    return scale * (eg - jnp.mean(eg, axis=-1, keepdims=True) - n * jnp.mean(eg * n, axis=-1, keepdims=True))


def column_of(row, size):
    eye = iota((size, size), 0) == iota((size, size), 1)
    return jnp.sum(jnp.where(eye, jnp.broadcast_to(row, (size, size)), 0.0), axis=1, keepdims=True)


def order_of(picked_ref, order_ref):
    cap = picked_ref.shape[1]
    before = jnp.where(iota((cap, cap), 0) < iota((cap, cap), 1), 1.0, 0.0).astype(BF)
    order_ref[...] = dot(picked_ref[...].astype(BF), before)


def pad_rows(selected, segment, picked_ref, marks_ref):
    count, length = selected.shape
    picked_ref[...] = jnp.zeros_like(picked_ref)
    picked_ref[0:count, 0:length] = selected[...].astype(F32)
    if marks_ref is not None:
        marks_ref[...] = jnp.zeros_like(marks_ref)
        marks_ref[0:count, 0:length] = segment[...].astype(F32)


def row_of(ref, r):
    return jnp.sum(jnp.where(iota(ref.shape, 0) == r, ref[...], 0.0), axis=0, keepdims=True)


def to_picked(order, picked, size):
    cap = order.shape[1]
    hit = (order == iota((size, cap), 0).astype(F32)) & (picked > 0.5)
    return jnp.where(hit, 1.0, 0.0)


def from_picked(order, picked, size):
    cap = order.shape[1]
    place = column_of(jnp.where(picked > 0.5, order, -1.0), cap)
    return jnp.where(place == iota((cap, size), 1).astype(F32), 1.0, 0.0).astype(BF)


def sizes(cap):
    half = up_to(cap // 2, HEAD)
    return [(half, up_to(half, LANES)), (cap, cap)]


def loop(count, what):
    lax.fori_loop(0, count, lambda i, c: (what(i), c)[1], 0)


def lanes(i, size):
    return pl.ds(pl.multiple_of(i * size, LANES), size)


def each_size(count, cap, what):
    low = 0
    for rows, keys in sizes(cap):

        @pl.when((count > low) & (count <= rows))
        def _(rows=rows, keys=keys):
            what(rows, keys)

        low = rows


def forbidden(hit, marks, count, size):
    segment_of = dot_nt(jnp.broadcast_to(marks, (8, marks.shape[1])).astype(BF), hit.astype(BF))[0:1]
    segment_of = jnp.where(iota((1, size), 1) < count, segment_of, 99.0)
    column = jnp.sum(hit * marks, axis=1, keepdims=True)
    column = jnp.where(iota((size, 1), 0) < count, column, 99.0)
    return jnp.where(column == segment_of, 0.0, FAR)


def two_heads(pair):
    first = iota(pair.shape, 1) < HEAD
    zero = jnp.zeros_like(pair)
    return jnp.concatenate([jnp.where(first, pair, zero), jnp.where(first, zero, pair)], axis=0)


def one_pair(turned):
    size = turned.shape[1] // 2
    return jnp.concatenate([turned[:HEAD, :size], turned[HEAD:, size:]], axis=0).T


def attend_kernel(r, x, segment, selected, wa, table, *refs):
    outs, kept = refs[-22:-14], refs[-14:-6]
    mid, xc, h, qkv, attn, branch, logs, gates = kept
    xs, picked, marks, order, bar, sems = refs[-6:]
    cap = xs.shape[0]
    span, width = x.shape[1], x.shape[2]
    pad_rows(selected, segment, picked, marks)
    order_of(picked, order)
    sel, place, mark = [ref[r : r + 1, :] for ref in (picked, order, marks)]
    count = jnp.sum(sel).astype(jnp.int32)
    xs[span:cap, :] = jnp.zeros((cap - span, width), BF)
    xs[0:span, :] = x[r]
    mid[...] = x[r].astype(F32)

    def leave(i, size):
        src, dst = kept[i], outs[i].at[r]
        if i not in (0, 6):
            src, dst = src.at[0:size], dst.at[0:size]
        return pltpu.make_async_copy(src, dst, sems.at[i])

    def work(rows, keys):
        hit = to_picked(place, sel, keys)
        block = forbidden(hit, mark, count, keys)
        bar[0:keys, 0:keys] = block
        bar[0:keys, keys : 2 * keys] = block
        x_in = dot(hit[:rows].astype(BF), xs[...])
        xc[0:rows, :] = x_in.astype(BF)
        n, _ = normalized(x_in)
        h_in = (n * table[GAIN1 : GAIN1 + 1, :] + table[BIAS1 : BIAS1 + 1, :]).astype(BF)
        h[0:rows, :] = h_in
        gate = jax.nn.sigmoid(jnp.sum(h_in.astype(F32) * table[ROUTER : ROUTER + 1, :], axis=1, keepdims=True))
        for i, b in enumerate((B_QUERY, None, B_VALUE)):
            part = dot(h_in, wa[:, i * width : (i + 1) * width])
            if b is not None:
                part = part + table[b : b + 1, :]
            qkv[0:rows, i * width : (i + 1) * width] = part.astype(BF)
        if keys > rows:
            qkv[rows:keys, :] = jnp.zeros((keys - rows, 3 * width), BF)
        for i in (1, 2, 3):
            leave(i, keys).start()

        def pair(i, carry):
            lane = i * LANES
            q = qkv[0:keys, pl.ds(pl.multiple_of(lane, LANES), LANES)]
            k = qkv[0:keys, pl.ds(pl.multiple_of(lane + width, LANES), LANES)]
            v = qkv[0:keys, pl.ds(pl.multiple_of(lane + 2 * width, LANES), LANES)]
            s = dot_nt(k, two_heads(q * BF(HEAD**-0.5))) + bar[0:keys, 0 : 2 * keys]
            top = jnp.max(s, axis=0, keepdims=True)
            e = jnp.exp(s - top)
            total = jnp.sum(e, axis=0, keepdims=True)
            out = one_pair(dot_tn(v, e.astype(BF)) * (1.0 / total))
            attn[0:keys, pl.ds(pl.multiple_of(lane, LANES), LANES)] = out.astype(BF)
            logs[i, 0:1, 0 : 2 * keys] = top + jnp.log(total)
            return carry

        lax.fori_loop(0, width // LANES, pair, 0)
        gates[0:rows, :] = jnp.broadcast_to(gate, (rows, LANES))
        for i in (4, 6, 7):
            leave(i, keys).start()
        out = dot(attn[0:rows, :], wa[:, 3 * width :]) + table[B_OUT : B_OUT + 1, :]
        branch[0:rows, :] = out.astype(BF)
        leave(5, keys).start()
        back = from_picked(place, sel, keys)[:span, :rows]
        mid[...] += dot(back, (out * gate).astype(BF))
        for i in range(1, 8):
            leave(i, keys).wait()

    each_size(count, cap, work)
    leave(0, cap).start()
    leave(0, cap).wait()


def attend(r, patches, segment, selected, wa, table, kept=()):
    count, span, width = patches.shape
    cap = up_to(span, LANES)
    shapes = [
        ((span, width), F32), ((cap, width), BF), ((cap, width), BF), ((cap, 3 * width), BF), ((cap, width), BF),
        ((cap, width), BF), ((width // LANES, 1, 2 * cap), F32), ((cap, LANES), F32),
    ]
    vmem, hbm = pl.BlockSpec(memory_space=pltpu.VMEM), pl.BlockSpec(memory_space=pl.ANY)
    return pl.pallas_call(
        partial(attend_kernel, r),
        out_shape=tuple(jax.ShapeDtypeStruct((count,) + s, d) for s, d in shapes),
        in_specs=[vmem] * 5 + [hbm] * len(kept),
        out_specs=(hbm,) * 8,
        scratch_shapes=[pltpu.VMEM(s, d) for s, d in shapes] + [
            pltpu.VMEM((cap, width), BF),
            pltpu.VMEM((8, cap), F32),
            pltpu.VMEM((8, cap), F32),
            pltpu.VMEM((8, cap), F32),
            pltpu.VMEM((cap, 2 * cap), F32),
            pltpu.SemaphoreType.DMA((8,)),
        ],
        input_output_aliases={5 + i: i for i in range(len(kept))},
        cost_estimate=pl.CostEstimate(flops=4 * 10**9, bytes_accessed=10**7, transcendentals=10**6),
        compiler_params=pltpu.CompilerParams(vmem_limit_bytes=60 * 2**20),
        name="attend",
    )(patches, segment, selected, wa, table, *kept)


def attend_back_kernel(mixed_in, gm, segment, selected, wa_in, table, *refs):
    kept_in, (rows_x, rows_mixed, grad_a, sums) = refs[:7], refs[7:11]
    kept, (wa, mixed) = refs[11:18], refs[18:20]
    xc, h, qkv, attn, branch, logs, gates = kept
    grad_x, high, picked, marks, order, bar, ga, dqkv, sems, whole_sems = refs[20:]
    cap = high.shape[0]
    span, width = gm.shape[1], gm.shape[2]
    pad_rows(selected, segment, picked, marks)
    order_of(picked, order)
    high[...] = jnp.zeros_like(high)
    grad_a[...] = jnp.zeros_like(grad_a)
    sums[...] = jnp.zeros_like(sums)

    def fetch(i, r, size):
        src, dst = kept_in[i].at[r], kept[i].at[r]
        if i != 5:
            src, dst = src.at[0:size], dst.at[0:size]
        return pltpu.make_async_copy(src, dst, sems.at[i, r])

    counts = [jnp.sum(picked[r : r + 1, :]).astype(jnp.int32) for r in range(gm.shape[0])]
    first = jnp.where(counts[0] > 0, 0, 1)
    load_wa = pltpu.make_async_copy(wa_in, wa, whole_sems.at[0])
    load_mixed = pltpu.make_async_copy(mixed_in, mixed, whole_sems.at[1])
    for r in range(gm.shape[0]):

        def begin(rows, keys, r=r):
            for i in (6, 4, 3, 2, 5, 1, 0):
                fetch(i, r, keys).start()

        each_size(counts[r], cap, begin)
        (load_mixed if r else load_wa).start()

    def add(i, v):
        sums[i : i + 1, :] += jnp.sum(v, axis=0, keepdims=True)

    def add_weight(i, j, v):
        at = slice(i * width, j * width)
        grad_a[:, at] = (grad_a[:, at].astype(F32) + v).astype(BF)

    def row(r, carry):
        sel, place, mark = row_of(picked, r), row_of(order, r), row_of(marks, r)
        count = jnp.sum(sel).astype(jnp.int32)
        high[0:span, :] = gm[r]

        @pl.when(count == 0)
        def _():
            grad_x[r] = gm[r]

        def work(rows, keys):
            hit = to_picked(place, sel, keys)
            block = forbidden(hit, mark, count, keys)
            bar[0:keys, 0:keys] = block
            bar[0:keys, keys : 2 * keys] = block
            take = hit[:rows].astype(BF)
            for i in (6, 4, 3):
                fetch(i, r, keys).wait()
            pl.when(r == first)(load_wa.wait)
            g = dot(take, high[...])
            gate = gates[r, 0:rows, 0:1]
            grad_logit = jnp.sum(g * branch[r, 0:rows, :].astype(F32), axis=1, keepdims=True) * gate * (1.0 - gate)
            gb = g * gate
            add(B_OUT, gb.astype(BF).astype(F32))
            gb = gb.astype(BF)
            add_weight(3, 4, dot_tn(attn[r, 0:rows, :], gb))
            ga[0:rows, :] = dot_nt(gb, wa[:, 3 * width :]).astype(BF)
            if keys > rows:
                ga[rows:keys, :] = jnp.zeros((keys - rows, width), BF)

            for i in (2, 5, 1, 0):
                fetch(i, r, keys).wait()

            def pair(i, carry):
                at = pl.ds(pl.multiple_of(i * LANES, LANES), LANES)
                at_k = pl.ds(pl.multiple_of(i * LANES + width, LANES), LANES)
                at_v = pl.ds(pl.multiple_of(i * LANES + 2 * width, LANES), LANES)
                q2 = two_heads(qkv[r, 0:keys, at] * BF(HEAD**-0.5))
                k = qkv[r, 0:keys, at_k]
                v = qkv[r, 0:keys, at_v]
                g2 = two_heads(ga[0:keys, at])
                p = jnp.exp(dot_nt(k, q2) + bar[0:keys, 0 : 2 * keys] - logs[r, i, 0:1, 0 : 2 * keys])
                dp = dot_nt(v, g2)
                ds = (p * (dp - jnp.sum(p * dp, axis=0, keepdims=True))).astype(BF)
                dqkv[0:keys, at] = one_pair(dot_tn(k, ds) * HEAD**-0.5).astype(BF)
                dqkv[0:keys, at_k] = dot(ds, q2).astype(BF)
                dqkv[0:keys, at_v] = dot(p.astype(BF), g2).astype(BF)
                return carry

            lax.fori_loop(0, width // LANES, pair, 0)
            add(B_QUERY, dqkv[0:rows, 0:width].astype(F32))
            add(B_VALUE, dqkv[0:rows, 2 * width :].astype(F32))
            h_in = h[r, 0:rows, :]
            add(ROUTER, h_in.astype(F32) * grad_logit)
            add_weight(0, 3, dot_tn(h_in, dqkv[0:rows, :]))
            gh = dot_nt(dqkv[0:rows, :], wa[:, : 3 * width]) + grad_logit * table[ROUTER : ROUTER + 1, :]
            n, scale = normalized(xc[r, 0:rows, :].astype(F32))
            add(GAIN1, n * gh)
            add(BIAS1, gh)
            dx = norm_back(n, scale, table[GAIN1 : GAIN1 + 1, :], gh).astype(BF)
            back = from_picked(place, sel, keys)[:span, :rows]
            grad_x[r] = (gm[r].astype(F32) + dot(back, dx)).astype(BF)

        each_size(count, cap, work)
        return carry

    lax.fori_loop(0, gm.shape[0], row, 0)

    pl.when(sum(counts) == 0)(load_wa.wait)

    load_mixed.wait()
    for r in range(gm.shape[0]):
        rows_x[:, r, :] = grad_x[r, 0 : rows_x.shape[0], :]
        rows_mixed[:, r, :] = mixed[r, 0 : rows_x.shape[0], :]


def attend_back(mixed, gm, segment, selected, wa, table, kept):
    count, span, width = gm.shape
    cap = up_to(span, LANES)
    vmem, hbm = pl.BlockSpec(memory_space=pltpu.VMEM), pl.BlockSpec(memory_space=pl.ANY)
    rows_out = jax.ShapeDtypeStruct((segment.shape[1], count, width), BF)
    rows_x, rows_mixed, grad_a, sums = pl.pallas_call(
        attend_back_kernel,
        out_shape=(
            rows_out,
            rows_out,
            jax.ShapeDtypeStruct(wa.shape, BF),
            jax.ShapeDtypeStruct((16, width), F32),
        ),
        in_specs=[hbm] + [vmem] * 3 + [hbm, vmem] + [hbm] * len(kept),
        out_specs=(vmem,) * 4,
        scratch_shapes=[
            *[pltpu.VMEM(v.shape, v.dtype) for v in kept],
            pltpu.VMEM(wa.shape, BF),
            pltpu.VMEM(mixed.shape, BF),
            pltpu.VMEM(gm.shape, BF),
            pltpu.VMEM((cap, width), BF),
            pltpu.VMEM((8, cap), F32),
            pltpu.VMEM((8, cap), F32),
            pltpu.VMEM((8, cap), F32),
            pltpu.VMEM((cap, 2 * cap), F32),
            pltpu.VMEM((cap, width), BF),
            pltpu.VMEM((cap, 3 * width), BF),
            pltpu.SemaphoreType.DMA((7, count)),
            pltpu.SemaphoreType.DMA((2,)),
        ],
        cost_estimate=pl.CostEstimate(flops=10**10, bytes_accessed=3 * 10**7, transcendentals=10**6),
        compiler_params=pltpu.CompilerParams(vmem_limit_bytes=60 * 2**20),
        name="attend_back",
    )(mixed, gm, segment, selected, wa, table, *kept)
    return rows_x.transpose(1, 0, 2), rows_mixed.transpose(1, 0, 2), grad_a, sums


def gelu_parts(p):
    z = jnp.abs(p)
    e = jnp.exp(-0.5 * p * p)
    t = 1.0 / (1.0 + (0.3275911 * 0.5**0.5) * z)
    poly = ((((1.061405429 * t - 1.453152027) * t + 1.421413741) * t - 0.284496736) * t + 0.254829592) * t
    tail = 0.5 * poly * e
    phi = jnp.where(p > 0, 1.0 - tail, tail)
    return phi, phi + p * (e * 0.3989422804014327)


BLOCK = 592


class ChunkScatter:
    def __init__(self, p, kind, whole, bufs, fin, sems):
        self.p, self.kind, self.whole, self.fin, self.sems = p, kind, whole, fin, sems
        self.got, self.one, self.give, self.two, self.line, self.far = bufs
        rail0 = p.c == 0
        self.me = p.y * 2 + p.x
        self.first = jnp.where(rail0, p.y * 2 + 1 - p.x, (1 - p.y) * 2 + p.x)
        self.second = jnp.where(rail0, (1 - p.y) * 2 + p.x, p.y * 2 + 1 - p.x)
        self.diag = (1 - p.y) * 2 + 1 - p.x
        self.to_first = (p.z, self.first * 2 + p.c)
        self.to_second = (p.z, self.second * 2 + p.c)

    def move(self, stage, j, src, dst, to):
        return push(src, dst, self.sems.at[0, stage, self.kind, j], self.sems.at[1, stage, self.kind, j], to)

    def rail(self, j, c):
        if self.kind == 0:
            return self.whole.at[j, :, c]
        return self.whole.at[j, :, :, :, lanes(c, self.whole.shape[4] // 2)]

    def block(self, j, chip):
        if self.kind == 0:
            return self.whole.at[j, chip, self.p.c]
        return self.whole.at[j, :, chip, :, lanes(self.p.c, self.whole.shape[4] // 2)]

    def core(self, j):
        return self.move(0, j, self.rail(j, 1 - self.p.c), self.got.at[j], self.p.to_core)

    def step1(self, j, slot):
        return self.move(1 + slot, j, self.block(j, self.diag if slot else self.first), self.one.at[j, slot], self.to_first)

    def step2(self, j):
        return self.move(3, j, self.give.at[j], self.two.at[j], self.to_second)

    def begin(self, j):
        self.core(j).start()

    def pair(self, j):
        self.core(j).wait_recv()
        mine = self.rail(j, self.p.c)
        mine[...] = (mine[...].astype(F32) + self.got[j].astype(F32)).astype(BF)
        self.step1(j, 1).start()
        self.step1(j, 0).start()

    def side(self, j):
        self.step1(j, 1).wait_recv()
        self.give[j] = (self.block(j, self.second)[...].astype(F32) + self.one[j, 1].astype(F32)).astype(BF)
        self.step2(j).start()

    def along(self, j, s):
        if self.kind == 0:
            src = self.line.at[j]
        else:
            src = self.line.at[j, s - 1]
        return self.move(3 + s, j, src, self.far.at[j, s - 1], self.p.to_z(s))

    def plane_sum(self, j, l):
        if self.kind == 0:
            return self.block(j, self.me)[...].astype(F32) + self.one[j, 0].astype(F32) + self.two[j].astype(F32)
        own = self.whole[j, l, self.me, :, lanes(self.p.c, self.whole.shape[4] // 2)]
        return own.astype(F32) + self.one[j, 0, l].astype(F32) + self.two[j, l].astype(F32)

    def cross(self, j, owner):
        z = self.p.z
        self.step1(j, 0).wait_recv()
        self.step2(j).wait_recv()
        if self.kind == 0:
            self.line[j] = self.plane_sum(j, 0).astype(BF)
            for s in (1, 2, 3):

                @pl.when(lax.rem(z + s, 4) == owner)
                def _(s=s):
                    self.along(j, s).start()

            return
        for s in (1, 2, 3):
            self.line[j, s - 1] = self.plane_sum(j, lax.rem(z + s, 4)).astype(BF)
            self.along(j, s).start()

    def last(self, j, owner):
        if self.kind == 0:

            @pl.when(self.p.z == owner)
            def _():
                total = self.plane_sum(j, 0)
                for s in (1, 2, 3):
                    self.along(j, s).wait_recv()
                    total = total + self.far[j, s - 1].astype(F32)
                self.fin[...] = total

            return
        total = self.plane_sum(j, self.p.z)
        for s in (1, 2, 3):
            self.along(j, s).wait_recv()
            total = total + self.far[j, s - 1].astype(F32)
        self.fin[j] = total

    def hand_over(self, j, give, mine):
        self.step1(j, 1).wait_recv()
        give[...] = (self.block(j, self.second)[...].astype(F32) + self.one[j, 1].astype(F32)).astype(BF)
        self.step1(j, 0).wait_recv()
        mine[...] = self.block(j, self.me)[...].astype(F32) + self.one[j, 0].astype(F32)

    def finish(self, owner_of, handed):
        def left(j):
            self.core(j).wait_send()
            self.step1(j, 0).wait_send()
            self.step1(j, 1).wait_send()

        left(handed)

        def one(j):
            left(j)
            self.step2(j).wait_send()
            for s in (1, 2, 3):
                if self.kind == 0:

                    @pl.when(lax.rem(self.p.z + s, 4) == owner_of(j))
                    def _(s=s):
                        self.along(j, s).wait_send()

                else:
                    self.along(j, s).wait_send()

        loop(handed, one)


def level_of(i):
    return jnp.where(i == 0, 0, jnp.where(i == 1, 3, i - 1))


def mlp_kernel(remote, mid, g, wu, wd, table, *refs):
    if remote:
        parts_d, refs = (wd,) + refs[:3], refs[3:]
    mlp_body(remote, mid, g, wu, parts_d if remote else (wd,), table, *refs)


def mlp_body(remote, mid, g, wu, parts_d, table, mixed, gm, sums, out_u, out_d, *refs):
    if remote:
        handed, refs = refs[:4], refs[4:]
    u, acc, act, gp, hold_u, hold_d, weight_sems = refs[:7]
    count, span, width = mid.shape
    tokens = count * span
    chunk = width
    chunks = 4 if remote else parts_d[0].shape[0] // chunk
    blocks = tokens // BLOCK
    per = span // BLOCK
    if remote:
        grad_d, grad_u, fin_u = refs[7:10]
        bufs_d, bufs_u = refs[10:16], refs[16:22]
        sems, last_sems, part_sems = refs[22:]
        p = Place()
        greet(p)
        down = ChunkScatter(p, 0, grad_d, bufs_d, out_d, sems)
        up = ChunkScatter(p, 1, grad_u, bufs_u, fin_u, sems)
        rail = width // 2
        rows = out_u.shape[0]

    def row(i):
        return table[i : i + 1, :]

    def each_block(what):
        loop(blocks, lambda b: what(b, pl.ds(pl.multiple_of(b * BLOCK, 16), BLOCK)))

    def mid_of(b):
        return mid[b // per, pl.ds(pl.multiple_of(lax.rem(b, per) * BLOCK, 16), BLOCK), :]

    def load(i):
        j, slot = level_of(i), lax.rem(i, 2)
        up_part = pltpu.make_async_copy(wu.at[:, lanes(j, chunk)], hold_u.at[slot], weight_sems.at[0, slot])
        if remote:
            return (up_part,)
        rows_d = parts_d[0].at[pl.ds(pl.multiple_of(j * chunk, 16), chunk)]
        return up_part, pltpu.make_async_copy(rows_d, hold_d.at[slot], weight_sems.at[1, slot])

    def weights(i):
        if remote:
            return hold_u[lax.rem(i, 2)], hold_d[i].reshape(chunk, width)
        return hold_u[lax.rem(i, 2)], hold_d[lax.rem(i, 2)]

    for cp in load(0):
        cp.start()
    if remote:
        chips = (p.y * 2 + p.x, p.y * 2 + 1 - p.x, (1 - p.y) * 2 + p.x, (1 - p.y) * 2 + 1 - p.x)

        def keep(i, n):
            return pltpu.make_async_copy(parts_d[n].at[level_of(i)], hold_d.at[i, chips[n], p.c], part_sems.at[2, i, n])

        def share(i, n):
            return push(
                parts_d[n].at[level_of(i)], hold_d.at[i, chips[n], p.c], part_sems.at[0, i, n], part_sems.at[1, i, n], p.to_core
            )

        for i in range(chunks):
            for n in range(4):
                keep(i, n).start()
                share(i, n).start()
    sums[...] = jnp.zeros_like(sums)
    acc[...] = jnp.zeros_like(acc)
    def start(b, at):
        n, _ = normalized(mid_of(b))
        u[at, :] = (n * row(GAIN2) + row(BIAS2)).astype(BF)
        sums[B_DOWN : B_DOWN + 1, :] += jnp.sum(g[at, :].astype(F32), axis=0, keepdims=True)

    each_block(start)

    def send_rail(i):
        lane = pl.ds(pl.multiple_of(level_of(i) * chunk + p.c * rail, TILE), rail)
        return push(
            fin_u.at[i, pl.ds(pl.multiple_of((1 - p.c) * rows, 8), rows)], out_u.at[:, lane],
            last_sems.at[0, i], last_sems.at[1, i], p.to_core,
        )

    def own_rail(i):
        up.last(i, 0)
        send_rail(i).start()
        lane = pl.ds(pl.multiple_of(level_of(i) * chunk + p.c * rail, TILE), rail)
        out_u[:, lane] = fin_u[i, pl.ds(pl.multiple_of(p.c * rows, 8), rows), :]

    def from_chunk(i, back, what):
        if remote:
            pl.when(i >= back)(lambda: what(i - back))

    def one_chunk(i):
        j, slot = level_of(i), lax.rem(i, 2)
        for cp in load(i):
            cp.wait()
        if remote:
            for n in range(4):
                keep(i, n).wait()
                share(i, n).wait_recv()

        @pl.when(i + 1 < chunks)
        def _():
            for cp in load(i + 1):
                cp.start()

        def hidden(b, at):
            in_u, in_d = weights(i)
            pre = dot(u[at, :], in_u) + table[pl.ds(B_UP + j, 1), :]
            phi, slope = gelu_parts(pre)
            act[at, :] = (pre * phi).astype(BF)
            grad_pre = (slope * dot_nt(g[at, :], in_d)).astype(BF)
            gp[at, :] = grad_pre
            sums[pl.ds(B_UP + j, 1), :] += jnp.sum(grad_pre.astype(F32), axis=0, keepdims=True)

        each_block(hidden)
        from_chunk(i, 1, lambda k: down.cross(k, level_of(k)))
        from_chunk(i, 1, lambda k: up.side(k))
        from_chunk(i, 2, own_rail)
        part = dot_tn(act[...], g[...]).astype(BF)
        if remote:
            grad_d[i] = part.reshape(grad_d.shape[1:])
            down.begin(i)
        else:
            out_d[pl.ds(pl.multiple_of(j * chunk, 16), chunk), :] = part
        part = dot_tn(u[...], gp[...]).astype(BF)
        if remote:
            grad_u[i] = part.reshape(grad_u.shape[1:])
            up.begin(i)
            down.pair(i)
        else:
            out_u[:, lanes(j, chunk)] = part
        from_chunk(i, 1, lambda k: up.cross(k, 0))

        def total(b, at):
            in_u, in_d = weights(i)
            acc[0, at, :] += dot(act[at, :], in_d)
            acc[1, at, :] += dot_nt(gp[at, :], in_u)

        for b in range(blocks):
            total(b, pl.ds(b * BLOCK, BLOCK))
            if remote and b == 0:
                up.pair(i)
        if remote:
            pl.when(i + 1 < chunks)(lambda: down.side(i))
        from_chunk(i, 1, lambda k: down.last(k, level_of(k)))

    loop(chunks, one_chunk)

    def end(b, at):
        m = mid_of(b)
        out = (m + acc[0, at, :] + row(B_DOWN)).astype(BF)
        mixed[b] = out
        n, scale = normalized(m)
        e = acc[1, at, :]
        sums[GAIN2 : GAIN2 + 1, :] += jnp.sum(n * e, axis=0, keepdims=True)
        sums[BIAS2 : BIAS2 + 1, :] += jnp.sum(e, axis=0, keepdims=True)
        gm[b] = (g[at, :].astype(F32) + norm_back(n, scale, row(GAIN2), e)).astype(BF)

    for b in range(blocks):
        end(b, pl.ds(b * BLOCK, BLOCK))
        if remote and b == 0:
            own_rail(chunks - 2)
    if remote:
        down.hand_over(chunks - 1, *handed[:2])
        up.hand_over(chunks - 1, *handed[2:])
        for i in range(chunks - 1):
            send_rail(i).wait()
        up.finish(level_of, chunks - 1)
        down.finish(level_of, chunks - 1)
        for i in range(chunks):
            for n in range(4):
                share(i, n).wait_send()


def mlp(remote, mid, cot, wu, parts_d, table):
    count, span, width = mid.shape
    tokens = count * span
    if remote:
        rows, depth = wu.shape[0] // 32, parts_d[0].shape[1]
        outs = [jax.ShapeDtypeStruct((rows, wu.shape[1]), F32), jax.ShapeDtypeStruct((depth, width), F32)]
        half = width // 2
        for shape in ((depth, width), (4, 2 * rows, half)):
            outs += [jax.ShapeDtypeStruct(shape, BF), jax.ShapeDtypeStruct(shape, F32)]
        extra = [
            pltpu.VMEM((4, 4, 2, depth, width), BF),
            pltpu.VMEM((4, 4, 4, 2 * rows, width), BF),
            pltpu.VMEM((4, 2 * rows, half), F32),
        ]
        extra += [pltpu.VMEM((4, 4, depth, width), BF), pltpu.VMEM((4, 2, depth, width), BF)]
        extra += [pltpu.VMEM((4, depth, width), BF)] * 3 + [pltpu.VMEM((4, 3, depth, width), BF)]
        extra += [pltpu.VMEM((4, 4, 4, 2 * rows, half), BF), pltpu.VMEM((4, 2, 4, 2 * rows, half), BF)]
        extra += [pltpu.VMEM((4, 4, 2 * rows, half), BF)] * 2 + [pltpu.VMEM((4, 3, 2 * rows, half), BF)] * 2
        extra += [pltpu.SemaphoreType.DMA((2, 7, 2, 4)), pltpu.SemaphoreType.DMA((2, 4)), pltpu.SemaphoreType.DMA((3, 4, 4))]
        hold_d = pltpu.VMEM((4, 4, 2, depth, width), BF)
        params = dict(collective_id=2, has_side_effects=True)
    else:
        outs = [jax.ShapeDtypeStruct(wu.shape, BF), jax.ShapeDtypeStruct(parts_d[0].shape, BF)]
        extra, params = [], {}
        hold_d = pltpu.VMEM((2, width, width), BF)
    vmem = pl.BlockSpec(memory_space=pltpu.VMEM)
    hbm = pl.BlockSpec(memory_space=pl.ANY)
    return pl.pallas_call(
        partial(mlp_kernel, remote),
        out_shape=(
            jax.ShapeDtypeStruct(mid.shape, BF),
            jax.ShapeDtypeStruct(mid.shape, BF),
            jax.ShapeDtypeStruct((16, width), F32),
            *outs,
        ),
        in_specs=[vmem, vmem, hbm, hbm, vmem] + [hbm] * (len(parts_d) - 1),
        out_specs=(vmem,) * (3 + len(outs)),
        scratch_shapes=[
            pltpu.VMEM((tokens, width), BF),
            pltpu.VMEM((2, tokens, width), F32),
            pltpu.VMEM((tokens, width), BF),
            pltpu.VMEM((tokens, width), BF),
            pltpu.VMEM((2, width, width), BF),
            hold_d,
            pltpu.SemaphoreType.DMA((2, 2)),
            *extra,
        ],
        compiler_params=pltpu.CompilerParams(vmem_limit_bytes=62 * 2**20, **params),
        name="mlp",
    )(mid, cot.reshape(tokens, width), wu, parts_d[0], table, *parts_d[1:])


def local(
    small, patches, segment_ids, selected, cotangent, ln1_gain, ln1_bias, w_router, w_query, b_query,
    w_key, w_value, b_value, w_out, b_out, ln2_gain, ln2_bias, w_up, b_up, w_down, b_down,
):
    length, width = patches.shape[1:]
    span = up_to(length, 16)
    vectors = (ln1_gain, ln1_bias, w_router, b_query, b_value, b_out, ln2_gain, ln2_bias, b_down)
    matrices = (w_query, w_key, w_value, w_out, w_up, w_down)
    if small:
        attn_w, up_w, down_z, table, x, cot = gather_all(vectors, b_up, matrices, (patches, cotangent), span)
        attn_w = attn_w.reshape(-1, attn_w.shape[2])
        up_w = up_w.reshape(-1, up_w.shape[2])
        down_x = lax.ppermute(down_z, "fsdp", [(i, i ^ 2) for i in range(8)])
        down_y = lax.ppermute(down_z, "fsdp", [(i, i ^ 4) for i in range(8)])
    else:
        whole = [lax.all_gather(v, AXES, axis=0, tiled=True) for v in vectors + (b_up,)]
        table = jnp.concatenate(
            [jnp.stack(whole[:VECTORS]), whole[VECTORS].reshape(4, width), jnp.zeros((3, width), BF)]
        ).astype(F32)
        attn_w = jnp.concatenate([lax.all_gather(w, AXES, axis=0, tiled=True) for w in matrices[:4]], axis=1)
        up_w = lax.all_gather(w_up, AXES, axis=0, tiled=True)
        down_w = lax.all_gather(w_down, AXES, axis=0, tiled=True)
        x, cot = [jnp.pad(v, ((0, 0), (0, span - length), (0, 0))) for v in (patches, cotangent)]
    kept = ()
    for r in range(x.shape[0]):
        kept = attend(r, x, segment_ids, selected, attn_w, table, kept)
        if small and r == 0:
            down_x, down_y, _ = lax.optimization_barrier((down_x, down_y, kept[6]))
            turn = jnp.where(lax.rem(lax.axis_index("fsdp"), 2) == 0, down_y, down_x)
            down_d = lax.ppermute(turn, "fsdp", [(i, i ^ (4 if i % 2 else 2)) for i in range(8)])
    mid, *kept = kept
    down_parts = (down_z, down_x, down_y, down_d) if small else (down_w,)
    mixed, grad_mid, sums_mlp, grad_u, grad_d, *handed = mlp(small, mid, cot, up_w, down_parts, table)
    if small:
        give_d, mine_d, give_u, mine_u = handed
        second = [(i, i ^ (2 if i % 2 else 4)) for i in range(8)]
        two_d, two_u = lax.ppermute(give_d, "fsdp", second), lax.ppermute(give_u, "fsdp", second)
    grad_x, mixed, grad_a, sums_attn = attend_back(mixed, grad_mid, segment_ids, selected, attn_w, table, kept)
    if small:
        own_a, own_v, own_b, grad_u, grad_d = scatter_all(
            grad_a.reshape(16, -1, grad_a.shape[1]), sums_mlp, sums_attn, grad_u, grad_d, two_d, mine_d, two_u, mine_u
        )
        own_m, (*own, own_up_b) = part_all(own_a, grad_u, grad_d, own_v, own_b, ln1_gain.shape[0], b_up.shape[0])
    else:
        sums = sums_mlp + sums_attn
        own = [lax.psum_scatter(sums[i], AXES, scatter_dimension=0, tiled=True) for i in range(VECTORS)]
        own_up_b = lax.psum_scatter(
            sums[VECTORS : VECTORS + 4].reshape(-1), AXES, scatter_dimension=0, tiled=True
        )
        own_m = [
            lax.psum_scatter(g.astype(F32), AXES, scatter_dimension=0, tiled=True)
            for g in jnp.split(grad_a, 4, axis=1) + [grad_u, grad_d]
        ]
    return (
        mixed, grad_x, own[0], own[1], own[2], own_m[0], own[3], own_m[1], own_m[2], own[4],
        own_m[3], own[5], own[6], own[7], own_m[4], own_up_b, own_m[5], own[8],
    )


def solution(mesh):
    flat, rows2, rows3 = P(AXES), P(AXES, None), P(AXES, None, None)
    vec, mat = flat, rows2
    small = mesh.shape["dp"] == 4 and mesh.shape["fsdp"] == 8
    return jax.shard_map(
        partial(local, small),
        mesh=mesh,
        in_specs=(
            rows3, rows2, rows2, rows3, vec, vec, vec, mat, vec, mat, mat, vec, mat, vec, vec, vec, mat, vec, mat, vec,
        ),
        out_specs=(
            rows3, rows3, vec, vec, vec, mat, vec, mat, mat, vec, mat, vec, vec, vec, mat, vec, mat, vec,
        ),
        check_vma=False,
    )
```

```python
from functools import partial
import math

import jax
import jax.numpy as jnp
from jax import lax
from jax.experimental import pallas as pl
from jax.experimental.pallas import tpu as pltpu
from jax.sharding import PartitionSpec as P

AXES = ("dp", "fsdp")
MESH = pl.DeviceIdType.MESH
BF = jnp.bfloat16
F32 = jnp.float32


class Place:
    def __init__(self):
        self.z = lax.axis_index("dp")
        self.f = lax.axis_index("fsdp")
        self.c = lax.rem(self.f, 2)
        self.x = lax.rem(self.f // 2, 2)
        self.y = self.f // 4
        self.chip = self.z * 4 + self.y * 2 + self.x
        self.chip_x = self.z * 4 + self.y * 2 + (1 - self.x)
        self.chip_y = self.z * 4 + (1 - self.y) * 2 + self.x
        self.to_core = (self.z, self.y * 4 + self.x * 2 + (1 - self.c))
        self.to_x = (self.z, self.y * 4 + (1 - self.x) * 2 + self.c)
        self.to_y = (self.z, (1 - self.y) * 4 + self.x * 2 + self.c)

    def to_z(self, step):
        return (lax.rem(self.z + step + 4, 4), self.f)


def greet(place):
    bar = pltpu.get_barrier_semaphore()
    others = [place.to_core, place.to_x, place.to_y] + [place.to_z(s) for s in (1, 2, 3)]
    for other in others:
        pl.semaphore_signal(bar, inc=1, device_id=other, device_id_type=MESH)
    pl.semaphore_wait(bar, len(others))


def push(src, dst, send, recv, to):
    return pltpu.make_async_remote_copy(
        src_ref=src, dst_ref=dst, send_sem=send, recv_sem=recv, device_id=to, device_id_type=MESH
    )


class Gather:
    def __init__(self, place, j, block, level, plane_first, sems):
        self.p, self.j, self.block, self.level, self.sems = place, j, block, level, sems
        self.plane_first = plane_first

    def copy(self, kind, i, ref, to):
        return push(ref, ref, self.sems.at[2 * kind, self.j, i], self.sems.at[2 * kind + 1, self.j, i], to)

    def piece(self, l):
        if self.plane_first:
            return self.level(l, self.p.c)
        return self.block(l * 4 + self.p.y * 2 + self.p.x)

    def up(self, k):
        return self.copy(0, k, self.piece(lax.rem(self.p.z - k + 4, 4)), self.p.to_z(1))

    def up_in(self, k):
        return self.copy(0, k, self.piece(lax.rem(self.p.z - k + 3, 4)), self.p.to_z(1))

    def down(self, k):
        return self.copy(1, k, self.piece(lax.rem(self.p.z + k, 4)), self.p.to_z(3))

    def down_in(self, k):
        return self.copy(1, k, self.piece(lax.rem(self.p.z + k + 1, 4)), self.p.to_z(3))

    def xs(self, l):
        return self.copy(2, l, self.block(l * 4 + self.p.y * 2 + self.p.x), self.p.to_x)

    def ys(self, l):
        return self.copy(3, l, self.block(l * 4 + self.p.y * 2 + self.p.x), self.p.to_y)

    def side_in(self, l, y_side):
        p = self.p
        chip = l * 4 + (p.y + y_side - 2 * p.y * y_side) * 2 + (p.x + (1 - y_side) - 2 * p.x * (1 - y_side))
        return self.copy(2 + y_side, l, self.block(chip), p.to_x)

    def forward(self, l):
        p = self.p
        chip = l * 4 + jnp.where(p.c == 0, (1 - p.y) * 2 + p.x, p.y * 2 + 1 - p.x)
        to = (p.z, jnp.where(p.c == 0, p.y * 4 + (1 - p.x) * 2 + p.c, (1 - p.y) * 4 + p.x * 2 + p.c))
        return self.copy(4, l, self.block(chip), to)

    def forward_in(self, l):
        return self.copy(4, l, self.block(l * 4 + (1 - self.p.y) * 2 + 1 - self.p.x), self.p.to_x)

    def cs(self, l):
        return self.copy(5, l, self.level(l, self.p.c), self.p.to_core)

    def cs_in(self, l):
        return self.copy(5, l, self.level(l, 1 - self.p.c), self.p.to_core)

    def sides(self, l):
        self.xs(l).start()
        self.ys(l).start()

    def ends(self, k):
        z = self.p.z

        @pl.when((z >= k) & (z < 3))
        def _():
            self.up(k).start()

        @pl.when((z + k <= 3) & (z > 0))
        def _():
            self.down(k).start()

    def begin(self):
        if not self.plane_first:
            self.ends(0)
        self.sides(self.p.z)

    def along_z(self, k, onward=True):
        z = self.p.z

        @pl.when(z > k)
        def _():
            self.up_in(k).wait_recv()

        @pl.when(z + k < 3)
        def _():
            self.down_in(k).wait_recv()

        if k < 2:
            self.ends(k + 1)
        if onward:
            self.each(k + 1, (lambda l: self.cs(l).start()) if self.plane_first else self.sides)

    def each(self, k, what):
        z = self.p.z
        if k == 0:
            what(z)
            return

        @pl.when(z >= k)
        def _():
            what(z - k)

        @pl.when(z + k <= 3)
        def _():
            what(z + k)

    def turn(self, l):
        self.side_in(l, 1 - self.p.c).wait_recv()
        self.forward(l).start()
        self.side_in(l, self.p.c).wait_recv()

    def across(self, l):
        self.forward_in(l).wait_recv()
        if self.plane_first:
            self.ends(0)
        self.cs(l).start()

    def finish(self):
        z = self.p.z
        self.finish_z()
        for l in range(4):
            if self.plane_first:
                continue
            self.xs(l).wait_send()
            self.ys(l).wait_send()
            self.forward(l).wait_send()
        if self.plane_first:
            self.xs(z).wait_send()
            self.ys(z).wait_send()
            self.forward(z).wait_send()
        for l in range(4):
            self.cs(l).wait_send()
            self.cs_in(l).wait_recv()

    def finish_z(self):
        z = self.p.z
        for k in range(3):

            @pl.when((z >= k) & (z < 3))
            def _():
                self.up(k).wait_send()

            @pl.when((z + k <= 3) & (z > 0))
            def _():
                self.down(k).wait_send()


VECTORS = 9
TILE = 128


def vector_steps(p, values, out_ref, hold, landed, sems):
    send, recv = sems.at[0], sems.at[1]
    state = {}

    def begin():
        state["value"] = values()
        hold[0] = state["value"]
        push(hold.at[0], landed.at[0], send.at[0], recv.at[0], p.to_core).start()

    def then(i, to, after):
        def step():
            push(hold.at[i], landed.at[i], send.at[i], recv.at[i], to).wait()
            hold[i + 1] = hold[i] + landed[i]
            after()
        return step

    def next_side():
        push(hold.at[1], landed.at[1], send.at[1], recv.at[1], p.to_x).start()

    def next_other():
        push(hold.at[2], landed.at[2], send.at[2], recv.at[2], p.to_y).start()

    def line(s):
        return push(hold.at[3], landed.at[2 + s], send.at[2 + s], recv.at[2 + s], p.to_z(s))

    def next_line():
        for s in (1, 2, 3):
            line(s).start()

    def last():
        for s in (1, 2, 3):
            line(s).wait()
        out_ref[...] = hold[3] + landed[3] + landed[4] + landed[5]

    return [begin, then(0, p.to_core, next_side), then(1, p.to_x, next_other), then(2, p.to_y, next_line), last]


def cut(cols, share):
    first = int(round(cols * (1 - share) / TILE)) * TILE
    return first


import os
PLANE_SHARE = 0.0


def gather_kernel(*refs):
    vectors, b_up = refs[:VECTORS], refs[VECTORS]
    wq, wk, wv, wo, wu, wd = refs[VECTORS + 1 : VECTORS + 7]
    rows_in = refs[VECTORS + 7 : VECTORS + 9]
    out_a, out_u, out_d, out_v = refs[VECTORS + 9 : VECTORS + 13]
    rows_out = refs[VECTORS + 13 : VECTORS + 15]
    rows_held = refs[VECTORS + 15 : VECTORS + 17]
    held, give, take, packed, hold, landed, sems, pair_sems, own_sems, vec_sems = refs[VECTORS + 17 :]
    p = Place()
    width = wq.shape[1]
    rail = 2 * width
    rows = wq.shape[0]
    lower = p.c == 0
    loads = [pltpu.make_async_copy(w, held.at[0, :, pl.ds(i * width, width)], own_sems.at[3 + i]) for i, w in enumerate((wq, wk, wv, wo))]
    loads.append(pltpu.make_async_copy(wu, held.at[1], own_sems.at[7]))
    own_d = pltpu.make_async_copy(wd, out_d.at[p.z], own_sems.at[2])
    moves = [pltpu.make_async_copy(a, b, own_sems.at[8 + i]) for i, (a, b) in enumerate(zip(rows_in, rows_held))]
    for cp in loads + moves:
        cp.start()
    own_d.start()
    greet(p)
    for cp in loads:
        cp.wait()
    mine = pl.ds(pl.multiple_of(p.c * rail, TILE), rail)
    other = pl.ds(pl.multiple_of((1 - p.c) * rail, TILE), rail)
    pair = []
    for i in range(2):
        give[i] = held[i, :, other].astype(F32)
        pair.append(push(give.at[i], take.at[i], pair_sems.at[0, i], pair_sems.at[1, i], p.to_core))
        pair[i].start()
    jobs = []

    def add_jobs(out, rail_cols, columns_by_rail):
        first = cut(rail_cols, PLANE_SHARE)
        for start, size, plane in ((0, first, False), (first, rail_cols - first, True)):
            if size == 0:
                continue
            if columns_by_rail:
                def lanes(c, start=start, size=size):
                    return pl.ds(pl.multiple_of(c * rail_cols + start, TILE), size)
                block = lambda chip, out=out, lanes=lanes: out.at[chip, :, lanes(p.c)]
                level = lambda l, c, out=out, lanes=lanes: out.at[pl.ds(l * 4, 4), :, lanes(c)]
            else:
                lane = pl.ds(start, size)
                block = lambda chip, out=out, lane=lane: out.at[chip, p.c, :, lane]
                level = lambda l, c, out=out, lane=lane: out.at[pl.ds(l * 4, 4), c, :, lane]
            jobs.append(Gather(p, len(jobs), block, level, plane, sems))

    add_jobs(out_a, rail, True)
    add_jobs(out_u, rail, True)
    per = len(jobs) // 2
    for i, out in enumerate((out_a, out_u)):
        pair[i].wait()
        own = held[i, :, mine].astype(F32)
        got = take[i]
        packed[i] = jnp.concatenate([jnp.where(lower, own, got), jnp.where(lower, got, own)], axis=0).astype(BF)
        cp = pltpu.make_async_copy(packed.at[i], out.at[p.chip, :, mine], own_sems.at[i])
        cp.start()
        cp.wait()
        for job in jobs[i * per : (i + 1) * per][::-1]:
            job.begin()
    rows_d = Gather(p, len(jobs), lambda chip: out_d.at[chip // 4], None, False, sems)
    own_d.wait()
    rows_d.ends(0)
    device = p.z * 8 + p.f

    def spread(ref):
        count = ref.shape[1]
        total = count * 32
        lane = lax.broadcasted_iota(jnp.int32, (count, total), 1)
        row = lax.broadcasted_iota(jnp.int32, (count, total), 0)
        place = (lane == row + device * count).astype(BF)
        return jnp.dot(ref[...], place, preferred_element_type=F32)

    def values():
        rows_of = [spread(v) for v in vectors]
        up = spread(b_up)
        rows_of += [up[:, i * width : (i + 1) * width] for i in range(4)]
        rows_of.append(jnp.zeros((3, width), F32))
        return jnp.concatenate(rows_of, axis=0)

    steps = vector_steps(p, values, out_v, hold, landed, vec_sems)
    steps[0]()
    plane = [job for job in jobs if job.plane_first]
    line = [job for job in jobs if not job.plane_first]
    for job in plane:
        job.turn(p.z)
    length, count = rows_in[0].shape[0], rows_in[0].shape[1]
    span = rows_out[0].shape[1]
    low = length // 16 * 16

    def lay_out(i, r):
        if r == 0:
            moves[i].wait()
        rows_out[i][r, low:span, :] = jnp.zeros((span - low, width), BF)
        rows_out[i][r, 0:length, :] = rows_held[i][:, r, :]

    work = [(i, r) for i in range(2) for r in range(count)]
    lay_out(*work[0])
    steps[1]()
    for job in plane:
        job.across(p.z)
    for r in range(1, count):
        lay_out(*work[r])
    for k in range(4):
        if k < 3:
            for job in line + plane:
                job.along_z(k)
            rows_d.along_z(k, False)
            steps[k + 2]()
        for job in line:
            job.each(k, job.turn)
        if k == 0:
            for item in work[count:]:
                lay_out(*item)
        if k > 0:
            for job in line:
                job.each(k - 1, job.across)
    for job in line:
        job.each(3, job.across)
    rows_d.finish_z()
    for job in jobs:
        job.finish()


def gather_all(vectors, b_up, matrices, rows_in, span):
    wq, wd = matrices[0], matrices[5]
    rows, width = wq.shape
    rail = 2 * width
    depth = wd.shape[0]
    turned = [v.transpose(1, 0, 2) for v in rows_in]
    count = rows_in[0].shape[0]
    return pl.pallas_call(
        gather_kernel,
        out_shape=(
            jax.ShapeDtypeStruct((16, 2 * rows, 4 * width), BF),
            jax.ShapeDtypeStruct((16, 2 * rows, 4 * width), BF),
            jax.ShapeDtypeStruct((4, depth, width), BF),
            jax.ShapeDtypeStruct((16, width), F32),
            jax.ShapeDtypeStruct((count, span, width), BF),
            jax.ShapeDtypeStruct((count, span, width), BF),
        ),
        in_specs=[pl.BlockSpec(memory_space=pltpu.VMEM)] * (VECTORS + 1) + [pl.BlockSpec(memory_space=pl.ANY)] * 8,
        out_specs=(pl.BlockSpec(memory_space=pl.ANY),) * 3 + (pl.BlockSpec(memory_space=pltpu.VMEM),) * 3,
        scratch_shapes=[
            pltpu.VMEM(turned[0].shape, BF),
            pltpu.VMEM(turned[1].shape, BF),
            pltpu.VMEM((2, rows, 2 * rail), BF),
            pltpu.VMEM((2, rows, rail), F32),
            pltpu.VMEM((2, rows, rail), F32),
            pltpu.VMEM((2, 2 * rows, rail), BF),
            pltpu.VMEM((4, 16, width), F32),
            pltpu.VMEM((6, 16, width), F32),
            pltpu.SemaphoreType.DMA((12, 6, 4)),
            pltpu.SemaphoreType.DMA((2, 2)),
            pltpu.SemaphoreType.DMA((10,)),
            pltpu.SemaphoreType.DMA((2, 6)),
        ],
        compiler_params=pltpu.CompilerParams(collective_id=0, has_side_effects=True, vmem_limit_bytes=60 * 2**20),
        name="gather_weights",
    )(*[v[None] for v in vectors], b_up[None], *matrices, *turned)


class Scatter:
    def __init__(self, place, j, level, bufs, sems):
        self.p, self.j, self.level, self.sems = place, j, level, sems
        self.acc, self.got, self.one, self.two, self.give, self.line, self.low, self.fin = bufs
        p = place
        rail0 = p.c == 0
        self.me = p.y * 2 + p.x
        self.first = jnp.where(rail0, p.y * 2 + 1 - p.x, (1 - p.y) * 2 + p.x)
        self.second = jnp.where(rail0, (1 - p.y) * 2 + p.x, p.y * 2 + 1 - p.x)
        self.diag = (1 - p.y) * 2 + 1 - p.x
        self.to_first = (p.z, self.first * 2 + p.c)
        self.to_second = (p.z, self.second * 2 + p.c)

    def move(self, kind, l, src, dst, to):
        return push(src, dst, self.sems.at[0, kind, self.j, l], self.sems.at[1, kind, self.j, l], to)

    def own(self, l):
        return pltpu.make_async_copy(self.level(l, self.p.c), self.acc.at[l], self.sems.at[0, 0, self.j, l])

    def core(self, l):
        return self.move(1, l, self.level(l, 1 - self.p.c), self.got.at[l], self.p.to_core)

    def step1(self, l, slot):
        block = self.first if slot == 0 else self.diag
        return self.move(2 + slot, l, self.acc.at[l, block], self.one.at[l, slot], self.to_first)

    def step2(self, l):
        return self.move(4, l, self.give.at[l], self.two.at[l], self.to_second)

    def along(self, l, s):
        return self.move(5, s, self.line.at[l], self.low.at[s], self.p.to_z(s))

    def begin(self, l):
        self.core(l).start()
        self.own(l).start()

    def pair(self, l):
        self.own(l).wait()
        self.core(l).wait_recv()
        self.acc[l] = (self.acc[l].astype(F32) + self.got[l].astype(F32)).astype(BF)
        self.step1(l, 0).start()
        self.step1(l, 1).start()

    def side(self, l):
        self.step1(l, 1).wait_recv()
        self.give[l] = (self.acc[l, self.second].astype(F32) + self.one[l, 1].astype(F32)).astype(BF)
        self.step2(l).start()

    def plane_sum(self, l):
        return self.acc[l, self.me].astype(F32) + self.one[l, 0].astype(F32) + self.two[l].astype(F32)

    def plane(self, l):
        self.step1(l, 0).wait_recv()
        self.step2(l).wait_recv()
        self.line[l] = self.plane_sum(l).astype(BF)
        self.along(l, lax.rem(l - self.p.z + 4, 4)).start()

    def last(self):
        z = self.p.z
        self.step1(z, 0).wait_recv()
        self.step2(z).wait_recv()
        self.fin[...] = self.plane_sum(z)
        for s in (1, 2, 3):
            self.along(z, s).wait_recv()
            self.fin[...] += self.low[s].astype(F32)

    def finish(self):
        for l in range(4):
            self.core(l).wait_send()
            self.step1(l, 0).wait_send()
            self.step1(l, 1).wait_send()
            self.step2(l).wait_send()
        for s in (1, 2, 3):
            self.along(self.p.z, s).wait_send()


def level_order(p):
    low = p.z < 2
    zz = jnp.where(low, p.z, 3 - p.z)
    order = [3, 2, 1 - zz, zz]
    return [jnp.where(low, l, 3 - l) for l in order]


PARTS = 1


def scatter_kernel(ga, vec_m, vec_a, u_so_far, d_so_far, two_d, mine_d, two_u, mine_u, *refs):
    out_a, out_v, out_b, out_u, out_d = refs[0:5]
    hold, landed, total, sems, last_sems, vec_sems = refs[5 + 8 * PARTS : 11 + 8 * PARTS]
    line_d, far_d, line_u, far_u, fin_u, tail_sems = refs[11 + 8 * PARTS :]
    p = Place()
    rail = ga.shape[2] // 2
    part = rail // PARTS
    rows = ga.shape[1] // 2

    def lanes_of(i, c):
        return pl.ds(pl.multiple_of(c * rail + i * part, TILE), part)

    jobs = [
        Scatter(
            p, i, lambda l, c, i=i: ga.at[pl.ds(l * 4, 4), :, lanes_of(i, c)], refs[5 + 8 * i : 13 + 8 * i], sems
        )
        for i in range(PARTS)
    ]
    out_u[...] = u_so_far[...]
    out_d[...] = d_so_far[...]
    greet(p)
    order = level_order(p)
    items = [(job, l) for l in order for job in jobs]
    for job, l in items:
        job.begin(l)
    owner = level_of(3)
    sum_d = mine_d[...] + two_d[...].astype(F32)
    line_d[...] = sum_d.astype(BF)

    def tail(kind, s):
        src, dst = (line_d, far_d.at[s - 1]) if kind == 0 else (line_u.at[s - 1], far_u.at[s - 1])
        return push(src, dst, tail_sems.at[0, kind, s], tail_sems.at[1, kind, s], p.to_z(s))

    def sum_u(l):
        return mine_u[l] + two_u[l].astype(F32)

    for s in (1, 2, 3):
        pl.when(lax.rem(p.z + s, 4) == owner)(lambda s=s: tail(0, s).start())
        line_u[s - 1] = sum_u(lax.rem(p.z + s, 4)).astype(BF)
        tail(1, s).start()
    steps = vector_steps(p, lambda: vec_m[...] + vec_a[...], total, hold, landed, vec_sems)
    number = len(items)
    for n in range(number + 2):
        if n < number:
            items[n][0].pair(items[n][1])
        if 1 <= n <= number:
            items[n - 1][0].side(items[n - 1][1])
        if 2 <= n:
            job, l = items[n - 2]
            if n - 2 < number - PARTS:
                job.plane(l)
            else:
                job.last()
        if n < 5:
            steps[n]()
    sends = []
    for i, job in enumerate(jobs):
        lane = lanes_of(i, p.c)
        cp = push(
            job.fin.at[pl.ds(pl.multiple_of((1 - p.c) * rows, 8), rows)], out_a.at[:, lane],
            last_sems.at[0, i], last_sems.at[1, i], p.to_core,
        )
        cp.start()
        sends.append(cp)
        out_a[:, lane] = job.fin[pl.ds(pl.multiple_of(p.c * rows, 8), rows), :]
    fin_u[...] = sum_u(p.z)
    for s in (1, 2, 3):
        tail(1, s).wait()
        fin_u[...] += far_u[s - 1].astype(F32)
    half = fin_u.shape[1]
    lane = pl.ds(pl.multiple_of(owner * 2 * half + p.c * half, TILE), half)
    cp = push(
        fin_u.at[pl.ds(pl.multiple_of((1 - p.c) * rows, 8), rows)], out_u.at[:, lane],
        tail_sems.at[0, 0, 0], tail_sems.at[1, 0, 0], p.to_core,
    )
    cp.start()
    sends.append(cp)
    out_u[:, lane] = fin_u[pl.ds(pl.multiple_of(p.c * rows, 8), rows), :]

    @pl.when(p.z == owner)
    def _():
        out_d[...] = sum_d
        for s in (1, 2, 3):
            tail(0, s).wait_recv()
            out_d[...] += far_d[s - 1].astype(F32)

    for s in (1, 2, 3):
        pl.when(lax.rem(p.z + s, 4) == owner)(lambda s=s: tail(0, s).wait_send())
    device = p.z * 8 + p.f
    width = total.shape[1]
    share = width // 32
    out_v[...] = pltpu.roll(total[...], lax.rem(width - device * share, width), 1)[:, :TILE]
    row = VECTORS + device // 8
    up = jnp.sum(jnp.where(lax.broadcasted_iota(jnp.int32, total.shape, 0) == row, total[...], 0.0), axis=0, keepdims=True)
    up = jnp.broadcast_to(up, (8, width))
    out_b[...] = pltpu.roll(up, lax.rem(width - lax.rem(device, 8) * 4 * share, width), 1)[:, :TILE]
    for job in jobs:
        job.finish()
    for cp in sends:
        cp.wait()


def scatter_all(ga, vec_m, vec_a, u_so_far, d_so_far, two_d, mine_d, two_u, mine_u):
    rows = ga.shape[1] // 2
    cols = ga.shape[2]
    width = vec_m.shape[1]
    block = (2 * rows, cols // 2 // PARTS)
    bufs = [
        pltpu.VMEM((4, 4) + block, BF),
        pltpu.VMEM((4, 4) + block, BF),
        pltpu.VMEM((4, 2) + block, BF),
        pltpu.VMEM((4,) + block, BF),
        pltpu.VMEM((4,) + block, BF),
        pltpu.VMEM((4,) + block, BF),
        pltpu.VMEM((4,) + block, BF),
        pltpu.VMEM(block, F32),
    ]
    vmem, hbm = pl.BlockSpec(memory_space=pltpu.VMEM), pl.BlockSpec(memory_space=pl.ANY)
    return pl.pallas_call(
        scatter_kernel,
        out_shape=(
            jax.ShapeDtypeStruct((rows, cols), F32),
            jax.ShapeDtypeStruct((16, TILE), F32),
            jax.ShapeDtypeStruct((8, TILE), F32),
            jax.ShapeDtypeStruct(u_so_far.shape, F32),
            jax.ShapeDtypeStruct(d_so_far.shape, F32),
        ),
        in_specs=[hbm] + [vmem] * 8,
        out_specs=(vmem,) * 5,
        scratch_shapes=[
            *(bufs * PARTS),
            pltpu.VMEM((4, 16, width), F32),
            pltpu.VMEM((6, 16, width), F32),
            pltpu.VMEM((16, width), F32),
            pltpu.SemaphoreType.DMA((2, 6, PARTS, 4)),
            pltpu.SemaphoreType.DMA((2, PARTS)),
            pltpu.SemaphoreType.DMA((2, 6)),
            pltpu.VMEM(two_d.shape, BF),
            pltpu.VMEM((3,) + two_d.shape, BF),
            pltpu.VMEM((3,) + two_u.shape[1:], BF),
            pltpu.VMEM((3,) + two_u.shape[1:], BF),
            pltpu.VMEM(two_u.shape[1:], F32),
            pltpu.SemaphoreType.DMA((2, 2, 4)),
        ],
        compiler_params=pltpu.CompilerParams(collective_id=1, has_side_effects=True, vmem_limit_bytes=60 * 2**20),
        name="scatter_gradients",
    )(ga, vec_m, vec_a, u_so_far, d_so_far, two_d, mine_d, two_u, mine_u)


def part_kernel(a, u, d, v, b, *outs):
    width = outs[0].shape[1]
    for i in range(4):
        outs[i][...] = a[:, i * width : (i + 1) * width]
    outs[4][...] = u[...]
    outs[5][...] = d[...]
    for i in range(VECTORS):
        outs[6 + i][...] = v[i : i + 1, : outs[6 + i].shape[1]]
    outs[6 + VECTORS][...] = b[0:1, : outs[6 + VECTORS].shape[1]]


def part_all(a, u, d, v, b, share, up_share):
    rows, width = a.shape[0], a.shape[1] // 4
    shapes = [(rows, width)] * 4 + [u.shape, d.shape] + [(1, share)] * VECTORS + [(1, up_share)]
    vmem = pl.BlockSpec(memory_space=pltpu.VMEM)
    outs = pl.pallas_call(
        part_kernel,
        out_shape=tuple(jax.ShapeDtypeStruct(s, F32) for s in shapes),
        in_specs=[vmem] * 5,
        out_specs=(vmem,) * len(shapes),
        name="part_gradients",
    )(a, u, d, v, b)
    return outs[:6], [w.reshape(-1) for w in outs[6:]]


HEAD = 64
EPSILON = 1e-06
LANES = 128
FAR = -1e30
GAIN1, BIAS1, ROUTER, B_QUERY, B_VALUE, B_OUT, GAIN2, BIAS2, B_DOWN, B_UP = range(10)


def dot(a, b):
    return lax.dot_general(a, b, (((1,), (0,)), ((), ())), preferred_element_type=F32)


def dot_nt(a, b):
    return lax.dot_general(a, b, (((1,), (1,)), ((), ())), preferred_element_type=F32)


def dot_tn(a, b):
    return lax.dot_general(a, b, (((0,), (0,)), ((), ())), preferred_element_type=F32)


def up_to(count, step):
    return (count + step - 1) // step * step


def iota(shape, dim):
    return lax.broadcasted_iota(jnp.int32, shape, dim)


def normalized(x):
    centred = x - jnp.mean(x, axis=-1, keepdims=True)
    scale = lax.rsqrt(jnp.mean(centred * centred, axis=-1, keepdims=True) + EPSILON)
    return centred * scale, scale


def norm_back(n, scale, gain, e):
    eg = e * gain
    return scale * (eg - jnp.mean(eg, axis=-1, keepdims=True) - n * jnp.mean(eg * n, axis=-1, keepdims=True))


def column_of(row, size):
    eye = iota((size, size), 0) == iota((size, size), 1)
    return jnp.sum(jnp.where(eye, jnp.broadcast_to(row, (size, size)), 0.0), axis=1, keepdims=True)


def order_of(picked_ref, order_ref):
    cap = picked_ref.shape[1]
    before = jnp.where(iota((cap, cap), 0) < iota((cap, cap), 1), 1.0, 0.0).astype(BF)
    order_ref[...] = dot(picked_ref[...].astype(BF), before)


def pad_rows(selected, segment, picked_ref, marks_ref):
    count, length = selected.shape
    picked_ref[...] = jnp.zeros_like(picked_ref)
    picked_ref[0:count, 0:length] = selected[...].astype(F32)
    if marks_ref is not None:
        marks_ref[...] = jnp.zeros_like(marks_ref)
        marks_ref[0:count, 0:length] = segment[...].astype(F32)


def row_of(ref, r):
    return jnp.sum(jnp.where(iota(ref.shape, 0) == r, ref[...], 0.0), axis=0, keepdims=True)


def to_picked(order, picked, size):
    cap = order.shape[1]
    hit = (order == iota((size, cap), 0).astype(F32)) & (picked > 0.5)
    return jnp.where(hit, 1.0, 0.0)


def from_picked(order, picked, size):
    cap = order.shape[1]
    place = column_of(jnp.where(picked > 0.5, order, -1.0), cap)
    return jnp.where(place == iota((cap, size), 1).astype(F32), 1.0, 0.0).astype(BF)


def sizes(cap):
    half = cap // 2 + HEAD // 2
    return [(half, up_to(half, LANES)), (cap, cap)]


def loop(count, what):
    lax.fori_loop(0, count, lambda i, c: (what(i), c)[1], 0)


def lanes(i, size):
    return pl.ds(pl.multiple_of(i * size, LANES), size)


def each_size(count, cap, what):
    low = 0
    for rows, keys in sizes(cap):

        @pl.when((count > low) & (count <= rows))
        def _(rows=rows, keys=keys):
            what(rows, keys)

        low = rows


def forbidden(hit, marks, count, size):
    segment_of = dot_nt(jnp.broadcast_to(marks, (8, marks.shape[1])).astype(BF), hit.astype(BF))[0:1]
    segment_of = jnp.where(iota((1, size), 1) < count, segment_of, 99.0)
    column = jnp.sum(hit * marks, axis=1, keepdims=True)
    column = jnp.where(iota((size, 1), 0) < count, column, 99.0)
    return jnp.where(column == segment_of, 0.0, FAR)


def two_heads(pair):
    first = iota(pair.shape, 1) < HEAD
    zero = jnp.zeros_like(pair)
    return jnp.concatenate([jnp.where(first, pair, zero), jnp.where(first, zero, pair)], axis=0)


def one_pair(turned):
    size = turned.shape[1] // 2
    return jnp.concatenate([turned[:HEAD, :size], turned[HEAD:, size:]], axis=0).T


def attend_kernel(r, x, segment, selected, wa, table, *refs):
    outs, kept = refs[-22:-14], refs[-14:-6]
    mid, xc, h, qkv, attn, branch, logs, gates = kept
    xs, picked, marks, order, bar, sems = refs[-6:]
    cap = xs.shape[0]
    span, width = x.shape[1], x.shape[2]
    pad_rows(selected, segment, picked, marks)
    order_of(picked, order)
    sel, place, mark = [ref[r : r + 1, :] for ref in (picked, order, marks)]
    count = jnp.sum(sel).astype(jnp.int32)
    xs[span:cap, :] = jnp.zeros((cap - span, width), BF)
    xs[0:span, :] = x[r]
    mid[...] = x[r].astype(F32)

    def leave(i, size):
        src, dst = kept[i], outs[i].at[r]
        if i not in (0, 6):
            src, dst = src.at[0:size], dst.at[0:size]
        return pltpu.make_async_copy(src, dst, sems.at[i])

    def work(rows, keys):
        hit = to_picked(place, sel, keys)
        block = forbidden(hit, mark, count, keys)
        bar[0:keys, 0:keys] = block
        bar[0:keys, keys : 2 * keys] = block
        x_in = dot(hit[:rows].astype(BF), xs[...])
        xc[0:rows, :] = x_in.astype(BF)
        n, _ = normalized(x_in)
        h_in = (n * table[GAIN1 : GAIN1 + 1, :] + table[BIAS1 : BIAS1 + 1, :]).astype(BF)
        h[0:rows, :] = h_in
        gate = jax.nn.sigmoid(jnp.sum(h_in.astype(F32) * table[ROUTER : ROUTER + 1, :], axis=1, keepdims=True))
        for i, b in enumerate((B_QUERY, None, B_VALUE)):
            part = dot(h_in, wa[:, i * width : (i + 1) * width])
            if b is not None:
                part = part + table[b : b + 1, :]
            qkv[0:rows, i * width : (i + 1) * width] = part.astype(BF)
        if keys > rows:
            qkv[rows:keys, :] = jnp.zeros((keys - rows, 3 * width), BF)
        for i in (1, 2, 3):
            leave(i, keys).start()

        def pair(i, carry):
            lane = i * LANES
            q = qkv[0:keys, pl.ds(pl.multiple_of(lane, LANES), LANES)]
            k = qkv[0:keys, pl.ds(pl.multiple_of(lane + width, LANES), LANES)]
            v = qkv[0:keys, pl.ds(pl.multiple_of(lane + 2 * width, LANES), LANES)]
            s = dot_nt(k, two_heads(q * BF(HEAD**-0.5))) + bar[0:keys, 0 : 2 * keys]
            top = jnp.max(s, axis=0, keepdims=True)
            e = jnp.exp(s - top)
            total = jnp.sum(e, axis=0, keepdims=True)
            out = one_pair(dot_tn(v, e.astype(BF)) * (1.0 / total))
            attn[0:keys, pl.ds(pl.multiple_of(lane, LANES), LANES)] = out.astype(BF)
            logs[i, 0:1, 0 : 2 * keys] = top + jnp.log(total)
            return carry

        lax.fori_loop(0, width // LANES, pair, 0)
        gates[0:rows, :] = jnp.broadcast_to(gate, (rows, LANES))
        for i in (4, 6, 7):
            leave(i, keys).start()
        out = dot(attn[0:rows, :], wa[:, 3 * width :]) + table[B_OUT : B_OUT + 1, :]
        branch[0:rows, :] = out.astype(BF)
        leave(5, keys).start()
        back = from_picked(place, sel, keys)[:span, :rows]
        mid[...] += dot(back, (out * gate).astype(BF))
        for i in range(1, 8):
            leave(i, keys).wait()

    each_size(count, cap, work)
    leave(0, cap).start()
    leave(0, cap).wait()


def attend(r, patches, segment, selected, wa, table, kept=()):
    count, span, width = patches.shape
    cap = up_to(span, LANES)
    shapes = [
        ((span, width), F32), ((cap, width), BF), ((cap, width), BF), ((cap, 3 * width), BF), ((cap, width), BF),
        ((cap, width), BF), ((width // LANES, 1, 2 * cap), F32), ((cap, LANES), F32),
    ]
    vmem, hbm = pl.BlockSpec(memory_space=pltpu.VMEM), pl.BlockSpec(memory_space=pl.ANY)
    return pl.pallas_call(
        partial(attend_kernel, r),
        out_shape=tuple(jax.ShapeDtypeStruct((count,) + s, d) for s, d in shapes),
        in_specs=[vmem] * 5 + [hbm] * len(kept),
        out_specs=(hbm,) * 8,
        scratch_shapes=[pltpu.VMEM(s, d) for s, d in shapes] + [
            pltpu.VMEM((cap, width), BF),
            pltpu.VMEM((8, cap), F32),
            pltpu.VMEM((8, cap), F32),
            pltpu.VMEM((8, cap), F32),
            pltpu.VMEM((cap, 2 * cap), F32),
            pltpu.SemaphoreType.DMA((8,)),
        ],
        input_output_aliases={5 + i: i for i in range(len(kept))},
        cost_estimate=pl.CostEstimate(flops=4 * 10**9, bytes_accessed=10**7, transcendentals=10**6),
        compiler_params=pltpu.CompilerParams(vmem_limit_bytes=60 * 2**20),
        name="attend",
    )(patches, segment, selected, wa, table, *kept)


def attend_back_kernel(mixed_in, gm, segment, selected, wa_in, table, *refs):
    kept_in, (rows_x, rows_mixed, grad_a, sums) = refs[:7], refs[7:11]
    kept, (wa, mixed) = refs[11:18], refs[18:20]
    xc, h, qkv, attn, branch, logs, gates = kept
    grad_x, high, picked, marks, order, bar, ga, dqkv, sems, whole_sems = refs[20:]
    cap = high.shape[0]
    span, width = gm.shape[1], gm.shape[2]
    pad_rows(selected, segment, picked, marks)
    order_of(picked, order)
    high[...] = jnp.zeros_like(high)
    grad_a[...] = jnp.zeros_like(grad_a)
    sums[...] = jnp.zeros_like(sums)

    def fetch(i, r, size):
        src, dst = kept_in[i].at[r], kept[i].at[r]
        if i != 5:
            src, dst = src.at[0:size], dst.at[0:size]
        return pltpu.make_async_copy(src, dst, sems.at[i, r])

    counts = [jnp.sum(picked[r : r + 1, :]).astype(jnp.int32) for r in range(gm.shape[0])]
    first = jnp.where(counts[0] > 0, 0, 1)
    load_wa = pltpu.make_async_copy(wa_in, wa, whole_sems.at[0])
    load_mixed = pltpu.make_async_copy(mixed_in, mixed, whole_sems.at[1])
    for r in range(gm.shape[0]):

        def begin(rows, keys, r=r):
            for i in (6, 4, 3, 2, 5, 1, 0):
                fetch(i, r, keys).start()

        each_size(counts[r], cap, begin)
        (load_mixed if r else load_wa).start()

    def add(i, v):
        sums[i : i + 1, :] += jnp.sum(v, axis=0, keepdims=True)

    def add_weight(i, j, v):
        at = slice(i * width, j * width)
        grad_a[:, at] = (grad_a[:, at].astype(F32) + v).astype(BF)

    def row(r, carry):
        sel, place, mark = row_of(picked, r), row_of(order, r), row_of(marks, r)
        count = jnp.sum(sel).astype(jnp.int32)
        high[0:span, :] = gm[r]

        @pl.when(count == 0)
        def _():
            grad_x[r] = gm[r]

        def work(rows, keys):
            hit = to_picked(place, sel, keys)
            block = forbidden(hit, mark, count, keys)
            bar[0:keys, 0:keys] = block
            bar[0:keys, keys : 2 * keys] = block
            take = hit[:rows].astype(BF)
            for i in (6, 4, 3):
                fetch(i, r, keys).wait()
            pl.when(r == first)(load_wa.wait)
            g = dot(take, high[...])
            gate = gates[r, 0:rows, 0:1]
            grad_logit = jnp.sum(g * branch[r, 0:rows, :].astype(F32), axis=1, keepdims=True) * gate * (1.0 - gate)
            gb = g * gate
            add(B_OUT, gb.astype(BF).astype(F32))
            gb = gb.astype(BF)
            add_weight(3, 4, dot_tn(attn[r, 0:rows, :], gb))
            ga[0:rows, :] = dot_nt(gb, wa[:, 3 * width :]).astype(BF)
            if keys > rows:
                ga[rows:keys, :] = jnp.zeros((keys - rows, width), BF)

            for i in (2, 5, 1, 0):
                fetch(i, r, keys).wait()

            def pair(i, carry):
                at = pl.ds(pl.multiple_of(i * LANES, LANES), LANES)
                at_k = pl.ds(pl.multiple_of(i * LANES + width, LANES), LANES)
                at_v = pl.ds(pl.multiple_of(i * LANES + 2 * width, LANES), LANES)
                q2 = two_heads(qkv[r, 0:keys, at] * BF(HEAD**-0.5))
                k = qkv[r, 0:keys, at_k]
                v = qkv[r, 0:keys, at_v]
                g2 = two_heads(ga[0:keys, at])
                p = jnp.exp(dot_nt(k, q2) + bar[0:keys, 0 : 2 * keys] - logs[r, i, 0:1, 0 : 2 * keys])
                dp = dot_nt(v, g2)
                ds = (p * (dp - jnp.sum(p * dp, axis=0, keepdims=True))).astype(BF)
                dqkv[0:keys, at] = one_pair(dot_tn(k, ds) * HEAD**-0.5).astype(BF)
                dqkv[0:keys, at_k] = dot(ds, q2).astype(BF)
                dqkv[0:keys, at_v] = dot(p.astype(BF), g2).astype(BF)
                return carry

            lax.fori_loop(0, width // LANES, pair, 0)
            add(B_QUERY, dqkv[0:rows, 0:width].astype(F32))
            add(B_VALUE, dqkv[0:rows, 2 * width :].astype(F32))
            h_in = h[r, 0:rows, :]
            add(ROUTER, h_in.astype(F32) * grad_logit)
            add_weight(0, 3, dot_tn(h_in, dqkv[0:rows, :]))
            gh = dot_nt(dqkv[0:rows, :], wa[:, : 3 * width]) + grad_logit * table[ROUTER : ROUTER + 1, :]
            n, scale = normalized(xc[r, 0:rows, :].astype(F32))
            add(GAIN1, n * gh)
            add(BIAS1, gh)
            dx = norm_back(n, scale, table[GAIN1 : GAIN1 + 1, :], gh).astype(BF)
            back = from_picked(place, sel, keys)[:span, :rows]
            grad_x[r] = (gm[r].astype(F32) + dot(back, dx)).astype(BF)

        each_size(count, cap, work)
        return carry

    lax.fori_loop(0, gm.shape[0], row, 0)

    pl.when(sum(counts) == 0)(load_wa.wait)

    load_mixed.wait()
    for r in range(gm.shape[0]):
        rows_x[:, r, :] = grad_x[r, 0 : rows_x.shape[0], :]
        rows_mixed[:, r, :] = mixed[r, 0 : rows_x.shape[0], :]


def attend_back(mixed, gm, segment, selected, wa, table, kept):
    count, span, width = gm.shape
    cap = up_to(span, LANES)
    vmem, hbm = pl.BlockSpec(memory_space=pltpu.VMEM), pl.BlockSpec(memory_space=pl.ANY)
    rows_out = jax.ShapeDtypeStruct((segment.shape[1], count, width), BF)
    rows_x, rows_mixed, grad_a, sums = pl.pallas_call(
        attend_back_kernel,
        out_shape=(
            rows_out,
            rows_out,
            jax.ShapeDtypeStruct(wa.shape, BF),
            jax.ShapeDtypeStruct((16, width), F32),
        ),
        in_specs=[hbm] + [vmem] * 3 + [hbm, vmem] + [hbm] * len(kept),
        out_specs=(vmem,) * 4,
        scratch_shapes=[
            *[pltpu.VMEM(v.shape, v.dtype) for v in kept],
            pltpu.VMEM(wa.shape, BF),
            pltpu.VMEM(mixed.shape, BF),
            pltpu.VMEM(gm.shape, BF),
            pltpu.VMEM((cap, width), BF),
            pltpu.VMEM((8, cap), F32),
            pltpu.VMEM((8, cap), F32),
            pltpu.VMEM((8, cap), F32),
            pltpu.VMEM((cap, 2 * cap), F32),
            pltpu.VMEM((cap, width), BF),
            pltpu.VMEM((cap, 3 * width), BF),
            pltpu.SemaphoreType.DMA((7, count)),
            pltpu.SemaphoreType.DMA((2,)),
        ],
        cost_estimate=pl.CostEstimate(flops=10**10, bytes_accessed=3 * 10**7, transcendentals=10**6),
        compiler_params=pltpu.CompilerParams(vmem_limit_bytes=60 * 2**20),
        name="attend_back",
    )(mixed, gm, segment, selected, wa, table, *kept)
    return rows_x.transpose(1, 0, 2), rows_mixed.transpose(1, 0, 2), grad_a, sums


def gelu_parts(p):
    z = jnp.abs(p)
    e = jnp.exp(-0.5 * p * p)
    t = 1.0 / (1.0 + (0.3275911 * 0.5**0.5) * z)
    poly = ((((1.061405429 * t - 1.453152027) * t + 1.421413741) * t - 0.284496736) * t + 0.254829592) * t
    tail = 0.5 * poly * e
    phi = jnp.where(p > 0, 1.0 - tail, tail)
    return phi, phi + p * (e * 0.3989422804014327)


BLOCK = 592


class ChunkScatter:
    def __init__(self, p, kind, whole, bufs, fin, sems):
        self.p, self.kind, self.whole, self.fin, self.sems = p, kind, whole, fin, sems
        self.got, self.one, self.give, self.two, self.line, self.far = bufs
        rail0 = p.c == 0
        self.me = p.y * 2 + p.x
        self.first = jnp.where(rail0, p.y * 2 + 1 - p.x, (1 - p.y) * 2 + p.x)
        self.second = jnp.where(rail0, (1 - p.y) * 2 + p.x, p.y * 2 + 1 - p.x)
        self.diag = (1 - p.y) * 2 + 1 - p.x
        self.to_first = (p.z, self.first * 2 + p.c)
        self.to_second = (p.z, self.second * 2 + p.c)

    def move(self, stage, j, src, dst, to):
        return push(src, dst, self.sems.at[0, stage, self.kind, j], self.sems.at[1, stage, self.kind, j], to)

    def rail(self, j, c):
        if self.kind == 0:
            return self.whole.at[j, :, c]
        return self.whole.at[j, :, :, :, lanes(c, self.whole.shape[4] // 2)]

    def block(self, j, chip):
        if self.kind == 0:
            return self.whole.at[j, chip, self.p.c]
        return self.whole.at[j, :, chip, :, lanes(self.p.c, self.whole.shape[4] // 2)]

    def core(self, j):
        return self.move(0, j, self.rail(j, 1 - self.p.c), self.got.at[j], self.p.to_core)

    def step1(self, j, slot):
        return self.move(1 + slot, j, self.block(j, self.diag if slot else self.first), self.one.at[j, slot], self.to_first)

    def step2(self, j):
        return self.move(3, j, self.give.at[j], self.two.at[j], self.to_second)

    def begin(self, j):
        self.core(j).start()

    def pair(self, j):
        self.core(j).wait_recv()
        mine = self.rail(j, self.p.c)
        mine[...] = (mine[...].astype(F32) + self.got[j].astype(F32)).astype(BF)
        self.step1(j, 1).start()
        self.step1(j, 0).start()

    def side(self, j):
        self.step1(j, 1).wait_recv()
        self.give[j] = (self.block(j, self.second)[...].astype(F32) + self.one[j, 1].astype(F32)).astype(BF)
        self.step2(j).start()

    def along(self, j, s):
        if self.kind == 0:
            src = self.line.at[j]
        else:
            src = self.line.at[j, s - 1]
        return self.move(3 + s, j, src, self.far.at[j, s - 1], self.p.to_z(s))

    def plane_sum(self, j, l):
        if self.kind == 0:
            return self.block(j, self.me)[...].astype(F32) + self.one[j, 0].astype(F32) + self.two[j].astype(F32)
        own = self.whole[j, l, self.me, :, lanes(self.p.c, self.whole.shape[4] // 2)]
        return own.astype(F32) + self.one[j, 0, l].astype(F32) + self.two[j, l].astype(F32)

    def cross(self, j, owner):
        z = self.p.z
        self.step1(j, 0).wait_recv()
        self.step2(j).wait_recv()
        if self.kind == 0:
            self.line[j] = self.plane_sum(j, 0).astype(BF)
            for s in (1, 2, 3):

                @pl.when(lax.rem(z + s, 4) == owner)
                def _(s=s):
                    self.along(j, s).start()

            return
        for s in (1, 2, 3):
            self.line[j, s - 1] = self.plane_sum(j, lax.rem(z + s, 4)).astype(BF)
            self.along(j, s).start()

    def last(self, j, owner):
        if self.kind == 0:

            @pl.when(self.p.z == owner)
            def _():
                total = self.plane_sum(j, 0)
                for s in (1, 2, 3):
                    self.along(j, s).wait_recv()
                    total = total + self.far[j, s - 1].astype(F32)
                self.fin[...] = total

            return
        total = self.plane_sum(j, self.p.z)
        for s in (1, 2, 3):
            self.along(j, s).wait_recv()
            total = total + self.far[j, s - 1].astype(F32)
        self.fin[j] = total

    def hand_over(self, j, give, mine):
        self.step1(j, 1).wait_recv()
        give[...] = (self.block(j, self.second)[...].astype(F32) + self.one[j, 1].astype(F32)).astype(BF)
        self.step1(j, 0).wait_recv()
        mine[...] = self.block(j, self.me)[...].astype(F32) + self.one[j, 0].astype(F32)

    def finish(self, owner_of, handed):
        def left(j):
            self.core(j).wait_send()
            self.step1(j, 0).wait_send()
            self.step1(j, 1).wait_send()

        left(handed)

        def one(j):
            left(j)
            self.step2(j).wait_send()
            for s in (1, 2, 3):
                if self.kind == 0:

                    @pl.when(lax.rem(self.p.z + s, 4) == owner_of(j))
                    def _(s=s):
                        self.along(j, s).wait_send()

                else:
                    self.along(j, s).wait_send()

        loop(handed, one)


def level_of(i):
    return jnp.where(i == 0, 0, jnp.where(i == 1, 3, i - 1))


def mlp_kernel(remote, mid, g, wu, wd, table, *refs):
    if remote:
        parts_d, refs = (wd,) + refs[:3], refs[3:]
    mlp_body(remote, mid, g, wu, parts_d if remote else (wd,), table, *refs)


def mlp_body(remote, mid, g, wu, parts_d, table, mixed, gm, sums, out_u, out_d, *refs):
    if remote:
        handed, refs = refs[:4], refs[4:]
    u, acc, act, gp, hold_u, hold_d, weight_sems = refs[:7]
    count, span, width = mid.shape
    tokens = count * span
    chunk = width
    chunks = 4 if remote else parts_d[0].shape[0] // chunk
    blocks = tokens // BLOCK
    per = span // BLOCK
    if remote:
        grad_d, grad_u, fin_u = refs[7:10]
        bufs_d, bufs_u = refs[10:16], refs[16:22]
        sems, last_sems, part_sems = refs[22:]
        p = Place()
        greet(p)
        down = ChunkScatter(p, 0, grad_d, bufs_d, out_d, sems)
        up = ChunkScatter(p, 1, grad_u, bufs_u, fin_u, sems)
        rail = width // 2
        rows = out_u.shape[0]

    def row(i):
        return table[i : i + 1, :]

    def each_block(what):
        loop(blocks, lambda b: what(b, pl.ds(pl.multiple_of(b * BLOCK, 16), BLOCK)))

    def mid_of(b):
        return mid[b // per, pl.ds(pl.multiple_of(lax.rem(b, per) * BLOCK, 16), BLOCK), :]

    def load(i):
        j, slot = level_of(i), lax.rem(i, 2)
        up_part = pltpu.make_async_copy(wu.at[:, lanes(j, chunk)], hold_u.at[slot], weight_sems.at[0, slot])
        if remote:
            return (up_part,)
        rows_d = parts_d[0].at[pl.ds(pl.multiple_of(j * chunk, 16), chunk)]
        return up_part, pltpu.make_async_copy(rows_d, hold_d.at[slot], weight_sems.at[1, slot])

    def weights(i):
        if remote:
            return hold_u[lax.rem(i, 2)], hold_d[i].reshape(chunk, width)
        return hold_u[lax.rem(i, 2)], hold_d[lax.rem(i, 2)]

    for cp in load(0):
        cp.start()
    if remote:
        chips = (p.y * 2 + p.x, p.y * 2 + 1 - p.x, (1 - p.y) * 2 + p.x, (1 - p.y) * 2 + 1 - p.x)

        def keep(i, n):
            return pltpu.make_async_copy(parts_d[n].at[level_of(i)], hold_d.at[i, chips[n], p.c], part_sems.at[2, i, n])

        def share(i, n):
            return push(
                parts_d[n].at[level_of(i)], hold_d.at[i, chips[n], p.c], part_sems.at[0, i, n], part_sems.at[1, i, n], p.to_core
            )

        for i in range(chunks):
            for n in range(4):
                keep(i, n).start()
                share(i, n).start()
    sums[...] = jnp.zeros_like(sums)
    acc[...] = jnp.zeros_like(acc)
    def start(b, at):
        n, _ = normalized(mid_of(b))
        u[at, :] = (n * row(GAIN2) + row(BIAS2)).astype(BF)
        sums[B_DOWN : B_DOWN + 1, :] += jnp.sum(g[at, :].astype(F32), axis=0, keepdims=True)

    each_block(start)

    def send_rail(i):
        lane = pl.ds(pl.multiple_of(level_of(i) * chunk + p.c * rail, TILE), rail)
        return push(
            fin_u.at[i, pl.ds(pl.multiple_of((1 - p.c) * rows, 8), rows)], out_u.at[:, lane],
            last_sems.at[0, i], last_sems.at[1, i], p.to_core,
        )

    def own_rail(i):
        up.last(i, 0)
        send_rail(i).start()
        lane = pl.ds(pl.multiple_of(level_of(i) * chunk + p.c * rail, TILE), rail)
        out_u[:, lane] = fin_u[i, pl.ds(pl.multiple_of(p.c * rows, 8), rows), :]

    def from_chunk(i, back, what):
        if remote:
            pl.when(i >= back)(lambda: what(i - back))

    def one_chunk(i):
        j, slot = level_of(i), lax.rem(i, 2)
        for cp in load(i):
            cp.wait()
        if remote:
            for n in range(4):
                keep(i, n).wait()
                share(i, n).wait_recv()

        @pl.when(i + 1 < chunks)
        def _():
            for cp in load(i + 1):
                cp.start()

        def hidden(b, at):
            in_u, in_d = weights(i)
            pre = dot(u[at, :], in_u) + table[pl.ds(B_UP + j, 1), :]
            phi, slope = gelu_parts(pre)
            act[at, :] = (pre * phi).astype(BF)
            grad_pre = (slope * dot_nt(g[at, :], in_d)).astype(BF)
            gp[at, :] = grad_pre
            sums[pl.ds(B_UP + j, 1), :] += jnp.sum(grad_pre.astype(F32), axis=0, keepdims=True)

        each_block(hidden)
        from_chunk(i, 1, lambda k: down.cross(k, level_of(k)))
        from_chunk(i, 1, lambda k: up.side(k))
        from_chunk(i, 2, own_rail)
        part = dot_tn(act[...], g[...]).astype(BF)
        if remote:
            grad_d[i] = part.reshape(grad_d.shape[1:])
            down.begin(i)
        else:
            out_d[pl.ds(pl.multiple_of(j * chunk, 16), chunk), :] = part
        part = dot_tn(u[...], gp[...]).astype(BF)
        if remote:
            grad_u[i] = part.reshape(grad_u.shape[1:])
            up.begin(i)
            down.pair(i)
        else:
            out_u[:, lanes(j, chunk)] = part
        from_chunk(i, 1, lambda k: up.cross(k, 0))

        def total(b, at):
            in_u, in_d = weights(i)
            acc[0, at, :] += dot(act[at, :], in_d)
            acc[1, at, :] += dot_nt(gp[at, :], in_u)

        for b in range(blocks):
            total(b, pl.ds(b * BLOCK, BLOCK))
            if remote and b == 0:
                up.pair(i)
        if remote:
            pl.when(i + 1 < chunks)(lambda: down.side(i))
        from_chunk(i, 1, lambda k: down.last(k, level_of(k)))

    loop(chunks, one_chunk)

    def end(b, at):
        m = mid_of(b)
        out = (m + acc[0, at, :] + row(B_DOWN)).astype(BF)
        mixed[b] = out
        n, scale = normalized(m)
        e = acc[1, at, :]
        sums[GAIN2 : GAIN2 + 1, :] += jnp.sum(n * e, axis=0, keepdims=True)
        sums[BIAS2 : BIAS2 + 1, :] += jnp.sum(e, axis=0, keepdims=True)
        gm[b] = (g[at, :].astype(F32) + norm_back(n, scale, row(GAIN2), e)).astype(BF)

    for b in range(blocks):
        end(b, pl.ds(b * BLOCK, BLOCK))
        if remote and b == 0:
            own_rail(chunks - 2)
    if remote:
        down.hand_over(chunks - 1, *handed[:2])
        up.hand_over(chunks - 1, *handed[2:])
        for i in range(chunks - 1):
            send_rail(i).wait()
        up.finish(level_of, chunks - 1)
        down.finish(level_of, chunks - 1)
        for i in range(chunks):
            for n in range(4):
                share(i, n).wait_send()


def mlp(remote, mid, cot, wu, parts_d, table):
    count, span, width = mid.shape
    tokens = count * span
    if remote:
        rows, depth = wu.shape[0] // 32, parts_d[0].shape[1]
        outs = [jax.ShapeDtypeStruct((rows, wu.shape[1]), F32), jax.ShapeDtypeStruct((depth, width), F32)]
        half = width // 2
        for shape in ((depth, width), (4, 2 * rows, half)):
            outs += [jax.ShapeDtypeStruct(shape, BF), jax.ShapeDtypeStruct(shape, F32)]
        extra = [
            pltpu.VMEM((4, 4, 2, depth, width), BF),
            pltpu.VMEM((4, 4, 4, 2 * rows, width), BF),
            pltpu.VMEM((4, 2 * rows, half), F32),
        ]
        extra += [pltpu.VMEM((4, 4, depth, width), BF), pltpu.VMEM((4, 2, depth, width), BF)]
        extra += [pltpu.VMEM((4, depth, width), BF)] * 3 + [pltpu.VMEM((4, 3, depth, width), BF)]
        extra += [pltpu.VMEM((4, 4, 4, 2 * rows, half), BF), pltpu.VMEM((4, 2, 4, 2 * rows, half), BF)]
        extra += [pltpu.VMEM((4, 4, 2 * rows, half), BF)] * 2 + [pltpu.VMEM((4, 3, 2 * rows, half), BF)] * 2
        extra += [pltpu.SemaphoreType.DMA((2, 7, 2, 4)), pltpu.SemaphoreType.DMA((2, 4)), pltpu.SemaphoreType.DMA((3, 4, 4))]
        hold_d = pltpu.VMEM((4, 4, 2, depth, width), BF)
        params = dict(collective_id=2, has_side_effects=True)
    else:
        outs = [jax.ShapeDtypeStruct(wu.shape, BF), jax.ShapeDtypeStruct(parts_d[0].shape, BF)]
        extra, params = [], {}
        hold_d = pltpu.VMEM((2, width, width), BF)
    vmem = pl.BlockSpec(memory_space=pltpu.VMEM)
    hbm = pl.BlockSpec(memory_space=pl.ANY)
    return pl.pallas_call(
        partial(mlp_kernel, remote),
        out_shape=(
            jax.ShapeDtypeStruct(mid.shape, BF),
            jax.ShapeDtypeStruct(mid.shape, BF),
            jax.ShapeDtypeStruct((16, width), F32),
            *outs,
        ),
        in_specs=[vmem, vmem, hbm, hbm, vmem] + [hbm] * (len(parts_d) - 1),
        out_specs=(vmem,) * (3 + len(outs)),
        scratch_shapes=[
            pltpu.VMEM((tokens, width), BF),
            pltpu.VMEM((2, tokens, width), F32),
            pltpu.VMEM((tokens, width), BF),
            pltpu.VMEM((tokens, width), BF),
            pltpu.VMEM((2, width, width), BF),
            hold_d,
            pltpu.SemaphoreType.DMA((2, 2)),
            *extra,
        ],
        compiler_params=pltpu.CompilerParams(vmem_limit_bytes=62 * 2**20, **params),
        name="mlp",
    )(mid, cot.reshape(tokens, width), wu, parts_d[0], table, *parts_d[1:])


def local(
    small, patches, segment_ids, selected, cotangent, ln1_gain, ln1_bias, w_router, w_query, b_query,
    w_key, w_value, b_value, w_out, b_out, ln2_gain, ln2_bias, w_up, b_up, w_down, b_down,
):
    length, width = patches.shape[1:]
    span = up_to(length, 16)
    vectors = (ln1_gain, ln1_bias, w_router, b_query, b_value, b_out, ln2_gain, ln2_bias, b_down)
    matrices = (w_query, w_key, w_value, w_out, w_up, w_down)
    if small:
        attn_w, up_w, down_z, table, x, cot = gather_all(vectors, b_up, matrices, (patches, cotangent), span)
        attn_w = attn_w.reshape(-1, attn_w.shape[2])
        up_w = up_w.reshape(-1, up_w.shape[2])
        down_x = lax.ppermute(down_z, "fsdp", [(i, i ^ 2) for i in range(8)])
        down_y = lax.ppermute(down_z, "fsdp", [(i, i ^ 4) for i in range(8)])
    else:
        whole = [lax.all_gather(v, AXES, axis=0, tiled=True) for v in vectors + (b_up,)]
        table = jnp.concatenate(
            [jnp.stack(whole[:VECTORS]), whole[VECTORS].reshape(4, width), jnp.zeros((3, width), BF)]
        ).astype(F32)
        attn_w = jnp.concatenate([lax.all_gather(w, AXES, axis=0, tiled=True) for w in matrices[:4]], axis=1)
        up_w = lax.all_gather(w_up, AXES, axis=0, tiled=True)
        down_w = lax.all_gather(w_down, AXES, axis=0, tiled=True)
        x, cot = [jnp.pad(v, ((0, 0), (0, span - length), (0, 0))) for v in (patches, cotangent)]
    kept = ()
    for r in range(x.shape[0]):
        kept = attend(r, x, segment_ids, selected, attn_w, table, kept)
        if small and r == 0:
            down_x, down_y, _ = lax.optimization_barrier((down_x, down_y, kept[6]))
            turn = jnp.where(lax.rem(lax.axis_index("fsdp"), 2) == 0, down_y, down_x)
            down_d = lax.ppermute(turn, "fsdp", [(i, i ^ (4 if i % 2 else 2)) for i in range(8)])
    mid, *kept = kept
    down_parts = (down_z, down_x, down_y, down_d) if small else (down_w,)
    mixed, grad_mid, sums_mlp, grad_u, grad_d, *handed = mlp(small, mid, cot, up_w, down_parts, table)
    if small:
        give_d, mine_d, give_u, mine_u = handed
        second = [(i, i ^ (2 if i % 2 else 4)) for i in range(8)]
        two_d, two_u = lax.ppermute(give_d, "fsdp", second), lax.ppermute(give_u, "fsdp", second)
    grad_x, mixed, grad_a, sums_attn = attend_back(mixed, grad_mid, segment_ids, selected, attn_w, table, kept)
    if small:
        own_a, own_v, own_b, grad_u, grad_d = scatter_all(
            grad_a.reshape(16, -1, grad_a.shape[1]), sums_mlp, sums_attn, grad_u, grad_d, two_d, mine_d, two_u, mine_u
        )
        own_m, (*own, own_up_b) = part_all(own_a, grad_u, grad_d, own_v, own_b, ln1_gain.shape[0], b_up.shape[0])
    else:
        sums = sums_mlp + sums_attn
        own = [lax.psum_scatter(sums[i], AXES, scatter_dimension=0, tiled=True) for i in range(VECTORS)]
        own_up_b = lax.psum_scatter(
            sums[VECTORS : VECTORS + 4].reshape(-1), AXES, scatter_dimension=0, tiled=True
        )
        own_m = [
            lax.psum_scatter(g.astype(F32), AXES, scatter_dimension=0, tiled=True)
            for g in jnp.split(grad_a, 4, axis=1) + [grad_u, grad_d]
        ]
    return (
        mixed, grad_x, own[0], own[1], own[2], own_m[0], own[3], own_m[1], own_m[2], own[4],
        own_m[3], own[5], own[6], own[7], own_m[4], own_up_b, own_m[5], own[8],
    )


def solution(mesh):
    flat, rows2, rows3 = P(AXES), P(AXES, None), P(AXES, None, None)
    vec, mat = flat, rows2
    small = mesh.shape["dp"] == 4 and mesh.shape["fsdp"] == 8
    return jax.shard_map(
        partial(local, small),
        mesh=mesh,
        in_specs=(
            rows3, rows2, rows2, rows3, vec, vec, vec, mat, vec, mat, mat, vec, mat, vec, vec, vec, mat, vec, mat, vec,
        ),
        out_specs=(
            rows3, rows3, vec, vec, vec, mat, vec, mat, mat, vec, mat, vec, vec, vec, mat, vec, mat, vec,
        ),
        check_vma=False,
    )
```
